1024 devices in a mesh: bx: 8 (over y, core), by: 8 (over z_hi, x), bz: 16 (over z_lo).
Axes of the slice: x: 4, y: 4, z: 32 (z_hi: 2, z_lo: 16; z = z_hi * 16 + z_lo), core: 2. Of those that a mesh axis runs over, the one named last changes fastest.
Arguments:
- features: bfloat16 [8, 8, 16, 64, 640], P('bx', 'by', 'bz'), may hold values from -5 to 5
- shifts: bfloat16 [8, 8, 16, 64, 3], P('bx', 'by', 'bz'), may hold values from -0.34960938 to 0.34960938
- block_counts: int32 [8, 8, 16], P('bx', 'by', 'bz'), may hold values from 16 to 48, as said below
- block_centres: int32 [8, 8, 16, 48, 4], P('bx', 'by', 'bz'), may hold values from 0 to 511, as said below
- block_neighbours: int32 [8, 8, 16, 48, 128], P('bx', 'by', 'bz'), may hold values from 0 to 511, as said below
- w_pair: bfloat16 [128, 128], replicated, may hold values from -0.5 to 0.5
- w_radial: float32 [8, 128], replicated, may hold values from -2 to 2
- w_mix: bfloat16 [128, 192], replicated, may hold values from -0.5 to 0.5
- w_self: bfloat16 [128, 128], replicated, may hold values from -0.5 to 0.5
- w_tensor: bfloat16 [64, 128], replicated, may hold values from -0.75 to 0.75
- w_out: float32 [128], replicated, may hold values from -0.125 to 0.125
Outputs:
- energies: float32 [8, 8, 16, 64], P('bx', 'by', 'bz')
- forces: float32 [8, 8, 16, 3, 64], P('bx', 'by', 'bz')
The draws below stay inside these ranges and needn't reach their ends.
Inputs may be any that keep to these rules, and one draw needn't show every extreme that they name: `block_counts`: every draw has boxes with all 48 blocks filled. `block_centres`: A block's 4 centres lie inside the box or in the two lattice layers around it. `block_neighbours`: each edge joins two different lattice sites at most 2 steps apart in each coordinate, at least one of them inside the box; a centre outside the box has only neighbours inside it.
All inputs are finite; a program needn't handle non-finite values.
Results may differ from the reference program's by a relative error of at most 0.015.
Values may be sent and summed in bfloat16 or wider, within the bound.
A program may use at most 32 MiB of HBM per device.

```python
import math
import jax
import jax.numpy as jnp
import numpy as np
from jax import lax

C = 64
LAT = 128
BASIS = 8
ROW = 640
A = 64
OCT = 8
BLK = 128
CB = 4
PER = 32
NBLK = 48
NBX = 8
NBY = 8
NBZ = 16


def neighbour_strides():
    offsets_table = np.stack(np.meshgrid(np.arange(-2, 3), np.arange(-2, 3), np.arange(-2, 3), indexing='ij'), -1).reshape(-1, 3)
    nonzero = np.any(offsets_table != 0, axis=1)
    return jnp.asarray(offsets_table[nonzero], dtype=jnp.int32)


def table_index(coord_x, coord_y, coord_z):
    cell_x = (coord_x + 2) // 2
    cell_y = (coord_y + 2) // 2
    cell_z = (coord_z + 2) // 2
    within = ((coord_x + 2) % 2 * 2 + (coord_y + 2) % 2) * 2 + (coord_z + 2) % 2
    return ((cell_x * 4 + cell_y) * 4 + cell_z) * 8 + within


def edge_lists(key):
    key_local, key_rim, key_coin, key_score = jax.random.split(key, 4)
    lattice_shape = (NBX, NBY, NBZ, NBLK, CB)
    inside_site = jax.random.randint(key_local, lattice_shape + (3,), 0, 4)
    outer_site = jax.random.randint(key_rim, lattice_shape + (3,), -2, 6)
    inside = jnp.all((outer_site >= 0) & (outer_site < 4), axis=-1, keepdims=True)
    pushed = jnp.where(outer_site < 2, outer_site - 2, outer_site + 2)
    first_axis = jnp.arange(3, dtype=jnp.int32) == 0
    outer_site = jnp.where(inside & first_axis, pushed, outer_site)
    outside = jax.random.randint(key_coin, lattice_shape + (1,), 0, 5) < 2
    centre = jnp.where(outside, outer_site, inside_site)
    scores = jax.random.randint(key_score, lattice_shape + (124,), 0, 1 << 20) * 128 + jnp.arange(124, dtype=jnp.int32)
    picked = jnp.argsort(scores, axis=-1)[..., :PER]
    strides = neighbour_strides()[picked]
    target = centre[..., None, :] + strides
    target = jnp.where(outside[..., None, :], jnp.clip(target, 0, 3), target)
    centres = table_index(centre[..., 0], centre[..., 1], centre[..., 2])
    neighbours = table_index(target[..., 0], target[..., 1], target[..., 2]).reshape(NBX, NBY, NBZ, NBLK, BLK)
    return (centres.astype(jnp.int32), neighbours.astype(jnp.int32))


def draw_block_centres(key, part):
    centres, neighbours = edge_lists(key)
    return centres


def draw_block_neighbours(key, part):
    centres, neighbours = edge_lists(key)
    return neighbours


def draw_block_counts(key, part):
    key = jax.random.fold_in(key, 7)
    key_base, key_crowd, key_spot = jax.random.split(key, 3)
    box_total = NBX * NBY * NBZ
    drawn = jax.random.randint(key_base, (box_total,), NBLK // 3, 2 * NBLK // 3 + 1)
    crowded = jax.random.randint(key_crowd, (box_total,), 0, 8) == 0
    chosen_box = jax.random.randint(key_spot, (), 0, box_total)
    flattened = jnp.where(crowded | (jnp.arange(box_total, dtype=jnp.int32) == chosen_box), NBLK, drawn)
    return flattened.reshape(NBX, NBY, NBZ).astype(jnp.int32)


def block_levels(own_key, dims, shards, low, top_value):
    factor_of, own = 1.0, jax.random.fold_in(own_key, 6)
    for axis_at, blocks in shards:
        steps = jnp.exp(jax.random.uniform(jax.random.fold_in(own, axis_at), (blocks,), jnp.float32, low / len(shards), top_value / len(shards)))
        factor_of = factor_of * jnp.repeat(steps, dims[axis_at] // blocks).reshape([-1 if axis == axis_at else 1 for axis in range(len(dims))])
    return factor_of


def bell_draw(own_key, shape, scale, limit, pieces=(), held_as=jnp.bfloat16):
    factor_of = block_levels(own_key, shape, pieces, -0.22, 0.18) if pieces else 1.0
    result = jax.random.normal(own_key, shape, jnp.float32) * scale * factor_of
    return jnp.minimum(jnp.maximum(result, -limit), limit).astype(held_as)


def setup_inputs(seed: int = 0) -> dict:
    keys = jax.random.split(jax.random.key(seed), 12)
    features = bell_draw(keys[0], (NBX, NBY, NBZ, A, ROW), 1.0, 5.0, ((0, 8), (1, 8), (2, 16)))
    shifts = jnp.clip(jax.random.uniform(keys[1], (NBX, NBY, NBZ, A, 3), jnp.float32, -0.34960938, 0.34960938) * block_levels(keys[1], (NBX, NBY, NBZ, A, 3), ((0, 8), (1, 8), (2, 16)), -0.4, 0.0), -0.34960938, 0.34960938).astype(jnp.bfloat16)
    block_counts = draw_block_counts(jax.random.fold_in(keys[11], 71), 0)
    block_centres = draw_block_centres(jax.random.fold_in(keys[11], 71), 0)
    block_neighbours = draw_block_neighbours(jax.random.fold_in(keys[11], 71), 0)
    w_pair = bell_draw(keys[5], (2 * C, LAT), (2 * C) ** -0.5, 0.5)
    w_radial = bell_draw(keys[6], (BASIS, LAT), BASIS ** -0.5, 2.0, (), jnp.float32)
    w_mix = bell_draw(keys[7], (LAT, 3 * C), LAT ** -0.5, 0.5)
    w_self = bell_draw(keys[8], (LAT, LAT), LAT ** -0.5, 0.5)
    w_tensor = bell_draw(keys[9], (C, LAT), C ** -0.5, 0.75)
    w_out = bell_draw(keys[10], (LAT,), (16 * LAT) ** -0.5, 0.125, (), jnp.float32)
    return dict(features=features, shifts=shifts, block_counts=block_counts, block_centres=block_centres, block_neighbours=block_neighbours, w_pair=w_pair, w_radial=w_radial, w_mix=w_mix, w_self=w_self, w_tensor=w_tensor, w_out=w_out)


cutoff_radius = 6.0
site_spacing = 1.7
root_three = math.sqrt(3.0)
root_five = math.sqrt(5.0)
root_fifteen = math.sqrt(15.0)

def harmonics(unit_x, unit_y, unit_z):
    return jnp.stack([jnp.ones_like(unit_x), root_three * unit_x, root_three * unit_y, root_three * unit_z, root_fifteen * unit_x * unit_y, root_fifteen * unit_y * unit_z, 0.5 * root_five * (3.0 * unit_z * unit_z - 1.0), root_fifteen * unit_x * unit_z, 0.5 * root_fifteen * (unit_x * unit_x - unit_y * unit_y)], axis=-1)

def lattice_places(octant_rows):
    indices = jnp.arange(64 * octant_rows, dtype=jnp.int32)
    cell_index = indices // octant_rows
    within = indices % octant_rows
    coord_x = 2 * (cell_index // 16 - 1) + within // 4
    coord_y = 2 * (cell_index // 4 % 4 - 1) + within // 2 % 2
    coord_z = 2 * (cell_index % 4 - 1) + within % 2
    coords = jnp.stack([coord_x, coord_y, coord_z], axis=1).astype(jnp.float32)
    return (coords + 0.5) * site_spacing

def edge_energy(vectors, centre_rows, neighbour_rows, weights):
    w_pair, w_radial, w_mix, w_self, w_tensor, w_out = weights
    block_count = vectors.shape[0]
    edge_count = vectors.shape[2]
    centre_slots = centre_rows.shape[1]
    channels = neighbour_rows.shape[2]
    latent_width = w_self.shape[0]
    basis_count = w_radial.shape[0]
    per_centre = edge_count // centre_slots
    distance = jnp.sqrt(lax.optimization_barrier(jnp.sum(vectors * vectors, axis=1)))
    direction = vectors / distance[:, None, :]
    scaled = jnp.minimum(distance / cutoff_radius, 1.0)
    envelope = 1.0 - 28.0 * scaled ** 6 + 48.0 * scaled ** 7 - 21.0 * scaled ** 8
    frequency = jnp.arange(1, basis_count + 1, dtype=jnp.float32) * math.pi
    radial_basis = math.sqrt(2.0 / cutoff_radius) * jnp.sin(scaled[..., None] * frequency) / distance[..., None] * envelope[..., None]
    centre = centre_rows.reshape(block_count, centre_slots, 10, channels)
    centre_part = jnp.dot(centre[:, :, 0, :].reshape(block_count * centre_slots, channels), w_pair[:channels], preferred_element_type=jnp.float32)
    neighbour_part = jnp.dot(neighbour_rows.reshape(block_count * edge_count, channels), w_pair[channels:], preferred_element_type=jnp.float32)
    radial = jnp.dot(radial_basis.reshape(block_count * edge_count, basis_count), w_radial, precision=lax.Precision.HIGHEST)
    latent_input = (neighbour_part + radial).reshape(block_count, centre_slots, per_centre, latent_width) + centre_part.reshape(block_count, centre_slots, 1, latent_width)
    latent = jax.nn.silu(latent_input).astype(jnp.bfloat16).reshape(block_count * edge_count, latent_width)
    mixing = jnp.dot(latent, w_mix, preferred_element_type=jnp.float32).reshape(block_count, centre_slots, per_centre, 3, channels)
    spherical = harmonics(direction[:, 0], direction[:, 1], direction[:, 2]).reshape(block_count, centre_slots, per_centre, 9)
    tensor = centre[:, :, 1:, :].astype(jnp.float32)

    def contract(lower_m, upper_m):
        return lax.optimization_barrier(jnp.sum(spherical[..., lower_m:upper_m, None] * tensor[:, :, None, lower_m:upper_m, :], axis=3))
    coupled = mixing[..., 0, :] * contract(0, 1) + mixing[..., 1, :] * contract(1, 4) + mixing[..., 2, :] * contract(4, 9)
    coupled = coupled.astype(jnp.bfloat16).reshape(block_count * edge_count, channels)
    hidden = jax.nn.silu(jnp.dot(latent, w_self, preferred_element_type=jnp.float32) + jnp.dot(coupled, w_tensor, preferred_element_type=jnp.float32))
    readout = jnp.dot(hidden, w_out, precision=lax.Precision.HIGHEST).reshape(block_count, edge_count)
    return readout * envelope

def energy_and_grad(vectors, centre_rows, neighbour_rows, weights):

    def evaluate(moved_vectors):
        return edge_energy(moved_vectors, centre_rows, neighbour_rows, weights)
    energy, pullback = jax.vjp(evaluate, vectors)
    gradient = pullback(jnp.ones_like(energy))[0]
    return (energy, gradient)

def cell_offset(cell_digit):
    return jnp.where(cell_digit == 0, -1, jnp.where(cell_digit == 3, 1, 0)).astype(jnp.int32)

def reference(features, shifts, block_counts, block_centres, block_neighbours, w_pair, w_radial, w_mix, w_self, w_tensor, w_out):
    weights = (w_pair, w_radial, w_mix, w_self, w_tensor, w_out)
    box_total = NBX * NBY * NBZ
    cell_ids = jnp.arange(64, dtype=jnp.int32)
    cell_x = cell_ids // 16
    cell_y = cell_ids // 4 % 4
    cell_z = cell_ids % 4
    octant = ((cell_x + 1) % 2 * 2 + (cell_y + 1) % 2) * 2 + (cell_z + 1) % 2
    atom_index = octant[:, None] * OCT + jnp.arange(OCT, dtype=jnp.int32)[None, :]
    inner_places = lattice_places(OCT)
    per_centre = BLK // CB

    def one_box(inputs):
        box_id, count_here, centres, neighbours = inputs
        box_x = box_id // (NBY * NBZ)
        box_y = box_id // NBZ % NBY
        box_z = box_id % NBZ
        source_x = ((box_x + cell_offset(cell_x)) % NBX)[:, None]
        source_y = ((box_y + cell_offset(cell_y)) % NBY)[:, None]
        source_z = ((box_z + cell_offset(cell_z)) % NBZ)[:, None]
        ext_table = features[source_x, source_y, source_z, atom_index].reshape(64 * OCT, ROW)
        ext_shifts = shifts[source_x, source_y, source_z, atom_index].reshape(64 * OCT, 3)
        places = inner_places + ext_shifts.astype(jnp.float32)
        centre_edges = jnp.repeat(centres, per_centre, axis=1)
        vectors = jnp.swapaxes(places[neighbours] - places[centre_edges], 1, 2)
        energy, gradient = energy_and_grad(vectors, ext_table[centres], ext_table[:, :C][neighbours], weights)
        active = jnp.arange(NBLK, dtype=jnp.int32) < count_here
        energy = jnp.where(active[:, None], energy, 0.0)
        gradient = jnp.where(active[:, None, None], gradient, 0.0)
        pulled = jnp.swapaxes(gradient, 1, 2).reshape(-1, 3)
        ext_energy = jnp.zeros((64 * OCT,), jnp.float32).at[centre_edges.reshape(-1)].add(energy.reshape(-1))
        ext_force = jnp.zeros((64 * OCT, 3), jnp.float32).at[centre_edges.reshape(-1)].add(pulled).at[neighbours.reshape(-1)].add(-pulled)
        inner_energy = ext_energy.reshape(4, 4, 4, OCT)[1:3, 1:3, 1:3].reshape(A)
        inner_force = ext_force.reshape(4, 4, 4, OCT, 3)[1:3, 1:3, 1:3].reshape(A, 3).T
        return (inner_energy, inner_force)
    energies, forces = lax.map(one_box, (jnp.arange(box_total, dtype=jnp.int32), block_counts.reshape(box_total), block_centres.reshape(box_total, NBLK, CB), block_neighbours.reshape(box_total, NBLK, BLK)))
    return (energies.reshape(NBX, NBY, NBZ, A), forces.reshape(NBX, NBY, NBZ, 3, A))
```

```python
import functools
import math

import jax
import jax.numpy as jnp
from jax import lax
from jax.experimental import pallas as pl
from jax.experimental.pallas import tpu as pltpu
from jax.sharding import PartitionSpec as P

MESH = pl.DeviceIdType.MESH
F32 = jnp.float32
BF16 = jnp.bfloat16

cutoff_radius = 6.0
site_spacing = 1.7
root_three = math.sqrt(3.0)
root_five = math.sqrt(5.0)
root_fifteen = math.sqrt(15.0)

ROWS = 512
HALF = 256
WIDE = 640
SLIM = 128
BLOCKS = 48
EDGES = 128
PAIRS = BLOCKS // 2
LANES = 2 * EDGES


def phase_two_sends():
    return (
        (0, 1, 32, 64, 32),
        (0, -1, 0, 96, 32),
        (1, 0, 16, 128, 16),
        (1, 0, 48, 144, 16),
        (-1, 0, 0, 160, 16),
        (-1, 0, 32, 176, 16),
        (1, 1, 48, 192, 16),
        (1, -1, 16, 208, 16),
        (-1, 1, 32, 224, 16),
        (-1, -1, 0, 240, 16),
    )


SENDS = len(phase_two_sends())


def wrapped(axis, step):
    size = lax.axis_size(axis)
    return lax.rem(lax.axis_index(axis) + size + step, size)


def at_device(dx, dy, dz):
    return (wrapped("bx", dx), wrapped("by", dy), wrapped("bz", dz))


def octants(rows, order):
    return jnp.concatenate([rows[8 * o : 8 * o + 8] for o in order], axis=0)


def place_own(features_ref, shifts_ref, slim, wide, by_slim_out, by_wide_out, packed):
    packed[...] = jnp.zeros_like(packed)
    packed[:, 0:64] = features_ref[:, 0:64].astype(F32)
    packed[:, 64:67] = shifts_ref[...].astype(F32)
    own = [4 * ox + 2 * oy + oz for oz in range(2) for ox in range(2) for oy in range(2)]
    for source, table, out in (
        (packed[...], slim, by_slim_out),
        (features_ref[...].astype(F32), wide, by_wide_out),
    ):
        table[0:64, :] = octants(source, own).astype(BF16)
        for oy in range(2):
            face = [4 * ox + 2 * oy + oz for oz in range(2) for ox in range(2)]
            out[oy] = octants(source, face).astype(BF16)


def place_halo(table, landed):
    pieces = []
    below, above = landed[0].astype(F32), landed[1].astype(F32)
    for q in range(4):
        pieces += [below[8 * q : 8 * q + 8], above[8 * q : 8 * q + 8]]
    table[HALF : HALF + 64, :] = jnp.concatenate(pieces, axis=0).astype(BF16)


def entry_barrier():
    barrier = pltpu.get_barrier_semaphore()
    partners = [(0, 1, 0), (0, -1, 0)] + [
        (dx, 0, dz) for dx in (-1, 0, 1) for dz in (-1, 0, 1) if dx or dz
    ]
    for dx, dy, dz in partners:
        pl.semaphore_signal(barrier, inc=1, device_id=at_device(dx, dy, dz), device_id_type=MESH)
    pl.semaphore_wait(barrier, len(partners))


def by_copies(out, landed, send_sem, recv_sem):
    return [
        pltpu.make_async_remote_copy(
            src_ref=out.at[1 - side],
            dst_ref=landed.at[side],
            send_sem=send_sem.at[side],
            recv_sem=recv_sem.at[side],
            device_id=at_device(0, 1 - 2 * side, 0),
            device_id_type=MESH,
        )
        for side in range(2)
    ]


def half_copies(table, half, send_sem, recv_sem):
    return [
        pltpu.make_async_remote_copy(
            src_ref=table.at[pl.ds(HALF * half + source, rows)],
            dst_ref=table.at[pl.ds(HALF * half + target, rows)],
            send_sem=send_sem.at[half, at],
            recv_sem=recv_sem.at[half, at],
            device_id=at_device(dx, 0, dz),
            device_id_type=MESH,
        )
        for at, (dx, dz, source, target, rows) in enumerate(phase_two_sends())
    ]


def halo_kernel(
    features_ref,
    shifts_ref,
    slim,
    wide,
    by_slim_out,
    by_wide_out,
    by_slim_in,
    by_wide_in,
    packed,
    by_send,
    by_recv,
    send_sem,
    recv_sem,
):
    place_own(features_ref, shifts_ref, slim, wide, by_slim_out, by_wide_out, packed)
    entry_barrier()
    tables = (
        (slim, by_slim_out, by_slim_in, 0),
        (wide, by_wide_out, by_wide_in, 1),
    )
    by = [by_copies(out, landed, by_send.at[t], by_recv.at[t]) for _, out, landed, t in tables]
    own = [half_copies(table, 0, send_sem.at[t], recv_sem.at[t]) for table, _, _, t in tables]
    far = [half_copies(table, 1, send_sem.at[t], recv_sem.at[t]) for table, _, _, t in tables]
    for t in range(2):
        for copy in by[t]:
            copy.start()
    for t in range(2):
        for copy in own[t]:
            copy.start()
    for table, _, landed, t in tables:
        for copy in by[t]:
            copy.wait()
        place_halo(table, landed)
        for copy in far[t]:
            copy.start()
    for t in range(2):
        for copy in own[t] + far[t]:
            copy.wait()


def dot_nn(left, right):
    return lax.dot_general(left, right, (((1,), (0,)), ((), ())), preferred_element_type=F32)


def dot_nt(left, right):
    return lax.dot_general(left, right, (((1,), (1,)), ((), ())), preferred_element_type=F32)


def split(value):
    high = value.astype(BF16)
    return high, (value - high.astype(F32)).astype(BF16)


def cell_digits(row):
    return row >> 7, (row >> 5) & 3, (row >> 3) & 3, row & 7


def coordinates(row):
    ci, cj, ck, w = cell_digits(row)
    return (
        2 * (ci - 1) + (w >> 2),
        2 * (cj - 1) + ((w >> 1) & 1),
        2 * (ck - 1) + (w & 1),
    )


def table_row(row):
    ci, cj, ck, w = cell_digits(row)
    ox, oz = ci - 1, ck - 1
    inner_x = (ci == 1) | (ci == 2)
    inner_y = (cj == 1) | (cj == 2)
    inner_z = (ck == 1) | (ck == 2)
    x_side, z_side = ci >> 1, ck >> 1
    base = jnp.where(
        inner_x,
        jnp.where(inner_z, 32 * oz + 16 * ox, 64 + 32 * z_side + 16 * ox),
        jnp.where(inner_z, 128 + 32 * x_side + 16 * oz, 192 + 32 * x_side + 16 * z_side),
    )
    y_part = jnp.where(inner_y, 8 * (cj - 1), HALF + 8 * (cj >> 1))
    return base + y_part + w


def inner_atom(row):
    ci, cj, ck, w = cell_digits(row)
    inside = (ci == 1) | (ci == 2)
    inside = inside & ((cj == 1) | (cj == 2)) & ((ck == 1) | (ck == 2))
    return jnp.where(inside, 8 * (4 * (ci - 1) + 2 * (cj - 1) + ck - 1) + w, -1)


def lane_slot(shape):
    return lax.broadcasted_iota(jnp.int32, shape, 1) >> 5


def over_edges(columns, slots):
    spread = [jnp.broadcast_to(column, slots.shape) for column in columns]
    low = jnp.where(slots == 0, spread[0], spread[1])
    high = jnp.where(slots == 2, spread[2], spread[3])
    return jnp.where(slots < 2, low, high)


def slot_mask():
    slots = lane_slot((8, LANES))
    return jnp.where(slots == lax.broadcasted_iota(jnp.int32, (8, LANES), 0), 1.0, 0.0).astype(F32)


def edges_kernel(
    slim,
    wide,
    count_ref,
    centres_ref,
    neighbours_ref,
    w_pair_ref,
    w_radial_ref,
    w_mix_ref,
    w_self_ref,
    w_tensor_ref,
    w_out_ref,
    energies_ref,
    forces_ref,
    scratch,
):
    (
        turned,
        spots,
        scalars,
        shift_rows,
        centre_slim,
        centre_wide,
        basis_rows,
        sphere_rows,
        back_rows,
        pulled,
    ) = scratch

    turned[...] = slim[...].astype(F32).T[0:80].astype(BF16)

    neighbours = neighbours_ref[...]
    centres = centres_ref[...]
    spots[...] = table_row(neighbours)
    centre_spots = table_row(centres)

    centre_shift = []
    lanes_of_rows = lax.broadcasted_iota(jnp.int32, (BLOCKS, ROWS), 1)
    for place in range(4):
        hits = jnp.where(centre_spots[:, place : place + 1] == lanes_of_rows, 1.0, 0.0).astype(BF16)
        got = dot_nn(hits, slim[...])
        centre_slim[pl.ds(place, BLOCKS, stride=4), :] = got
        centre_shift.append([got[:, 64 + axis : 65 + axis] for axis in range(3)])
        got = dot_nn(hits, wide[...])
        for at in range(WIDE // 128):
            centre_wide[at, pl.ds(place, BLOCKS, stride=4), :] = got[:, 128 * at : 128 * at + 128]

    def gather(pair, _):
        hits = []
        rows = lax.broadcasted_iota(jnp.int32, (ROWS, EDGES), 0).astype(jnp.int16)
        for block in range(2):
            spot = spots[pl.ds(2 * pair + block, 1), :].astype(jnp.int16)
            hits.append(
                jnp.where(rows == spot, jnp.ones((), BF16), jnp.zeros((), BF16))
            )
        got = dot_nn(turned[...], jnp.concatenate(hits, axis=1))
        scalars[pair] = got[0:64].astype(BF16)
        for block in range(2):
            shift_rows[pl.ds(pl.multiple_of((2 * pair + block) * 8, 8), 8), :] = got[
                64:72, EDGES * block : EDGES * block + EDGES
            ]
        return 0

    lax.fori_loop(0, PAIRS, gather, 0)

    slots = lane_slot((BLOCKS, EDGES))
    centre_rows = over_edges([centres[:, j : j + 1] for j in range(4)], slots)
    vector = []
    for axis, (one, other) in enumerate(zip(coordinates(neighbours), coordinates(centre_rows))):
        near = shift_rows[pl.ds(axis, BLOCKS, stride=8), :]
        far = over_edges([centre_shift[j][axis] for j in range(4)], slots)
        vector.append((one - other).astype(F32) * site_spacing + (near - far))
    distance = jnp.sqrt(vector[0] * vector[0] + vector[1] * vector[1] + vector[2] * vector[2])
    inverse = 1.0 / distance
    ux, uy, uz = [part * inverse for part in vector]
    inside = distance < cutoff_radius
    scaled = jnp.minimum(distance * (1.0 / cutoff_radius), 1.0)
    fifth = (scaled * scaled) * (scaled * scaled) * scaled
    envelope = 1.0 - fifth * scaled * (28.0 - scaled * (48.0 - 21.0 * scaled))
    envelope_slope = jnp.where(
        inside, fifth * (-168.0 + scaled * (336.0 - 168.0 * scaled)) * (1.0 / cutoff_radius), 0.0
    )
    sine, cosine = jnp.sin(math.pi * scaled), jnp.cos(math.pi * scaled)
    norm = math.sqrt(2.0 / cutoff_radius) * inverse
    cut_norm = norm * envelope
    slope_sine = norm * (envelope_slope - envelope * inverse)
    slope_cosine = jnp.where(inside, cut_norm * (math.pi / cutoff_radius), 0.0)
    sines, cosines = [sine], [cosine]
    for _ in range(7):
        s, c = sines[-1], cosines[-1]
        sines.append(s * cosine + c * sine)
        cosines.append(c * cosine - s * sine)
    for k in range(8):
        basis_rows[pl.ds(k, BLOCKS, stride=8), :] = sines[k] * cut_norm
    sphere = (
        root_three * ux,
        root_three * uy,
        root_three * uz,
        root_fifteen * ux * uy,
        root_fifteen * uy * uz,
        0.5 * root_five * (3.0 * uz * uz - 1.0),
        root_fifteen * ux * uz,
        0.5 * root_fifteen * (ux * ux - uy * uy),
    )
    for m in range(8):
        sphere_rows[pl.ds(m, BLOCKS, stride=8), :] = sphere[m]

    mask = slot_mask()
    mask_b = mask.astype(BF16)
    w_pair = w_pair_ref[...]
    centre_part = dot_nn(
        centre_slim[:, 0:64].astype(BF16), w_pair[0:64]
    )
    centre_slim[...] = centre_part
    radial = w_radial_ref[...]
    radial_high, radial_low = split(radial)
    radial_rows = jnp.concatenate([radial_high.astype(F32), radial_low.astype(F32)], axis=0).astype(BF16)
    w_mix = w_mix_ref[...].astype(F32)
    mix_turned = w_mix.T
    mix_turned = jnp.concatenate(
        [mix_turned[128:192], mix_turned[64:128], mix_turned[0:64]], axis=0
    )
    mix_back = mix_turned.T.astype(BF16)
    mix_turned = mix_turned.astype(BF16)
    update = jnp.concatenate([w_self_ref[...], w_tensor_ref[...]], axis=0)
    update_turned = update.astype(F32).T.astype(BF16)
    w_out = jnp.broadcast_to(w_out_ref[...].astype(F32), (128, 128)).T
    w_out = jnp.concatenate([w_out, w_out], axis=1)
    low_half = lax.broadcasted_iota(jnp.int32, (8, 128), 1) < 64
    nothing = jnp.zeros((8, 128), F32)

    group = 4

    def latents(pair):
        at = pl.multiple_of(8 * pair, 8)
        high, low = split(centre_slim[pl.ds(at, 8), :])
        left = jnp.concatenate(
            [
                w_pair[64:128].astype(F32),
                high.astype(F32),
                low.astype(F32),
                radial_high.astype(F32),
                radial_high.astype(F32),
                radial_low.astype(F32),
                jnp.zeros((24, 128), F32),
            ],
            axis=0,
        ).T.astype(BF16)
        at = pl.multiple_of(16 * pair, 16)
        basis = jnp.concatenate(
            [basis_rows[pl.ds(at, 8), :], basis_rows[pl.ds(at + 8, 8), :]], axis=1
        )
        high, low = split(basis)
        right = jnp.concatenate(
            [mask, mask, high.astype(F32), low.astype(F32), high.astype(F32), jnp.zeros((24, LANES), F32)],
            axis=0,
        ).astype(BF16)
        return dot_nn(left, jnp.concatenate([scalars[pair], right], axis=0))

    def tensors(pair):
        at = pl.multiple_of(8 * pair, 8)
        parts = [centre_wide[g, pl.ds(at, 8), :] for g in range(5)]
        turns = [pltpu.roll(part, 64, 1) for part in parts]
        order_one = [turns[1], parts[1], turns[2]]
        order_two = [turns[2], parts[3], turns[3], parts[4], turns[4]]
        rows = [jnp.where(low_half, 0.0, part) for part in order_one]
        rows += [jnp.where(low_half, part, 0.0) for part in order_two]
        back = jnp.concatenate(rows, axis=0)
        zero = jnp.where(low_half, turns[0], 0.0)
        first = jnp.concatenate([back, nothing, nothing], axis=0).T
        second = jnp.concatenate([nothing] * 8 + [zero, nothing], axis=0).T[0:64]
        front = jnp.concatenate([first, second], axis=0)
        return front.astype(BF16), back.astype(BF16)

    def spheres(pair):
        at = pl.multiple_of(16 * pair, 16)
        sphere = jnp.concatenate(
            [sphere_rows[pl.ds(at, 8), :], sphere_rows[pl.ds(at + 8, 8), :]], axis=1
        )
        rows = [jnp.broadcast_to(sphere[m : m + 1], (8, LANES)) * mask for m in range(8)]
        return jnp.concatenate(rows + [mask, jnp.zeros((8, LANES), F32)], axis=0).astype(BF16)

    def silu_parts(x):
        gate = 0.5 * jnp.tanh(0.5 * x) + 0.5
        value = x * gate
        return value, gate + value * (1.0 - gate)

    def one_group(turn, _):
        pairs = [turn * group + g for g in range(group)]
        each = range(group)
        x1 = [latents(p) for p in pairs]
        sides = [tensors(p) for p in pairs]
        contracted = [dot_nn(sides[g][0], spheres(pairs[g])) for g in each]
        first = [silu_parts(x) for x in x1]
        latent = [value.astype(BF16) for value, _ in first]
        mixing = [dot_nn(mix_turned, value) for value in latent]
        coupled = []
        for g in each:
            product = mixing[g] * contracted[g]
            coupled.append((product[0:64] + product[64:128] + product[128:192]).astype(BF16))
        hidden_in = [
            dot_nn(update_turned, jnp.concatenate([latent[g], coupled[g]], axis=0)) for g in each
        ]
        second = [silu_parts(x) for x in hidden_in]
        readout = [jnp.sum(value * w_out, axis=0, keepdims=True) for value, _ in second]
        back = [dot_nn(update, (slope * w_out).astype(BF16)) for _, slope in second]
        for g in each:
            cotangent = back[g][128:192].astype(BF16).astype(F32)
            cotangents = jnp.concatenate([cotangent, cotangent, cotangent], axis=0)
            to_mixing = (cotangents * contracted[g]).astype(BF16)
            to_contracted = (cotangents[0:128] * mixing[g][0:128]).astype(BF16)
            to_latent = back[g][0:128] + dot_nn(mix_back, to_mixing)
            to_sphere = dot_nn(sides[g][1], to_contracted)
            to_sphere = jnp.sum(to_sphere.reshape(8, 8, LANES) * mask[None], axis=1)
            to_input = (to_latent * first[g][1]).astype(BF16)
            to_basis = dot_nn(radial_rows, to_input)
            to_basis = to_basis[0:8] + to_basis[8:16]
            for block in range(2):
                at = (2 * pairs[g] + block) * 24
                lanes = slice(EDGES * block, EDGES * block + EDGES)
                back_rows[pl.ds(pl.multiple_of(at, 8), 8), :] = to_sphere[:, lanes]
                back_rows[pl.ds(pl.multiple_of(at + 8, 8), 8), :] = to_basis[:, lanes]
                back_rows[pl.ds(pl.multiple_of(at + 16, 8), 8), :] = jnp.broadcast_to(
                    readout[g][:, lanes], (8, EDGES)
                )
        return 0

    lax.fori_loop(0, PAIRS // group, one_group, 0)

    def backs(row):
        return back_rows[pl.ds(row, BLOCKS, stride=24), :]

    count = count_ref[...]
    active = lax.broadcasted_iota(jnp.int32, (BLOCKS, EDGES), 0) < count
    readout = backs(16)
    energy = jnp.where(active, envelope * readout, 0.0)
    radial_pull = envelope_slope * readout
    along_sine, along_cosine = 0.0, 0.0
    for k in range(8):
        to_basis = backs(8 + k)
        along_sine = along_sine + to_basis * sines[k]
        along_cosine = along_cosine + to_basis * (cosines[k] * (k + 1.0))
    radial_pull = radial_pull + envelope * (along_sine * slope_sine + along_cosine * slope_cosine)
    y1, y2, y3, y4, y5, y6, y7, y8 = [backs(m) for m in range(8)]
    gx = root_three * y1 + root_fifteen * (uy * y4 + uz * y7 + ux * y8)
    gy = root_three * y2 + root_fifteen * (ux * y4 + uz * y5 - uy * y8)
    gz = root_three * y3 + root_fifteen * (uy * y5 + ux * y7) + (3.0 * root_five) * uz * y6
    turn_norm = envelope * inverse
    radial_pull = radial_pull - turn_norm * (gx * ux + gy * uy + gz * uz)
    pulls = [
        jnp.where(active, radial_pull * u + turn_norm * g, 0.0)
        for u, g in ((ux, gx), (uy, gy), (uz, gz))
    ]
    pulled[...] = jnp.zeros_like(pulled)
    for at, value in enumerate(pulls + [energy]):
        high, low = split(value)
        low_low = value - high.astype(F32) - low.astype(F32)
        for part, piece in enumerate((high.astype(F32), low.astype(F32), low_low)):
            pulled[pl.ds(4 * part + at, BLOCKS, stride=16), :] = piece
    near_atom = inner_atom(neighbours)
    far_atom = inner_atom(centre_rows)
    spots[...] = near_atom
    shift_rows[0:BLOCKS, :] = far_atom.astype(F32)

    def scatter(block, totals):
        atoms = lax.broadcasted_iota(jnp.int32, (64, EDGES), 0)
        near = jnp.where(atoms == spots[pl.ds(block, 1), :], 1.0, 0.0)
        far = jnp.where(atoms == shift_rows[pl.ds(block, 1), :].astype(jnp.int32), 1.0, 0.0)
        values = pulled[pl.ds(pl.multiple_of(16 * block, 16), 16), :].astype(BF16)
        return (
            totals[0] + dot_nt(values, (far - near).astype(BF16)),
            totals[1] + dot_nt(values, far.astype(BF16)),
        )

    start = jnp.zeros((16, 64), F32)
    force, energy = lax.fori_loop(0, BLOCKS, scatter, (start, start))
    forces_ref[...] = force[0:3] + force[4:7] + force[8:11]
    energies_ref[...] = energy[3:4] + energy[7:8] + energy[11:12]


def edge_scratch():
    return [
        pltpu.VMEM((80, ROWS), BF16),
        pltpu.VMEM((BLOCKS, EDGES), jnp.int32),
        pltpu.VMEM((PAIRS, 64, LANES), BF16),
        pltpu.VMEM((8 * BLOCKS, EDGES), F32),
        pltpu.VMEM((4 * BLOCKS, SLIM), F32),
        pltpu.VMEM((WIDE // 128, 4 * BLOCKS, 128), F32),
        pltpu.VMEM((8 * BLOCKS, EDGES), F32),
        pltpu.VMEM((8 * BLOCKS, EDGES), F32),
        pltpu.VMEM((24 * BLOCKS, EDGES), F32),
        pltpu.VMEM((16 * BLOCKS, EDGES), F32),
    ]


VMEM = pl.BlockSpec(memory_space=pltpu.VMEM)


def halo(features, shifts):
    return pl.pallas_call(
        halo_kernel,
        out_shape=(
            jax.ShapeDtypeStruct((ROWS, SLIM), BF16),
            jax.ShapeDtypeStruct((ROWS, WIDE), BF16),
        ),
        in_specs=[VMEM, VMEM],
        out_specs=(VMEM, VMEM),
        scratch_shapes=[
            pltpu.VMEM((2, 32, SLIM), BF16),
            pltpu.VMEM((2, 32, WIDE), BF16),
            pltpu.VMEM((2, 32, SLIM), BF16),
            pltpu.VMEM((2, 32, WIDE), BF16),
            pltpu.VMEM((64, SLIM), F32),
            pltpu.SemaphoreType.DMA((2, 2)),
            pltpu.SemaphoreType.DMA((2, 2)),
            pltpu.SemaphoreType.DMA((2, 2, SENDS)),
            pltpu.SemaphoreType.DMA((2, 2, SENDS)),
        ],
        compiler_params=pltpu.CompilerParams(
            collective_id=0, has_side_effects=True, vmem_limit_bytes=32 * 2**20
        ),
        name="halo",
    )(features, shifts)


def edges(slim, wide, *rest):
    def kernel(*refs):
        edges_kernel(*refs[:13], refs[13:])

    return pl.pallas_call(
        kernel,
        out_shape=(
            jax.ShapeDtypeStruct((1, 64), F32),
            jax.ShapeDtypeStruct((3, 64), F32),
        ),
        in_specs=[VMEM] * 11,
        out_specs=(VMEM, VMEM),
        scratch_shapes=edge_scratch(),
        compiler_params=pltpu.CompilerParams(vmem_limit_bytes=48 * 2**20),
        name="edges",
    )(slim, wide, *rest)


def per_device(
    features,
    shifts,
    block_counts,
    block_centres,
    block_neighbours,
    w_pair,
    w_radial,
    w_mix,
    w_self,
    w_tensor,
    w_out,
):
    slim, wide = halo(features.reshape(64, WIDE), shifts.reshape(64, 3))
    energies, forces = edges(
        slim,
        wide,
        block_counts.reshape(1, 1),
        block_centres.reshape(BLOCKS, 4),
        block_neighbours.reshape(BLOCKS, EDGES),
        w_pair,
        w_radial,
        w_mix,
        w_self,
        w_tensor,
        w_out.reshape(1, 128),
    )
    return energies.reshape(1, 1, 1, 64), forces.reshape(1, 1, 1, 3, 64)


def solution(mesh):
    in_specs = (
        P("bx", "by", "bz", None, None),
        P("bx", "by", "bz", None, None),
        P("bx", "by", "bz"),
        P("bx", "by", "bz", None, None),
        P("bx", "by", "bz", None, None),
        P(),
        P(),
        P(),
        P(),
        P(),
        P(),
    )
    out_specs = (P("bx", "by", "bz", None), P("bx", "by", "bz", None, None))
    return jax.shard_map(
        per_device, mesh=mesh, in_specs=in_specs, out_specs=out_specs, check_vma=False
    )
```

```python
import math

import jax
import jax.numpy as jnp
from jax import lax
from jax.experimental import pallas as pl
from jax.experimental.pallas import tpu as pltpu
from jax.sharding import PartitionSpec as P

MESH = pl.DeviceIdType.MESH
F32 = jnp.float32
BF16 = jnp.bfloat16

cutoff_radius = 6.0
site_spacing = 1.7
root_three = math.sqrt(3.0)
root_five = math.sqrt(5.0)
root_fifteen = math.sqrt(15.0)

ROWS = 512
HALF = 256
WIDE = 640
SLIM = 128
BLOCKS = 48
EDGES = 128
PAIRS = BLOCKS // 2
SCATTER = 24
GATHER = 12
FIRST = 12
SECOND = 8
LANES = 2 * EDGES


def phase_two_sends():
    return (
        (0, 1, 32, 64, 32),
        (0, -1, 0, 96, 32),
        (1, 0, 16, 128, 16),
        (1, 0, 48, 144, 16),
        (-1, 0, 0, 160, 16),
        (-1, 0, 32, 176, 16),
        (1, 1, 48, 192, 16),
        (1, -1, 16, 208, 16),
        (-1, 1, 32, 224, 16),
        (-1, -1, 0, 240, 16),
    )


SENDS = len(phase_two_sends())


def wrapped(axis, step):
    size = lax.axis_size(axis)
    return lax.rem(lax.axis_index(axis) + size + step, size)


def at_device(dx, dy, dz):
    return (wrapped("bx", dx), wrapped("by", dy), wrapped("bz", dz))


def octants(rows, order):
    return jnp.concatenate([rows[8 * o : 8 * o + 8] for o in order], axis=0)


def place_own(features_ref, shifts_ref, slim, wide, by_slim_out, by_wide_out, packed):
    packed[...] = jnp.zeros_like(packed)
    packed[:, 0:64] = features_ref[:, 0:64].astype(F32)
    packed[:, 64:67] = shifts_ref[...].astype(F32)
    own = [4 * ox + 2 * oy + oz for oz in range(2) for ox in range(2) for oy in range(2)]
    for source, table, out in (
        (packed[...], slim, by_slim_out),
        (features_ref[...].astype(F32), wide, by_wide_out),
    ):
        table[0:64, :] = octants(source, own).astype(BF16)
        for oy in range(2):
            face = [4 * ox + 2 * oy + oz for oz in range(2) for ox in range(2)]
            out[oy] = octants(source, face).astype(BF16)


def place_octants(table, first, landed, count):
    pieces = []
    below, above = landed[0].astype(F32), landed[1].astype(F32)
    for q in range(count):
        pieces += [below[8 * q : 8 * q + 8], above[8 * q : 8 * q + 8]]
    table[first : first + 16 * count, :] = jnp.concatenate(pieces, axis=0).astype(BF16)


def low_wrap():
    return lax.axis_index("bz") == 0


def high_wrap():
    return lax.axis_index("bz") == lax.axis_size("bz") - 1


def greet():
    barrier = pltpu.get_barrier_semaphore()
    partners = [(0, 1, 0), (0, -1, 0)] + [
        (dx, 0, dz) for dx in (-1, 0, 1) for dz in (-1, 0, 1) if dx or dz
    ]

    def signal(dx, dy, dz):
        pl.semaphore_signal(barrier, inc=1, device_id=at_device(dx, dy, dz), device_id_type=MESH)

    for wraps, dz in ((low_wrap, -1), (high_wrap, 1)):

        @pl.when(wraps())
        def _():
            signal(0, 1, dz)
            signal(0, -1, dz)

    for partner in partners:
        signal(*partner)
    return len(partners)


def meet(count):
    ends = jnp.where(low_wrap() | high_wrap(), 2, 0)
    pl.semaphore_wait(pltpu.get_barrier_semaphore(), count + ends)


class Exchange:
    def __init__(self, table, out, landed, corner, by_send, by_recv, send, recv):
        self.table, self.out, self.landed, self.corner = table, out, landed, corner
        self.by_send, self.by_recv, self.send, self.recv = by_send, by_recv, send, recv

    def copy(self, source, target, send, recv, dx, dy, dz):
        return pltpu.make_async_remote_copy(
            src_ref=source,
            dst_ref=target,
            send_sem=send,
            recv_sem=recv,
            device_id=at_device(dx, dy, dz),
            device_id_type=MESH,
        )

    def by_copies(self):
        return [
            self.copy(
                self.out.at[1 - side],
                self.landed.at[side],
                self.by_send.at[side],
                self.by_recv.at[side],
                0,
                1 - 2 * side,
                0,
            )
            for side in range(2)
        ]

    def corner_copies(self, dz):
        source = 16 if dz > 0 else 0
        return [
            self.copy(
                self.out.at[1 - side, pl.ds(source, 16)],
                self.corner.at[side],
                self.by_send.at[2 + side],
                self.by_recv.at[2 + side],
                0,
                1 - 2 * side,
                dz,
            )
            for side in range(2)
        ]

    def half_copies(self, half):
        return [
            (
                self.copy(
                    self.table.at[pl.ds(HALF * half + source, rows)],
                    self.table.at[pl.ds(HALF * half + target, rows)],
                    self.send.at[half, at],
                    self.recv.at[half, at],
                    dx,
                    0,
                    dz,
                ),
                dz,
            )
            for at, (dx, dz, source, target, rows) in enumerate(phase_two_sends())
        ]

    def late_copies(self, high):
        piece = HALF + (96 if high else 64)
        return [
            self.copy(
                self.table.at[pl.ds(piece + 16, 16)],
                self.table.at[pl.ds(HALF + 192 + 16 * high, 16)],
                self.send.at[2, 0],
                self.recv.at[2, 0],
                1,
                0,
                0,
            ),
            self.copy(
                self.table.at[pl.ds(piece, 16)],
                self.table.at[pl.ds(HALF + 224 + 16 * high, 16)],
                self.send.at[2, 1],
                self.recv.at[2, 1],
                -1,
                0,
                0,
            ),
        ]

    def start_far(self):
        for copy in self.by_copies():
            copy.start()
        for wraps, dz in ((low_wrap, -1), (high_wrap, 1)):

            @pl.when(wraps())
            def _():
                for copy in self.corner_copies(dz):
                    copy.start()

    def start_own(self):
        for copy, _ in self.half_copies(0):
            copy.start()

    def pass_on(self):
        for copy in self.by_copies():
            copy.wait_recv()
        place_octants(self.table, HALF, self.landed, 4)
        for copy, dz in self.half_copies(1):
            if dz == 0:
                copy.start()
            else:

                @pl.when(jnp.logical_not(high_wrap() if dz > 0 else low_wrap()))
                def _():
                    copy.start()

        for wraps, dz in ((low_wrap, -1), (high_wrap, 1)):

            @pl.when(wraps())
            def _():
                for copy in self.corner_copies(dz):
                    copy.wait_recv()
                place_octants(self.table, HALF + (64 if dz < 0 else 96), self.corner, 2)
                for copy in self.late_copies(int(dz > 0)):
                    copy.start()

    def arrive(self):
        for copy, _ in self.half_copies(0):
            copy.wait_recv()
        for copy, dz in self.half_copies(1):
            if dz == 0:
                copy.wait_recv()
            else:

                @pl.when(jnp.logical_not(low_wrap() if dz > 0 else high_wrap()))
                def _():
                    copy.wait_recv()

        for wraps, high in ((low_wrap, 0), (high_wrap, 1)):

            @pl.when(wraps())
            def _():
                for copy in self.late_copies(high):
                    copy.wait_recv()

    def close(self):
        for copy in self.by_copies():
            copy.wait_send()
        for copy, _ in self.half_copies(0):
            copy.wait_send()
        for copy, dz in self.half_copies(1):
            if dz == 0:
                copy.wait_send()
            else:

                @pl.when(jnp.logical_not(high_wrap() if dz > 0 else low_wrap()))
                def _():
                    copy.wait_send()

        for wraps, high in ((low_wrap, 0), (high_wrap, 1)):

            @pl.when(wraps())
            def _():
                for copy in self.corner_copies(2 * high - 1) + self.late_copies(high):
                    copy.wait_send()


def dot_nn(left, right):
    return lax.dot_general(left, right, (((1,), (0,)), ((), ())), preferred_element_type=F32)


def dot_nt(left, right):
    return lax.dot_general(left, right, (((1,), (1,)), ((), ())), preferred_element_type=F32)


def split(value):
    high = value.astype(BF16)
    return high, (value - high.astype(F32)).astype(BF16)


def cell_digits(row):
    return row >> 7, (row >> 5) & 3, (row >> 3) & 3, row & 7


def coordinates(row):
    ci, cj, ck, w = cell_digits(row)
    return (
        2 * (ci - 1) + (w >> 2),
        2 * (cj - 1) + ((w >> 1) & 1),
        2 * (ck - 1) + (w & 1),
    )


def table_row(row):
    ci, cj, ck, w = cell_digits(row)
    ox, oz = ci - 1, ck - 1
    inner_x = (ci == 1) | (ci == 2)
    inner_y = (cj == 1) | (cj == 2)
    inner_z = (ck == 1) | (ck == 2)
    x_side, z_side = ci >> 1, ck >> 1
    base = jnp.where(
        inner_x,
        jnp.where(inner_z, 32 * oz + 16 * ox, 64 + 32 * z_side + 16 * ox),
        jnp.where(inner_z, 128 + 32 * x_side + 16 * oz, 192 + 32 * x_side + 16 * z_side),
    )
    y_part = jnp.where(inner_y, 8 * (cj - 1), HALF + 8 * (cj >> 1))
    return base + y_part + w


def inner_atom(row):
    ci, cj, ck, w = cell_digits(row)
    inside = (ci == 1) | (ci == 2)
    inside = inside & ((cj == 1) | (cj == 2)) & ((ck == 1) | (ck == 2))
    return jnp.where(inside, 8 * (4 * (ci - 1) + 2 * (cj - 1) + ck - 1) + w, -1)


def lane_slot(shape):
    return lax.broadcasted_iota(jnp.int32, shape, 1) >> 5


def over_edges(columns, slots):
    spread = [jnp.broadcast_to(column, slots.shape) for column in columns]
    low = jnp.where(slots == 0, spread[0], spread[1])
    high = jnp.where(slots == 2, spread[2], spread[3])
    return jnp.where(slots < 2, low, high)


def slot_mask():
    slots = lane_slot((8, LANES))
    return jnp.where(slots == lax.broadcasted_iota(jnp.int32, (8, LANES), 0), 1.0, 0.0).astype(F32)


def edge_work(
    stop,
    slim_ready,
    wide_ready,
    slim,
    wide,
    count_ref,
    centres_ref,
    neighbours_ref,
    w_pair_ref,
    w_radial_ref,
    w_mix_ref,
    w_self_ref,
    w_tensor_ref,
    w_out_ref,
    energies_ref,
    forces_ref,
    turned,
    spots,
    scalars,
    shift_rows,
    centre_slim,
    centre_wide,
    basis_rows,
    sphere_rows,
    back_rows,
    pulled,
    far_spots,
    latent_rows,
    slope_rows,
    mixing_rows,
):
    neighbours = neighbours_ref[...]
    centres = centres_ref[...]
    spots[...] = table_row(neighbours)
    centre_spots = table_row(centres)
    slots = lane_slot((BLOCKS, EDGES))
    centre_rows = over_edges([centres[:, j : j + 1] for j in range(4)], slots)
    steps = [
        (one - other).astype(F32) * site_spacing
        for one, other in zip(coordinates(neighbours), coordinates(centre_rows))
    ]
    mask = slot_mask()
    w_pair = w_pair_ref[...]
    radial = w_radial_ref[...]
    radial_high, radial_low = split(radial)
    radial_rows = jnp.concatenate([radial_high.astype(F32), radial_low.astype(F32)], axis=0).astype(BF16)
    w_mix = w_mix_ref[...].astype(F32)
    mix_turned = w_mix.T
    mix_turned = jnp.concatenate(
        [mix_turned[128:192], mix_turned[64:128], mix_turned[0:64]], axis=0
    )
    mix_back = mix_turned.T.astype(BF16)
    mix_turned = mix_turned.astype(BF16)
    update = jnp.concatenate([w_self_ref[...], w_tensor_ref[...]], axis=0)
    update_turned = update.astype(F32).T.astype(BF16)
    w_out = jnp.broadcast_to(w_out_ref[...].astype(F32), (128, 128)).T
    w_out = jnp.concatenate([w_out, w_out], axis=1)
    low_half = lax.broadcasted_iota(jnp.int32, (8, 128), 1) < 64
    nothing = jnp.zeros((8, 128), F32)

    slim_ready()
    if stop == 0:
        return

    turned[...] = slim[...].astype(F32).T[0:80].astype(BF16)

    centre_shift = []
    lanes_of_rows = lax.broadcasted_iota(jnp.int32, (BLOCKS, ROWS), 1)
    for place in range(4):
        hits = jnp.where(centre_spots[:, place : place + 1] == lanes_of_rows, 1.0, 0.0).astype(BF16)
        got = dot_nn(hits, slim[...])
        centre_slim[pl.ds(place, BLOCKS, stride=4), :] = got
        centre_shift.append([got[:, 64 + axis : 65 + axis] for axis in range(3)])

    def gather(turn, _):
        rows = lax.broadcasted_iota(jnp.int32, (ROWS, EDGES), 0).astype(jnp.int16)
        one, none = jnp.ones((), BF16), jnp.zeros((), BF16)
        for pair in [turn * GATHER + at for at in range(GATHER)]:
            hits = []
            for block in range(2):
                spot = spots[pl.ds(2 * pair + block, 1), :].astype(jnp.int16)
                hits.append(jnp.where(rows == spot, one, none))
            got = dot_nn(turned[...], jnp.concatenate(hits, axis=1))
            scalars[pair] = got[0:64].astype(BF16)
            for block in range(2):
                shift_rows[pl.ds(pl.multiple_of((2 * pair + block) * 8, 8), 8), :] = got[
                    64:72, EDGES * block : EDGES * block + EDGES
                ]
        return 0

    lax.fori_loop(0, PAIRS // GATHER, gather, 0)
    if stop == 1:
        return

    vector = []
    for axis in range(3):
        near = shift_rows[pl.ds(axis, BLOCKS, stride=8), :]
        far = over_edges([centre_shift[j][axis] for j in range(4)], slots)
        vector.append(steps[axis] + (near - far))
    distance = jnp.sqrt(vector[0] * vector[0] + vector[1] * vector[1] + vector[2] * vector[2])
    inverse = 1.0 / distance
    ux, uy, uz = [part * inverse for part in vector]
    inside = distance < cutoff_radius
    scaled = jnp.minimum(distance * (1.0 / cutoff_radius), 1.0)
    fifth = (scaled * scaled) * (scaled * scaled) * scaled
    envelope = 1.0 - fifth * scaled * (28.0 - scaled * (48.0 - 21.0 * scaled))
    envelope_slope = jnp.where(
        inside, fifth * (-168.0 + scaled * (336.0 - 168.0 * scaled)) * (1.0 / cutoff_radius), 0.0
    )
    sine, cosine = jnp.sin(math.pi * scaled), jnp.cos(math.pi * scaled)
    norm = math.sqrt(2.0 / cutoff_radius) * inverse
    cut_norm = norm * envelope
    slope_sine = norm * (envelope_slope - envelope * inverse)
    slope_cosine = jnp.where(inside, cut_norm * (math.pi / cutoff_radius), 0.0)
    sines, cosines = [sine], [cosine]
    for _ in range(7):
        s, c = sines[-1], cosines[-1]
        sines.append(s * cosine + c * sine)
        cosines.append(c * cosine - s * sine)
    for k in range(8):
        basis_rows[pl.ds(k, BLOCKS, stride=8), :] = sines[k] * cut_norm
    sphere = (
        root_three * ux,
        root_three * uy,
        root_three * uz,
        root_fifteen * ux * uy,
        root_fifteen * uy * uz,
        0.5 * root_five * (3.0 * uz * uz - 1.0),
        root_fifteen * ux * uz,
        0.5 * root_fifteen * (ux * ux - uy * uy),
    )
    for m in range(8):
        sphere_rows[pl.ds(m, BLOCKS, stride=8), :] = sphere[m]

    centre_slim[...] = dot_nn(centre_slim[:, 0:64].astype(BF16), w_pair[0:64])

    if stop == 2:
        return

    def latents(pair):
        at = pl.multiple_of(8 * pair, 8)
        high, low = split(centre_slim[pl.ds(at, 8), :])
        left = jnp.concatenate(
            [
                w_pair[64:128].astype(F32),
                high.astype(F32),
                low.astype(F32),
                radial_high.astype(F32),
                radial_high.astype(F32),
                radial_low.astype(F32),
                jnp.zeros((24, 128), F32),
            ],
            axis=0,
        ).T.astype(BF16)
        at = pl.multiple_of(16 * pair, 16)
        basis = jnp.concatenate(
            [basis_rows[pl.ds(at, 8), :], basis_rows[pl.ds(at + 8, 8), :]], axis=1
        )
        high, low = split(basis)
        right = jnp.concatenate(
            [mask, mask, high.astype(F32), low.astype(F32), high.astype(F32), jnp.zeros((24, LANES), F32)],
            axis=0,
        ).astype(BF16)
        return dot_nn(left, jnp.concatenate([scalars[pair], right], axis=0))

    def tensors(pair):
        at = pl.multiple_of(8 * pair, 8)
        parts = [centre_wide[g, pl.ds(at, 8), :] for g in range(5)]
        turns = [pltpu.roll(part, 64, 1) for part in parts]
        order_one = [turns[1], parts[1], turns[2]]
        order_two = [turns[2], parts[3], turns[3], parts[4], turns[4]]
        rows = [jnp.where(low_half, 0.0, part) for part in order_one]
        rows += [jnp.where(low_half, part, 0.0) for part in order_two]
        back = jnp.concatenate(rows, axis=0)
        zero = jnp.where(low_half, turns[0], 0.0)
        first = jnp.concatenate([back, nothing, nothing], axis=0).T
        second = jnp.concatenate([nothing] * 8 + [zero, nothing], axis=0).T[0:64]
        front = jnp.concatenate([first, second], axis=0)
        return front.astype(BF16), back.astype(BF16)

    def spheres(pair):
        at = pl.multiple_of(16 * pair, 16)
        sphere = jnp.concatenate(
            [sphere_rows[pl.ds(at, 8), :], sphere_rows[pl.ds(at + 8, 8), :]], axis=1
        )
        rows = [jnp.broadcast_to(sphere[m : m + 1], (8, LANES)) * mask for m in range(8)]
        return jnp.concatenate(rows + [mask, jnp.zeros((8, LANES), F32)], axis=0).astype(BF16)

    def silu_parts(x):
        gate = 0.5 * jnp.tanh(0.5 * x) + 0.5
        value = x * gate
        return value, gate + value * (1.0 - gate)

    each = range(FIRST)

    def first_group(turn, _):
        pairs = [turn * FIRST + g for g in each]
        first = [silu_parts(latents(p)) for p in pairs]
        for g in each:
            latent = first[g][0].astype(BF16)
            latent_rows[pairs[g]] = latent
            slope_rows[pairs[g]] = first[g][1]
            mixing_rows[pairs[g]] = dot_nn(mix_turned, latent)
        return 0

    lax.fori_loop(0, PAIRS // FIRST, first_group, 0)
    if stop == 3:
        return

    wide_ready()
    for place in range(4):
        hits = jnp.where(centre_spots[:, place : place + 1] == lanes_of_rows, 1.0, 0.0).astype(BF16)
        got = dot_nn(hits, wide[...])
        for at in range(WIDE // 128):
            centre_wide[at, pl.ds(place, BLOCKS, stride=4), :] = got[:, 128 * at : 128 * at + 128]

    if stop == 4:
        return

    def second_group(turn, _):
        each = range(SECOND)
        pairs = [turn * SECOND + g for g in each]
        sides = [tensors(p) for p in pairs]
        contracted = [dot_nn(sides[g][0], spheres(pairs[g])) for g in each]
        mixing = [mixing_rows[p] for p in pairs]
        coupled = []
        for g in each:
            product = mixing[g] * contracted[g]
            coupled.append((product[0:64] + product[64:128] + product[128:192]).astype(BF16))
        hidden_in = [
            dot_nn(update_turned, jnp.concatenate([latent_rows[pairs[g]], coupled[g]], axis=0))
            for g in each
        ]
        second = [silu_parts(x) for x in hidden_in]
        readout = [jnp.sum(value * w_out, axis=0, keepdims=True) for value, _ in second]
        back = [dot_nn(update, (slope * w_out).astype(BF16)) for _, slope in second]
        for g in each:
            cotangent = back[g][128:192].astype(BF16).astype(F32)
            cotangents = jnp.concatenate([cotangent, cotangent, cotangent], axis=0)
            to_mixing = (cotangents * contracted[g]).astype(BF16)
            to_contracted = (cotangents[0:128] * mixing[g][0:128]).astype(BF16)
            to_latent = back[g][0:128] + dot_nn(mix_back, to_mixing)
            to_sphere = dot_nn(sides[g][1], to_contracted)
            to_sphere = jnp.sum(to_sphere.reshape(8, 8, LANES) * mask[None], axis=1)
            to_input = (to_latent * slope_rows[pairs[g]]).astype(BF16)
            to_basis = dot_nn(radial_rows, to_input)
            to_basis = to_basis[0:8] + to_basis[8:16]
            for block in range(2):
                at = (2 * pairs[g] + block) * 24
                lanes = slice(EDGES * block, EDGES * block + EDGES)
                back_rows[pl.ds(pl.multiple_of(at, 8), 8), :] = to_sphere[:, lanes]
                back_rows[pl.ds(pl.multiple_of(at + 8, 8), 8), :] = to_basis[:, lanes]
                back_rows[pl.ds(pl.multiple_of(at + 16, 8), 8), :] = jnp.broadcast_to(
                    readout[g][:, lanes], (8, EDGES)
                )
        return 0

    lax.fori_loop(0, PAIRS // SECOND, second_group, 0)
    if stop == 5:
        return

    def backs(row):
        return back_rows[pl.ds(row, BLOCKS, stride=24), :]

    count = count_ref[...]
    active = lax.broadcasted_iota(jnp.int32, (BLOCKS, EDGES), 0) < count
    readout = backs(16)
    energy = jnp.where(active, envelope * readout, 0.0)
    radial_pull = envelope_slope * readout
    along_sine, along_cosine = 0.0, 0.0
    for k in range(8):
        to_basis = backs(8 + k)
        along_sine = along_sine + to_basis * sines[k]
        along_cosine = along_cosine + to_basis * (cosines[k] * (k + 1.0))
    radial_pull = radial_pull + envelope * (along_sine * slope_sine + along_cosine * slope_cosine)
    y1, y2, y3, y4, y5, y6, y7, y8 = [backs(m) for m in range(8)]
    gx = root_three * y1 + root_fifteen * (uy * y4 + uz * y7 + ux * y8)
    gy = root_three * y2 + root_fifteen * (ux * y4 + uz * y5 - uy * y8)
    gz = root_three * y3 + root_fifteen * (uy * y5 + ux * y7) + (3.0 * root_five) * uz * y6
    turn_norm = envelope * inverse
    radial_pull = radial_pull - turn_norm * (gx * ux + gy * uy + gz * uz)
    pulls = [
        jnp.where(active, radial_pull * u + turn_norm * g, 0.0)
        for u, g in ((ux, gx), (uy, gy), (uz, gz))
    ]
    for at, value in enumerate(pulls + [energy]):
        high, low = split(value)
        pulled[pl.ds(at, BLOCKS, stride=8), :] = high.astype(F32)
        pulled[pl.ds(4 + at, BLOCKS, stride=8), :] = low.astype(F32)
    spots[...] = inner_atom(neighbours)
    far_spots[...] = inner_atom(centre_rows)
    if stop == 6:
        return

    def scatter(turn, total):
        near, far, values = [], [], []
        atoms = lax.broadcasted_iota(jnp.int32, (64, EDGES), 0).astype(jnp.int16)
        one, none = jnp.ones((), BF16), jnp.zeros((), BF16)
        for at in range(SCATTER):
            block = turn * SCATTER + at
            spot = spots[pl.ds(block, 1), :].astype(jnp.int16)
            near.append(jnp.where(atoms == spot, one, none))
            spot = far_spots[pl.ds(block, 1), :].astype(jnp.int16)
            far.append(jnp.where(atoms == spot, one, none))
            values.append(pulled[pl.ds(pl.multiple_of(8 * block, 8), 8), :])
        near = jnp.concatenate(near, axis=1)
        far = jnp.concatenate(far, axis=1)
        values = jnp.concatenate(values, axis=1).astype(BF16)
        return total + dot_nt(jnp.concatenate([far - near, far], axis=0), values)

    total = lax.fori_loop(0, BLOCKS // SCATTER, scatter, jnp.zeros((128, 8), F32))
    total = jnp.concatenate([total, jnp.zeros((128, 120), F32)], axis=1).T
    forces_ref[...] = total[0:3, 0:64] + total[4:7, 0:64]
    energies_ref[...] = total[3:4, 64:128] + total[7:8, 64:128]


def edge_scratch():
    return [
        pltpu.VMEM((80, ROWS), BF16),
        pltpu.VMEM((BLOCKS, EDGES), jnp.int32),
        pltpu.VMEM((PAIRS, 64, LANES), BF16),
        pltpu.VMEM((8 * BLOCKS, EDGES), F32),
        pltpu.VMEM((4 * BLOCKS, SLIM), F32),
        pltpu.VMEM((WIDE // 128, 4 * BLOCKS, 128), F32),
        pltpu.VMEM((8 * BLOCKS, EDGES), F32),
        pltpu.VMEM((8 * BLOCKS, EDGES), F32),
        pltpu.VMEM((24 * BLOCKS, EDGES), F32),
        pltpu.VMEM((8 * BLOCKS, EDGES), F32),
        pltpu.VMEM((BLOCKS, EDGES), jnp.int32),
        pltpu.VMEM((PAIRS, 128, LANES), BF16),
        pltpu.VMEM((PAIRS, 128, LANES), F32),
        pltpu.VMEM((PAIRS, 192, LANES), F32),
    ]


HALO_SCRATCH = 13


def whole_kernel(features_ref, shifts_ref, *refs):
    operands, refs = refs[:11], refs[11:]
    slim, wide, by_slim_out, by_wide_out, by_slim_in, by_wide_in = refs[:6]
    corner_slim, corner_wide, packed, by_send, by_recv, send_sem, recv_sem = refs[6:HALO_SCRATCH]
    partners = greet()
    place_own(features_ref, shifts_ref, slim, wide, by_slim_out, by_wide_out, packed)
    exchanges = [
        Exchange(
            table, out, landed, corner, by_send.at[t], by_recv.at[t], send_sem.at[t], recv_sem.at[t]
        )
        for t, (table, out, landed, corner) in enumerate(
            (
                (slim, by_slim_out, by_slim_in, corner_slim),
                (wide, by_wide_out, by_wide_in, corner_wide),
            )
        )
    ]

    def slim_ready():
        meet(partners)
        for exchange in exchanges:
            exchange.start_far()
        for exchange in exchanges:
            exchange.start_own()
        for exchange in exchanges:
            exchange.pass_on()
        exchanges[0].arrive()

    def wide_ready():
        exchanges[1].arrive()

    edge_work(None, slim_ready, wide_ready, slim, wide, *operands, *refs[HALO_SCRATCH:])
    for exchange in exchanges:
        exchange.close()


VMEM = pl.BlockSpec(memory_space=pltpu.VMEM)


def whole(*operands):
    return pl.pallas_call(
        whole_kernel,
        out_shape=(
            jax.ShapeDtypeStruct((1, 64), F32),
            jax.ShapeDtypeStruct((3, 64), F32),
        ),
        in_specs=[VMEM] * 11,
        out_specs=(VMEM, VMEM),
        scratch_shapes=[
            pltpu.VMEM((ROWS, SLIM), BF16),
            pltpu.VMEM((ROWS, WIDE), BF16),
            pltpu.VMEM((2, 32, SLIM), BF16),
            pltpu.VMEM((2, 32, WIDE), BF16),
            pltpu.VMEM((2, 32, SLIM), BF16),
            pltpu.VMEM((2, 32, WIDE), BF16),
            pltpu.VMEM((2, 16, SLIM), BF16),
            pltpu.VMEM((2, 16, WIDE), BF16),
            pltpu.VMEM((64, SLIM), F32),
            pltpu.SemaphoreType.DMA((2, 4)),
            pltpu.SemaphoreType.DMA((2, 4)),
            pltpu.SemaphoreType.DMA((2, 3, SENDS)),
            pltpu.SemaphoreType.DMA((2, 3, SENDS)),
        ]
        + edge_scratch(),
        compiler_params=pltpu.CompilerParams(
            collective_id=0, has_side_effects=True, vmem_limit_bytes=56 * 2**20
        ),
        name="boxes",
    )(*operands)


def per_device(
    features,
    shifts,
    block_counts,
    block_centres,
    block_neighbours,
    w_pair,
    w_radial,
    w_mix,
    w_self,
    w_tensor,
    w_out,
):
    energies, forces = whole(
        features.reshape(64, WIDE),
        shifts.reshape(64, 3),
        block_counts.reshape(1, 1),
        block_centres.reshape(BLOCKS, 4),
        block_neighbours.reshape(BLOCKS, EDGES),
        w_pair,
        w_radial,
        w_mix,
        w_self,
        w_tensor,
        w_out.reshape(1, 128),
    )
    return energies.reshape(1, 1, 1, 64), forces.reshape(1, 1, 1, 3, 64)


def solution(mesh):
    in_specs = (
        P("bx", "by", "bz", None, None),
        P("bx", "by", "bz", None, None),
        P("bx", "by", "bz"),
        P("bx", "by", "bz", None, None),
        P("bx", "by", "bz", None, None),
        P(),
        P(),
        P(),
        P(),
        P(),
        P(),
    )
    out_specs = (P("bx", "by", "bz", None), P("bx", "by", "bz", None, None))
    return jax.shard_map(
        per_device, mesh=mesh, in_specs=in_specs, out_specs=out_specs, check_vma=False
    )
```

```python
import functools
import math

import jax
import jax.numpy as jnp
from jax import lax
from jax.experimental import pallas as pl
from jax.experimental.pallas import tpu as pltpu
from jax.sharding import PartitionSpec as P

MESH = pl.DeviceIdType.MESH
F32 = jnp.float32
BF16 = jnp.bfloat16

cutoff_radius = 6.0
site_spacing = 1.7
root_three = math.sqrt(3.0)
root_five = math.sqrt(5.0)
root_fifteen = math.sqrt(15.0)

ROWS = 512
HALF = 256
WIDE = 640
SLIM = 128
BLOCKS = 48
EDGES = 128
PAIRS = BLOCKS // 2
SCATTER = 24
GATHER = 12
FIRST = 12
SECOND = 8
LANES = 2 * EDGES


def phase_two_sends():
    return (
        (0, 1, 32, 64, 32),
        (0, -1, 0, 96, 32),
        (1, 0, 16, 128, 16),
        (1, 0, 48, 144, 16),
        (-1, 0, 0, 160, 16),
        (-1, 0, 32, 176, 16),
        (1, 1, 48, 192, 16),
        (1, -1, 16, 208, 16),
        (-1, 1, 32, 224, 16),
        (-1, -1, 0, 240, 16),
    )


SENDS = len(phase_two_sends())


def wrapped(axis, step):
    size = lax.axis_size(axis)
    return lax.rem(lax.axis_index(axis) + size + step, size)


def at_device(dx, dy, dz):
    return (wrapped("bx", dx), wrapped("by", dy), wrapped("bz", dz))


def octants(rows, order):
    return jnp.concatenate([rows[8 * o : 8 * o + 8] for o in order], axis=0)


def place_own(features_ref, shifts_ref, slim, wide, by_slim_out, by_wide_out, packed):
    packed[...] = jnp.zeros_like(packed)
    packed[:, 0:64] = features_ref[:, 0:64].astype(F32)
    packed[:, 64:72] = turned_rows(shifts_ref[...].astype(F32))[0:64]
    own = [4 * ox + 2 * oy + oz for oz in range(2) for ox in range(2) for oy in range(2)]
    for source, table, out in (
        (packed[...], slim, by_slim_out),
        (features_ref[...].astype(F32), wide, by_wide_out),
    ):
        table[0:64, :] = octants(source, own).astype(BF16)
        for oy in range(2):
            face = [4 * ox + 2 * oy + oz for oz in range(2) for ox in range(2)]
            out[oy] = octants(source, face).astype(BF16)


def place_octants(table, first, landed, count):
    pieces = []
    below, above = landed[0].astype(F32), landed[1].astype(F32)
    for q in range(count):
        pieces += [below[8 * q : 8 * q + 8], above[8 * q : 8 * q + 8]]
    table[first : first + 16 * count, :] = jnp.concatenate(pieces, axis=0).astype(BF16)


class Place:
    def __init__(self):
        self.bx, self.by, self.bz = (lax.axis_index(axis) for axis in ("bx", "by", "bz"))
        self.ends = lax.axis_size("bz") - 1
        self.x, self.z_hi = lax.rem(self.by, 4), lax.div(self.by, 4)
        self.first_x, self.last_x = self.x == 0, self.x == 3
        self.edge = self.first_x | self.last_x
        self.early = self.z_hi == 0
        self.late = self.z_hi == 1
        self.low = self.bz == 0
        self.high = self.bz == self.ends
        self.middle = lax.div(lax.axis_size("bz"), 2)
        self.upper = self.bz >= self.middle
        self.by_helper = jnp.logical_not(self.edge) & self.late & (self.bz < self.middle)
        self.wrap_helper = self.late & (self.bz == self.middle)


def flips(place, side):
    return place.last_x if side == 0 else place.first_x


def signal(semaphore, device):
    pl.semaphore_signal(semaphore, inc=1, device_id=device, device_id_type=MESH)


def as_count(condition, amount):
    return jnp.where(condition, amount, 0)


def greet(place):
    barrier = pltpu.get_barrier_semaphore()
    for dx in (-1, 1):
        signal(barrier, at_device(dx, 0, 0))
    for side, dy in ((0, 1), (1, -1)):

        @pl.when(jnp.logical_not(flips(place, side)) | place.early)
        def _():
            signal(barrier, at_device(0, dy, 0))

    for dx in (-1, 0, 1):
        signal(barrier, at_device(dx, 0, -1))

        @pl.when(jnp.logical_not(place.high))
        def _():
            signal(barrier, at_device(dx, 0, 1))

    for side, dy in ((0, 1), (1, -1)):

        @pl.when(place.low)
        def _():
            signal(barrier, at_device(0, dy, -1))

        @pl.when(place.high & place.early & flips(place, side))
        def _():
            signal(barrier, at_device(0, dy, 1))

    @pl.when(place.edge & place.upper)
    def _():
        near_first = place.first_x == place.early
        signal(barrier, (place.bx, jnp.where(near_first, 5, 6), place.bz - place.middle))

    @pl.when(place.late & place.low)
    def _():
        signal(barrier, (place.bx, place.by, place.middle))

    @pl.when(place.late & place.high)
    def _():
        for dx in (-1, 0, 1):
            signal(barrier, (wrapped("bx", dx), place.by, place.middle))

        for side, dy in ((0, 1), (1, -1)):

            @pl.when(jnp.logical_not(flips(place, side)))
            def _():
                signal(barrier, (place.bx, place.by + dy, place.middle))


def meet(place):
    count = 2 + as_count(jnp.logical_not(place.edge), 1) + 1
    count = count + as_count(place.edge & place.late, 1)
    count = count + as_count(jnp.logical_not(place.low), 3) + 3
    count = count + as_count(place.high, 2)
    count = count + as_count(place.low & place.late & place.edge, 1)
    count = count + as_count(place.by_helper, 2)
    count = count + as_count(place.wrap_helper, 5 + as_count(jnp.logical_not(place.edge), 1))
    pl.semaphore_wait(pltpu.get_barrier_semaphore(), count)


def help_others(place, go):
    @pl.when(place.by_helper)
    def _():
        signal(go.at[0], (place.bx, jnp.where(place.x == 1, 0, 3), place.bz + place.middle))

    @pl.when(place.wrap_helper)
    def _():
        signal(go.at[1], (place.bx, place.by, 0))


class Exchange:
    def __init__(self, place, table, out, landed, corner, by_send, by_recv, send, recv):
        self.place = place
        self.table, self.out, self.landed, self.corner = table, out, landed, corner
        self.by_send, self.by_recv, self.send, self.recv = by_send, by_recv, send, recv

    def copy(self, source, target, send, recv, dx, dy, dz):
        return pltpu.make_async_remote_copy(
            src_ref=source,
            dst_ref=target,
            send_sem=send,
            recv_sem=recv,
            device_id=at_device(dx, dy, dz),
            device_id_type=MESH,
        )

    def by_copy(self, side):
        return self.copy(
            self.out.at[1 - side],
            self.landed.at[side],
            self.by_send.at[side],
            self.by_recv.at[side],
            0,
            1 - 2 * side,
            0,
        )

    def corner_copy(self, dz, side):
        return self.copy(
            self.out.at[1 - side, pl.ds(16 if dz > 0 else 0, 16)],
            self.corner.at[side],
            self.by_send.at[2 + side],
            self.by_recv.at[2 + side],
            0,
            1 - 2 * side,
            dz,
        )

    def half_copies(self, half):
        return [
            (
                functools.partial(
                    self.copy,
                    self.table.at[pl.ds(HALF * half + source, rows)],
                    self.table.at[pl.ds(HALF * half + target, rows)],
                    self.send.at[half, at],
                    self.recv.at[half, at],
                    dx,
                    0,
                    dz,
                ),
                dz,
            )
            for at, (dx, dz, source, target, rows) in enumerate(phase_two_sends())
        ]

    def late_copies(self, high):
        piece = HALF + (96 if high else 64)
        return [
            self.copy(
                self.table.at[pl.ds(piece + 16, 16)],
                self.table.at[pl.ds(HALF + 192 + 16 * high, 16)],
                self.send.at[2, 0],
                self.recv.at[2, 0],
                1,
                0,
                0,
            ),
            self.copy(
                self.table.at[pl.ds(piece, 16)],
                self.table.at[pl.ds(HALF + 224 + 16 * high, 16)],
                self.send.at[2, 1],
                self.recv.at[2, 1],
                -1,
                0,
                0,
            ),
        ]

    def start_by(self, far):
        for side in range(2):

            @pl.when(flips(self.place, side) if far else jnp.logical_not(flips(self.place, side)))
            def _():
                self.by_copy(side).start()

    def start_wrap(self, dz):
        for copy, along in self.half_copies(0):
            if along == dz:
                copy().start()

    def start_corners(self, dz, flipped=(True, False)):
        for side in range(2):
            if len(flipped) == 2:
                self.corner_copy(dz, side).start()
            else:

                @pl.when(flips(self.place, side) == flipped[0])
                def _():
                    self.corner_copy(dz, side).start()

    def start_own(self):
        for copy, dz in self.half_copies(0):
            if dz == 0:
                copy().start()
            else:

                @pl.when(jnp.logical_not(self.place.high if dz > 0 else self.place.low))
                def _():
                    copy().start()

    def spread_by(self):
        place_octants(self.table, HALF, self.landed, 4)
        for copy, dz in self.half_copies(1):
            if dz == 0:
                copy().start()
            else:

                @pl.when(jnp.logical_not(self.place.high if dz > 0 else self.place.low))
                def _():
                    copy().start()

    def wait_corners(self, dz):
        for side in range(2):
            self.corner_copy(dz, side).wait_recv()

    def take_corners(self, dz):
        place_octants(self.table, HALF + (64 if dz < 0 else 96), self.corner, 2)
        for copy in self.late_copies(int(dz > 0)):
            copy.start()

    def wait_wrap(self, dz):
        for copy, along in self.half_copies(0):
            if along == dz:
                copy().wait_recv()

    def arrive(self):
        for copy, dz in self.half_copies(0):
            if self.wraps_waited(dz):

                @pl.when(jnp.logical_not(self.place.low & self.place.early))
                def _():
                    copy().wait_recv()
            else:
                copy().wait_recv()
        for copy, dz in self.half_copies(1):
            if dz == 0:
                copy().wait_recv()
            else:

                @pl.when(jnp.logical_not(self.place.low if dz > 0 else self.place.high))
                def _():
                    copy().wait_recv()

        for wraps, high in ((self.place.low, 0), (self.place.high, 1)):

            @pl.when(wraps)
            def _():
                for copy in self.late_copies(high):
                    copy.wait_recv()

    def wraps_waited(self, dz):
        return False

    def close(self):
        for side in range(2):
            self.by_copy(side).wait_send()
        for copy, _ in self.half_copies(0):
            copy().wait_send()
        for copy, dz in self.half_copies(1):
            if dz == 0:
                copy().wait_send()
            else:

                @pl.when(jnp.logical_not(self.place.high if dz > 0 else self.place.low))
                def _():
                    copy().wait_send()

        for wraps, high in ((self.place.low, 0), (self.place.high, 1)):

            @pl.when(wraps)
            def _():
                for side in range(2):
                    self.corner_copy(2 * high - 1, side).wait_send()
                for copy in self.late_copies(high):
                    copy.wait_send()


class SlimExchange(Exchange):
    def wraps_waited(self, dz):
        return dz > 0


def start_first(place, exchanges):
    slim, wide = exchanges

    @pl.when(place.edge & place.late)
    def _():
        for exchange in exchanges:
            exchange.start_by(True)

    @pl.when(place.high)
    def _():
        slim.start_corners(1)
        slim.start_wrap(1)
        wide.start_corners(1)

    @pl.when(place.low & place.late)
    def _():
        for exchange in exchanges:
            exchange.start_corners(-1, (True,))

    for exchange in exchanges:
        exchange.start_by(False)
    slim.start_own()


def start_second(place, exchanges, go):
    wide = exchanges[1]
    wide.start_own()

    @pl.when(place.high)
    def _():
        wide.start_wrap(1)

    @pl.when(place.edge & place.early & place.upper)
    def _():
        pl.semaphore_wait(go.at[0], 1)
        for exchange in exchanges:
            exchange.start_by(True)

    @pl.when(place.low & place.late)
    def _():
        pl.semaphore_wait(go.at[1], 1)
        for exchange in exchanges:
            exchange.start_wrap(-1)
            exchange.start_corners(-1, (False,))


def pass_on(place, exchanges):
    slim, wide = exchanges
    for side in range(2):
        slim.by_copy(side).wait_recv()

    slim.spread_by()

    @pl.when(place.edge & place.early & jnp.logical_not(place.upper))
    def _():
        for exchange in exchanges:
            exchange.start_by(True)

    @pl.when(place.low & place.early)
    def _():
        slim.wait_wrap(1)
        for exchange in exchanges:
            exchange.start_wrap(-1)
        slim.wait_corners(-1)
        for exchange in exchanges:
            exchange.start_corners(-1)
        slim.take_corners(-1)

    @pl.when(place.low & place.late)
    def _():
        slim.wait_corners(-1)
        slim.take_corners(-1)

    @pl.when(place.high)
    def _():
        slim.wait_corners(1)
        slim.take_corners(1)

    for side in range(2):
        wide.by_copy(side).wait_recv()
    wide.spread_by()
    for wraps, dz in ((place.low, -1), (place.high, 1)):

        @pl.when(wraps)
        def _():
            wide.wait_corners(dz)
            wide.take_corners(dz)


def dot_nn(left, right):
    return lax.dot_general(left, right, (((1,), (0,)), ((), ())), preferred_element_type=F32)


def dot_nt(left, right):
    return lax.dot_general(left, right, (((1,), (1,)), ((), ())), preferred_element_type=F32)


def split(value):
    high = value.astype(BF16)
    return high, (value - high.astype(F32)).astype(BF16)


def cell_digits(row):
    return row >> 7, (row >> 5) & 3, (row >> 3) & 3, row & 7


def coordinates(row):
    ci, cj, ck, w = cell_digits(row)
    return (
        2 * (ci - 1) + (w >> 2),
        2 * (cj - 1) + ((w >> 1) & 1),
        2 * (ck - 1) + (w & 1),
    )


def table_row(row):
    ci, cj, ck, w = cell_digits(row)
    ox, oz = ci - 1, ck - 1
    inner_x = (ci == 1) | (ci == 2)
    inner_y = (cj == 1) | (cj == 2)
    inner_z = (ck == 1) | (ck == 2)
    x_side, z_side = ci >> 1, ck >> 1
    base = jnp.where(
        inner_x,
        jnp.where(inner_z, 32 * oz + 16 * ox, 64 + 32 * z_side + 16 * ox),
        jnp.where(inner_z, 128 + 32 * x_side + 16 * oz, 192 + 32 * x_side + 16 * z_side),
    )
    y_part = jnp.where(inner_y, 8 * (cj - 1), HALF + 8 * (cj >> 1))
    return base + y_part + w


def inner_atom(row):
    ci, cj, ck, w = cell_digits(row)
    inside = (ci == 1) | (ci == 2)
    inside = inside & ((cj == 1) | (cj == 2)) & ((ck == 1) | (ck == 2))
    return jnp.where(inside, 8 * (4 * (ci - 1) + 2 * (cj - 1) + ck - 1) + w, -1)


def lane_slot(shape):
    return lax.broadcasted_iota(jnp.int32, shape, 1) >> 5


def over_edges(columns, slots):
    spread = [jnp.broadcast_to(column, slots.shape) for column in columns]
    low = jnp.where(slots == 0, spread[0], spread[1])
    high = jnp.where(slots == 2, spread[2], spread[3])
    return jnp.where(slots < 2, low, high)


def turned_rows(value):
    rows, columns = value.shape
    value = jnp.concatenate([value, jnp.zeros((8 - rows, columns), F32)], axis=0)
    return jnp.concatenate([value, jnp.zeros((8, 128 - columns), F32)], axis=1).T


def slot_mask():
    slots = lane_slot((8, LANES))
    return jnp.where(slots == lax.broadcasted_iota(jnp.int32, (8, LANES), 0), 1.0, 0.0).astype(F32)


def edge_work(
    stop,
    begin,
    slim_ready,
    wide_ready,
    slim,
    wide,
    count_ref,
    centres_ref,
    neighbours_ref,
    w_pair_ref,
    w_radial_ref,
    w_mix_ref,
    w_self_ref,
    w_tensor_ref,
    w_out_ref,
    energies_ref,
    forces_ref,
    turned,
    spots,
    scalars,
    shift_rows,
    centre_slim,
    centre_wide,
    basis_rows,
    sphere_rows,
    back_rows,
    pulled,
    far_spots,
    latent_rows,
    slope_rows,
    mixing_rows,
):
    begin()

    neighbours = neighbours_ref[...]
    centres = turned_rows(centres_ref[...].astype(F32))[0:BLOCKS].astype(jnp.int32)
    spots[...] = table_row(neighbours)
    centre_spots = table_row(centres)
    slots = lane_slot((BLOCKS, EDGES))
    centre_rows = over_edges([centres[:, j : j + 1] for j in range(4)], slots)
    steps = [
        (one - other).astype(F32) * site_spacing
        for one, other in zip(coordinates(neighbours), coordinates(centre_rows))
    ]
    mask = slot_mask()
    w_pair = w_pair_ref[...]
    radial = w_radial_ref[...]
    radial_high, radial_low = split(radial)
    radial_rows = jnp.concatenate([radial_high.astype(F32), radial_low.astype(F32)], axis=0).astype(BF16)
    mix_turned = w_mix_ref[...].astype(F32)
    mix_turned = jnp.concatenate(
        [mix_turned[128:192], mix_turned[64:128], mix_turned[0:64]], axis=0
    )
    mix_back = mix_turned.T.astype(BF16)
    mix_turned = mix_turned.astype(BF16)
    update = jnp.concatenate([w_self_ref[...], w_tensor_ref[...]], axis=0)
    update_turned = update.astype(F32).T.astype(BF16)
    w_out = jnp.broadcast_to(w_out_ref[...].astype(F32), (128, 128)).T
    w_out = jnp.concatenate([w_out, w_out], axis=1)
    low_half = lax.broadcasted_iota(jnp.int32, (8, 128), 1) < 64
    nothing = jnp.zeros((8, 128), F32)

    slim_ready()
    if stop == 0:
        return

    turned[...] = slim[...].astype(F32).T[0:80].astype(BF16)

    centre_shift = []
    lanes_of_rows = lax.broadcasted_iota(jnp.int32, (BLOCKS, ROWS), 1)
    for place in range(4):
        hits = jnp.where(centre_spots[:, place : place + 1] == lanes_of_rows, 1.0, 0.0).astype(BF16)
        got = dot_nn(hits, slim[...])
        centre_slim[pl.ds(place, BLOCKS, stride=4), :] = got
        centre_shift.append([got[:, 64 + axis : 65 + axis] for axis in range(3)])

    def gather(turn, _):
        rows = lax.broadcasted_iota(jnp.int32, (ROWS, EDGES), 0).astype(jnp.int16)
        one, none = jnp.ones((), BF16), jnp.zeros((), BF16)
        for pair in [turn * GATHER + at for at in range(GATHER)]:
            hits = []
            for block in range(2):
                spot = spots[pl.ds(2 * pair + block, 1), :].astype(jnp.int16)
                hits.append(jnp.where(rows == spot, one, none))
            got = dot_nn(turned[...], jnp.concatenate(hits, axis=1))
            scalars[pair] = got[0:64].astype(BF16)
            for block in range(2):
                shift_rows[pl.ds(pl.multiple_of((2 * pair + block) * 8, 8), 8), :] = got[
                    64:72, EDGES * block : EDGES * block + EDGES
                ]
        return 0

    lax.fori_loop(0, PAIRS // GATHER, gather, 0)
    if stop == 1:
        return

    vector = []
    for axis in range(3):
        near = shift_rows[pl.ds(axis, BLOCKS, stride=8), :]
        far = over_edges([centre_shift[j][axis] for j in range(4)], slots)
        vector.append(steps[axis] + (near - far))
    distance = jnp.sqrt(vector[0] * vector[0] + vector[1] * vector[1] + vector[2] * vector[2])
    inverse = 1.0 / distance
    ux, uy, uz = [part * inverse for part in vector]
    inside = distance < cutoff_radius
    scaled = jnp.minimum(distance * (1.0 / cutoff_radius), 1.0)
    fifth = (scaled * scaled) * (scaled * scaled) * scaled
    envelope = 1.0 - fifth * scaled * (28.0 - scaled * (48.0 - 21.0 * scaled))
    envelope_slope = jnp.where(
        inside, fifth * (-168.0 + scaled * (336.0 - 168.0 * scaled)) * (1.0 / cutoff_radius), 0.0
    )
    sine, cosine = jnp.sin(math.pi * scaled), jnp.cos(math.pi * scaled)
    norm = math.sqrt(2.0 / cutoff_radius) * inverse
    cut_norm = norm * envelope
    slope_sine = norm * (envelope_slope - envelope * inverse)
    slope_cosine = jnp.where(inside, cut_norm * (math.pi / cutoff_radius), 0.0)
    sines, cosines = [sine], [cosine]
    for _ in range(7):
        s, c = sines[-1], cosines[-1]
        sines.append(s * cosine + c * sine)
        cosines.append(c * cosine - s * sine)
    for k in range(8):
        basis_rows[pl.ds(k, BLOCKS, stride=8), :] = sines[k] * cut_norm
    sphere = (
        root_three * ux,
        root_three * uy,
        root_three * uz,
        root_fifteen * ux * uy,
        root_fifteen * uy * uz,
        0.5 * root_five * (3.0 * uz * uz - 1.0),
        root_fifteen * ux * uz,
        0.5 * root_fifteen * (ux * ux - uy * uy),
    )
    for m in range(8):
        sphere_rows[pl.ds(m, BLOCKS, stride=8), :] = sphere[m]

    centre_slim[...] = dot_nn(centre_slim[:, 0:64].astype(BF16), w_pair[0:64])

    if stop == 2:
        return

    def latents(pair):
        at = pl.multiple_of(8 * pair, 8)
        high, low = split(centre_slim[pl.ds(at, 8), :])
        left = jnp.concatenate(
            [
                w_pair[64:128].astype(F32),
                high.astype(F32),
                low.astype(F32),
                radial_high.astype(F32),
                radial_high.astype(F32),
                radial_low.astype(F32),
                jnp.zeros((24, 128), F32),
            ],
            axis=0,
        ).T.astype(BF16)
        at = pl.multiple_of(16 * pair, 16)
        basis = jnp.concatenate(
            [basis_rows[pl.ds(at, 8), :], basis_rows[pl.ds(at + 8, 8), :]], axis=1
        )
        high, low = split(basis)
        right = jnp.concatenate(
            [mask, mask, high.astype(F32), low.astype(F32), high.astype(F32), jnp.zeros((24, LANES), F32)],
            axis=0,
        ).astype(BF16)
        return dot_nn(left, jnp.concatenate([scalars[pair], right], axis=0))

    def tensors(pair):
        at = pl.multiple_of(8 * pair, 8)
        parts = [centre_wide[g, pl.ds(at, 8), :] for g in range(5)]
        turns = [pltpu.roll(part, 64, 1) for part in parts]
        order_one = [turns[1], parts[1], turns[2]]
        order_two = [turns[2], parts[3], turns[3], parts[4], turns[4]]
        rows = [jnp.where(low_half, 0.0, part) for part in order_one]
        rows += [jnp.where(low_half, part, 0.0) for part in order_two]
        back = jnp.concatenate(rows, axis=0)
        zero = jnp.where(low_half, turns[0], 0.0)
        first = jnp.concatenate([back, nothing, nothing], axis=0).T
        second = jnp.concatenate([nothing] * 8 + [zero, nothing], axis=0).T[0:64]
        front = jnp.concatenate([first, second], axis=0)
        return front.astype(BF16), back.astype(BF16)

    def spheres(pair):
        at = pl.multiple_of(16 * pair, 16)
        sphere = jnp.concatenate(
            [sphere_rows[pl.ds(at, 8), :], sphere_rows[pl.ds(at + 8, 8), :]], axis=1
        )
        rows = [jnp.broadcast_to(sphere[m : m + 1], (8, LANES)) * mask for m in range(8)]
        return jnp.concatenate(rows + [mask, jnp.zeros((8, LANES), F32)], axis=0).astype(BF16)

    def silu_parts(x):
        gate = 0.5 * jnp.tanh(0.5 * x) + 0.5
        value = x * gate
        return value, gate + value * (1.0 - gate)

    each = range(FIRST)

    def first_group(turn, _):
        pairs = [turn * FIRST + g for g in each]
        first = [silu_parts(latents(p)) for p in pairs]
        for g in each:
            latent = first[g][0].astype(BF16)
            latent_rows[pairs[g]] = latent
            slope_rows[pairs[g]] = first[g][1]
            mixing_rows[pairs[g]] = dot_nn(mix_turned, latent)
        return 0

    lax.fori_loop(0, PAIRS // FIRST, first_group, 0)
    if stop == 3:
        return

    wide_ready()
    for place in range(4):
        hits = jnp.where(centre_spots[:, place : place + 1] == lanes_of_rows, 1.0, 0.0).astype(BF16)
        got = dot_nn(hits, wide[...])
        for at in range(WIDE // 128):
            centre_wide[at, pl.ds(place, BLOCKS, stride=4), :] = got[:, 128 * at : 128 * at + 128]

    if stop == 4:
        return

    def second_group(turn, _):
        each = range(SECOND)
        pairs = [turn * SECOND + g for g in each]
        sides = [tensors(p) for p in pairs]
        contracted = [dot_nn(sides[g][0], spheres(pairs[g])) for g in each]
        mixing = [mixing_rows[p] for p in pairs]
        coupled = []
        for g in each:
            product = mixing[g] * contracted[g]
            coupled.append((product[0:64] + product[64:128] + product[128:192]).astype(BF16))
        hidden_in = [
            dot_nn(update_turned, jnp.concatenate([latent_rows[pairs[g]], coupled[g]], axis=0))
            for g in each
        ]
        second = [silu_parts(x) for x in hidden_in]
        readout = [jnp.sum(value * w_out, axis=0, keepdims=True) for value, _ in second]
        back = [dot_nn(update, (slope * w_out).astype(BF16)) for _, slope in second]
        for g in each:
            cotangent = back[g][128:192].astype(BF16).astype(F32)
            cotangents = jnp.concatenate([cotangent, cotangent, cotangent], axis=0)
            to_mixing = (cotangents * contracted[g]).astype(BF16)
            to_contracted = (cotangents[0:128] * mixing[g][0:128]).astype(BF16)
            to_latent = back[g][0:128] + dot_nn(mix_back, to_mixing)
            to_sphere = dot_nn(sides[g][1], to_contracted)
            to_sphere = jnp.sum(to_sphere.reshape(8, 8, LANES) * mask[None], axis=1)
            to_input = (to_latent * slope_rows[pairs[g]]).astype(BF16)
            to_basis = dot_nn(radial_rows, to_input)
            to_basis = to_basis[0:8] + to_basis[8:16]
            for block in range(2):
                at = (2 * pairs[g] + block) * 24
                lanes = slice(EDGES * block, EDGES * block + EDGES)
                back_rows[pl.ds(pl.multiple_of(at, 8), 8), :] = to_sphere[:, lanes]
                back_rows[pl.ds(pl.multiple_of(at + 8, 8), 8), :] = to_basis[:, lanes]
                back_rows[pl.ds(pl.multiple_of(at + 16, 8), 8), :] = jnp.broadcast_to(
                    readout[g][:, lanes], (8, EDGES)
                )
        return 0

    lax.fori_loop(0, PAIRS // SECOND, second_group, 0)
    if stop == 5:
        return

    def backs(row):
        return back_rows[pl.ds(row, BLOCKS, stride=24), :]

    count = count_ref[...]
    active = lax.broadcasted_iota(jnp.int32, (BLOCKS, EDGES), 0) < count
    readout = backs(16)
    energy = jnp.where(active, envelope * readout, 0.0)
    radial_pull = envelope_slope * readout
    along_sine, along_cosine = 0.0, 0.0
    for k in range(8):
        to_basis = backs(8 + k)
        along_sine = along_sine + to_basis * sines[k]
        along_cosine = along_cosine + to_basis * (cosines[k] * (k + 1.0))
    radial_pull = radial_pull + envelope * (along_sine * slope_sine + along_cosine * slope_cosine)
    y1, y2, y3, y4, y5, y6, y7, y8 = [backs(m) for m in range(8)]
    gx = root_three * y1 + root_fifteen * (uy * y4 + uz * y7 + ux * y8)
    gy = root_three * y2 + root_fifteen * (ux * y4 + uz * y5 - uy * y8)
    gz = root_three * y3 + root_fifteen * (uy * y5 + ux * y7) + (3.0 * root_five) * uz * y6
    turn_norm = envelope * inverse
    radial_pull = radial_pull - turn_norm * (gx * ux + gy * uy + gz * uz)
    pulls = [
        jnp.where(active, radial_pull * u + turn_norm * g, 0.0)
        for u, g in ((ux, gx), (uy, gy), (uz, gz))
    ]
    for at, value in enumerate(pulls + [energy]):
        high, low = split(value)
        pulled[pl.ds(at, BLOCKS, stride=8), :] = high.astype(F32)
        pulled[pl.ds(4 + at, BLOCKS, stride=8), :] = low.astype(F32)
    spots[...] = inner_atom(neighbours)
    far_spots[...] = inner_atom(centre_rows)
    if stop == 6:
        return

    def scatter(turn, total):
        near, far, values = [], [], []
        atoms = lax.broadcasted_iota(jnp.int32, (64, EDGES), 0).astype(jnp.int16)
        one, none = jnp.ones((), BF16), jnp.zeros((), BF16)
        for at in range(SCATTER):
            block = turn * SCATTER + at
            spot = spots[pl.ds(block, 1), :].astype(jnp.int16)
            near.append(jnp.where(atoms == spot, one, none))
            spot = far_spots[pl.ds(block, 1), :].astype(jnp.int16)
            far.append(jnp.where(atoms == spot, one, none))
            values.append(pulled[pl.ds(pl.multiple_of(8 * block, 8), 8), :])
        near = jnp.concatenate(near, axis=1)
        far = jnp.concatenate(far, axis=1)
        values = jnp.concatenate(values, axis=1).astype(BF16)
        return total + dot_nt(jnp.concatenate([far - near, far], axis=0), values)

    total = lax.fori_loop(0, BLOCKS // SCATTER, scatter, jnp.zeros((128, 8), F32))
    total = jnp.concatenate([total, jnp.zeros((128, 120), F32)], axis=1).T
    for axis in range(3):
        forces_ref[axis] = total[axis : axis + 1, 0:64] + total[4 + axis : 5 + axis, 0:64]
    energies_ref[...] = total[3:4, 64:128] + total[7:8, 64:128]


def edge_scratch():
    return [
        pltpu.VMEM((80, ROWS), BF16),
        pltpu.VMEM((BLOCKS, EDGES), jnp.int32),
        pltpu.VMEM((PAIRS, 64, LANES), BF16),
        pltpu.VMEM((8 * BLOCKS, EDGES), F32),
        pltpu.VMEM((4 * BLOCKS, SLIM), F32),
        pltpu.VMEM((WIDE // 128, 4 * BLOCKS, 128), F32),
        pltpu.VMEM((8 * BLOCKS, EDGES), F32),
        pltpu.VMEM((8 * BLOCKS, EDGES), F32),
        pltpu.VMEM((24 * BLOCKS, EDGES), F32),
        pltpu.VMEM((8 * BLOCKS, EDGES), F32),
        pltpu.VMEM((BLOCKS, EDGES), jnp.int32),
        pltpu.VMEM((PAIRS, 128, LANES), BF16),
        pltpu.VMEM((PAIRS, 128, LANES), F32),
        pltpu.VMEM((PAIRS, 192, LANES), F32),
    ]


HALO_SCRATCH = 14


def whole_kernel(features_ref, shifts_ref, *refs):
    operands, refs = refs[:11], refs[11:]
    slim, wide, by_slim_out, by_wide_out, by_slim_in, by_wide_in = refs[:6]
    corner_slim, corner_wide, packed = refs[6:9]
    by_send, by_recv, send_sem, recv_sem, go = refs[9:HALO_SCRATCH]
    place = Place()
    greet(place)
    place_own(features_ref, shifts_ref, slim, wide, by_slim_out, by_wide_out, packed)
    exchanges = [
        kind(
            place,
            table,
            out,
            landed,
            corner,
            by_send.at[t],
            by_recv.at[t],
            send_sem.at[t],
            recv_sem.at[t],
        )
        for t, (kind, table, out, landed, corner) in enumerate(
            (
                (SlimExchange, slim, by_slim_out, by_slim_in, corner_slim),
                (Exchange, wide, by_wide_out, by_wide_in, corner_wide),
            )
        )
    ]

    def begin():
        meet(place)
        help_others(place, go)
        start_first(place, exchanges)

    def slim_ready():
        start_second(place, exchanges, go)
        pass_on(place, exchanges)
        exchanges[0].arrive()

    def wide_ready():
        exchanges[1].arrive()

    edge_work(None, begin, slim_ready, wide_ready, slim, wide, *operands, *refs[HALO_SCRATCH:])
    for exchange in exchanges:
        exchange.close()


VMEM = pl.BlockSpec(memory_space=pltpu.VMEM)


def whole(*operands):
    return pl.pallas_call(
        whole_kernel,
        out_shape=(
            jax.ShapeDtypeStruct((1, 64), F32),
            jax.ShapeDtypeStruct((3, 1, 64), F32),
        ),
        in_specs=[VMEM] * 11,
        out_specs=(VMEM, VMEM),
        scratch_shapes=[
            pltpu.VMEM((ROWS, SLIM), BF16),
            pltpu.VMEM((ROWS, WIDE), BF16),
            pltpu.VMEM((2, 32, SLIM), BF16),
            pltpu.VMEM((2, 32, WIDE), BF16),
            pltpu.VMEM((2, 32, SLIM), BF16),
            pltpu.VMEM((2, 32, WIDE), BF16),
            pltpu.VMEM((2, 16, SLIM), BF16),
            pltpu.VMEM((2, 16, WIDE), BF16),
            pltpu.VMEM((64, SLIM), F32),
            pltpu.SemaphoreType.DMA((2, 4)),
            pltpu.SemaphoreType.DMA((2, 4)),
            pltpu.SemaphoreType.DMA((2, 3, SENDS)),
            pltpu.SemaphoreType.DMA((2, 3, SENDS)),
            pltpu.SemaphoreType.REGULAR((2,)),
        ]
        + edge_scratch(),
        compiler_params=pltpu.CompilerParams(
            collective_id=0, has_side_effects=True, vmem_limit_bytes=56 * 2**20
        ),
        name="boxes",
    )(*operands)


def per_device(
    features,
    shifts,
    block_counts,
    block_centres,
    block_neighbours,
    w_pair,
    w_radial,
    w_mix,
    w_self,
    w_tensor,
    w_out,
):
    energies, forces = whole(
        features.reshape(64, WIDE),
        shifts.reshape(64, 3).T,
        block_counts.reshape(1, 1),
        block_centres.reshape(BLOCKS, 4).T,
        block_neighbours.reshape(BLOCKS, EDGES),
        w_pair,
        w_radial,
        w_mix.T,
        w_self,
        w_tensor,
        w_out.reshape(1, 128),
    )
    return energies.reshape(1, 1, 1, 64), forces.reshape(1, 1, 1, 3, 64)


def solution(mesh):
    in_specs = (
        P("bx", "by", "bz", None, None),
        P("bx", "by", "bz", None, None),
        P("bx", "by", "bz"),
        P("bx", "by", "bz", None, None),
        P("bx", "by", "bz", None, None),
        P(),
        P(),
        P(),
        P(),
        P(),
        P(),
    )
    out_specs = (P("bx", "by", "bz", None), P("bx", "by", "bz", None, None))
    return jax.shard_map(
        per_device, mesh=mesh, in_specs=in_specs, out_specs=out_specs, check_vma=False
    )
```

```python
import functools
import math

import jax
import jax.numpy as jnp
from jax import lax
from jax.experimental import pallas as pl
from jax.experimental.pallas import tpu as pltpu
from jax.sharding import PartitionSpec as P

MESH = pl.DeviceIdType.MESH
F32 = jnp.float32
BF16 = jnp.bfloat16

cutoff_radius = 6.0
site_spacing = 1.7
root_three = math.sqrt(3.0)
root_five = math.sqrt(5.0)
root_fifteen = math.sqrt(15.0)

ROWS = 512
HALF = 256
WIDE = 640
SLIM = 128
BLOCKS = 48
EDGES = 128
PAIRS = BLOCKS // 2
SCATTER = 24
GATHER = 12
FIRST = 12
SECOND = 12
LANES = 2 * EDGES


def phase_two_sends():
    return (
        (0, 1, 32, 64, 32),
        (0, -1, 0, 96, 32),
        (1, 0, 16, 128, 16),
        (1, 0, 48, 144, 16),
        (-1, 0, 0, 160, 16),
        (-1, 0, 32, 176, 16),
        (1, 1, 48, 192, 16),
        (1, -1, 16, 208, 16),
        (-1, 1, 32, 224, 16),
        (-1, -1, 0, 240, 16),
    )


SENDS = len(phase_two_sends())


def wrapped(axis, step):
    size = lax.axis_size(axis)
    return lax.rem(lax.axis_index(axis) + size + step, size)


def at_device(dx, dy, dz):
    return (wrapped("bx", dx), wrapped("by", dy), wrapped("bz", dz))


def octants(rows, order):
    return jnp.concatenate([rows[8 * o : 8 * o + 8] for o in order], axis=0)


def place_own(features_ref, shifts_ref, slim, wide, by_slim_out, by_wide_out, packed):
    packed[...] = jnp.zeros_like(packed)
    packed[:, 0:64] = features_ref[:, 0:64].astype(F32)
    packed[:, 64:72] = turned_rows(shifts_ref[...].astype(F32))[0:64]
    own = [4 * ox + 2 * oy + oz for oz in range(2) for ox in range(2) for oy in range(2)]
    for source, table, out in (
        (packed[...], slim, by_slim_out),
        (features_ref[...].astype(F32), wide, by_wide_out),
    ):
        table[0:64, :] = octants(source, own).astype(BF16)
        for oy in range(2):
            face = [4 * ox + 2 * oy + oz for oz in range(2) for ox in range(2)]
            out[oy] = octants(source, face).astype(BF16)


def place_octants(table, first, landed, count):
    pieces = []
    below, above = landed[0].astype(F32), landed[1].astype(F32)
    for q in range(count):
        pieces += [below[8 * q : 8 * q + 8], above[8 * q : 8 * q + 8]]
    table[first : first + 16 * count, :] = jnp.concatenate(pieces, axis=0).astype(BF16)


class Place:
    def __init__(self):
        self.bx, self.by, self.bz = (lax.axis_index(axis) for axis in ("bx", "by", "bz"))
        self.ends = lax.axis_size("bz") - 1
        self.x, self.z_hi = lax.rem(self.by, 4), lax.div(self.by, 4)
        self.first_x, self.last_x = self.x == 0, self.x == 3
        self.edge = self.first_x | self.last_x
        self.early = self.z_hi == 0
        self.late = self.z_hi == 1
        self.low = self.bz == 0
        self.high = self.bz == self.ends
        self.middle = lax.div(lax.axis_size("bz"), 2)
        self.upper = self.bz >= self.middle
        self.by_helper = jnp.logical_not(self.edge) & self.late & (self.bz < self.middle)
        self.wrap_helper = self.late & (self.bz == self.middle)


def flips(place, side):
    return place.last_x if side == 0 else place.first_x


def signal(semaphore, device):
    pl.semaphore_signal(semaphore, inc=1, device_id=device, device_id_type=MESH)


def as_count(condition, amount):
    return jnp.where(condition, amount, 0)


def greet(place):
    barrier = pltpu.get_barrier_semaphore()
    for dx in (-1, 1):
        signal(barrier, at_device(dx, 0, 0))
    for side, dy in ((0, 1), (1, -1)):

        @pl.when(jnp.logical_not(flips(place, side)) | place.early)
        def _():
            signal(barrier, at_device(0, dy, 0))

    for dx in (-1, 0, 1):
        signal(barrier, at_device(dx, 0, -1))

        @pl.when(jnp.logical_not(place.high))
        def _():
            signal(barrier, at_device(dx, 0, 1))

    for side, dy in ((0, 1), (1, -1)):

        @pl.when(place.low)
        def _():
            signal(barrier, at_device(0, dy, -1))

        @pl.when(place.high & place.early & flips(place, side))
        def _():
            signal(barrier, at_device(0, dy, 1))

    @pl.when(place.edge & place.upper)
    def _():
        near_first = place.first_x == place.early
        signal(barrier, (place.bx, jnp.where(near_first, 5, 6), place.bz - place.middle))

    @pl.when(place.late & place.low)
    def _():
        signal(barrier, (place.bx, place.by, place.middle))

    @pl.when(place.late & place.high)
    def _():
        for dx in (-1, 0, 1):
            signal(barrier, (wrapped("bx", dx), place.by, place.middle))

        for side, dy in ((0, 1), (1, -1)):

            @pl.when(jnp.logical_not(flips(place, side)))
            def _():
                signal(barrier, (place.bx, place.by + dy, place.middle))


def meet(place):
    count = 2 + as_count(jnp.logical_not(place.edge), 1) + 1
    count = count + as_count(place.edge & place.late, 1)
    count = count + as_count(jnp.logical_not(place.low), 3) + 3
    count = count + as_count(place.high, 2)
    count = count + as_count(place.low & place.late & place.edge, 1)
    count = count + as_count(place.by_helper, 2)
    count = count + as_count(place.wrap_helper, 5 + as_count(jnp.logical_not(place.edge), 1))
    pl.semaphore_wait(pltpu.get_barrier_semaphore(), count)


def help_others(place, go):
    @pl.when(place.by_helper)
    def _():
        signal(go.at[0], (place.bx, jnp.where(place.x == 1, 0, 3), place.bz + place.middle))

    @pl.when(place.wrap_helper)
    def _():
        signal(go.at[1], (place.bx, place.by, 0))


class Exchange:
    def __init__(self, place, table, out, landed, corner, by_send, by_recv, send, recv):
        self.place = place
        self.table, self.out, self.landed, self.corner = table, out, landed, corner
        self.by_send, self.by_recv, self.send, self.recv = by_send, by_recv, send, recv

    def copy(self, source, target, send, recv, dx, dy, dz):
        return pltpu.make_async_remote_copy(
            src_ref=source,
            dst_ref=target,
            send_sem=send,
            recv_sem=recv,
            device_id=at_device(dx, dy, dz),
            device_id_type=MESH,
        )

    def by_copy(self, side):
        return self.copy(
            self.out.at[1 - side],
            self.landed.at[side],
            self.by_send.at[side],
            self.by_recv.at[side],
            0,
            1 - 2 * side,
            0,
        )

    def corner_copy(self, dz, side):
        return self.copy(
            self.out.at[1 - side, pl.ds(16 if dz > 0 else 0, 16)],
            self.corner.at[side],
            self.by_send.at[2 + side],
            self.by_recv.at[2 + side],
            0,
            1 - 2 * side,
            dz,
        )

    def half_copies(self, half):
        return [
            (
                functools.partial(
                    self.copy,
                    self.table.at[pl.ds(HALF * half + source, rows)],
                    self.table.at[pl.ds(HALF * half + target, rows)],
                    self.send.at[half, at],
                    self.recv.at[half, at],
                    dx,
                    0,
                    dz,
                ),
                dz,
            )
            for at, (dx, dz, source, target, rows) in enumerate(phase_two_sends())
        ]

    def late_copies(self, high):
        piece = HALF + (96 if high else 64)
        return [
            self.copy(
                self.table.at[pl.ds(piece + 16, 16)],
                self.table.at[pl.ds(HALF + 192 + 16 * high, 16)],
                self.send.at[2, 0],
                self.recv.at[2, 0],
                1,
                0,
                0,
            ),
            self.copy(
                self.table.at[pl.ds(piece, 16)],
                self.table.at[pl.ds(HALF + 224 + 16 * high, 16)],
                self.send.at[2, 1],
                self.recv.at[2, 1],
                -1,
                0,
                0,
            ),
        ]

    def start_by(self, far):
        for side in range(2):

            @pl.when(flips(self.place, side) if far else jnp.logical_not(flips(self.place, side)))
            def _():
                self.by_copy(side).start()

    def start_wrap(self, dz):
        for copy, along in self.half_copies(0):
            if along == dz:
                copy().start()

    def start_corners(self, dz, flipped=(True, False)):
        for side in range(2):
            if len(flipped) == 2:
                self.corner_copy(dz, side).start()
            else:

                @pl.when(flips(self.place, side) == flipped[0])
                def _():
                    self.corner_copy(dz, side).start()

    def start_own(self):
        for copy, dz in self.half_copies(0):
            if dz == 0:
                copy().start()
            else:

                @pl.when(jnp.logical_not(self.place.high if dz > 0 else self.place.low))
                def _():
                    copy().start()

    def spread_by(self):
        place_octants(self.table, HALF, self.landed, 4)
        for copy, dz in self.half_copies(1):
            if dz == 0:
                copy().start()
            else:

                @pl.when(jnp.logical_not(self.place.high if dz > 0 else self.place.low))
                def _():
                    copy().start()

    def wait_corners(self, dz):
        for side in range(2):
            self.corner_copy(dz, side).wait_recv()

    def take_corners(self, dz):
        place_octants(self.table, HALF + (64 if dz < 0 else 96), self.corner, 2)
        for copy in self.late_copies(int(dz > 0)):
            copy.start()

    def wait_wrap(self, dz):
        for copy, along in self.half_copies(0):
            if along == dz:
                copy().wait_recv()

    def arrive(self):
        for copy, dz in self.half_copies(0):
            if self.wraps_waited(dz):

                @pl.when(jnp.logical_not(self.place.low & self.place.early))
                def _():
                    copy().wait_recv()
            else:
                copy().wait_recv()
        for copy, dz in self.half_copies(1):
            if dz == 0:
                copy().wait_recv()
            else:

                @pl.when(jnp.logical_not(self.place.low if dz > 0 else self.place.high))
                def _():
                    copy().wait_recv()

        for wraps, high in ((self.place.low, 0), (self.place.high, 1)):

            @pl.when(wraps)
            def _():
                for copy in self.late_copies(high):
                    copy.wait_recv()

    def wraps_waited(self, dz):
        return False

    def close(self):
        for side in range(2):
            self.by_copy(side).wait_send()
        for copy, _ in self.half_copies(0):
            copy().wait_send()
        for copy, dz in self.half_copies(1):
            if dz == 0:
                copy().wait_send()
            else:

                @pl.when(jnp.logical_not(self.place.high if dz > 0 else self.place.low))
                def _():
                    copy().wait_send()

        for wraps, high in ((self.place.low, 0), (self.place.high, 1)):

            @pl.when(wraps)
            def _():
                for side in range(2):
                    self.corner_copy(2 * high - 1, side).wait_send()
                for copy in self.late_copies(high):
                    copy.wait_send()


class SlimExchange(Exchange):
    def wraps_waited(self, dz):
        return dz > 0


def start_first(place, exchanges):
    slim, wide = exchanges

    @pl.when(place.edge & place.late)
    def _():
        for exchange in exchanges:
            exchange.start_by(True)

    @pl.when(place.high)
    def _():
        slim.start_corners(1)
        slim.start_wrap(1)
        wide.start_corners(1)

    @pl.when(place.low & place.late)
    def _():
        for exchange in exchanges:
            exchange.start_corners(-1, (True,))

    for exchange in exchanges:
        exchange.start_by(False)
    slim.start_own()


def start_second(place, exchanges, go):
    wide = exchanges[1]
    wide.start_own()

    @pl.when(place.high)
    def _():
        wide.start_wrap(1)

    @pl.when(place.edge & place.early & place.upper)
    def _():
        pl.semaphore_wait(go.at[0], 1)
        for exchange in exchanges:
            exchange.start_by(True)

    @pl.when(place.low & place.late)
    def _():
        pl.semaphore_wait(go.at[1], 1)
        for exchange in exchanges:
            exchange.start_wrap(-1)
            exchange.start_corners(-1, (False,))


def pass_on(place, exchanges):
    slim, wide = exchanges
    for side in range(2):
        slim.by_copy(side).wait_recv()

    slim.spread_by()

    @pl.when(place.low & place.early)
    def _():
        slim.wait_wrap(1)
        slim.wait_corners(-1)
        slim.take_corners(-1)

    @pl.when(place.low & place.late)
    def _():
        slim.wait_corners(-1)
        slim.take_corners(-1)

    @pl.when(place.high)
    def _():
        slim.wait_corners(1)
        slim.take_corners(1)

    for side in range(2):
        wide.by_copy(side).wait_recv()
    wide.spread_by()
    for wraps, dz in ((place.low, -1), (place.high, 1)):

        @pl.when(wraps)
        def _():
            wide.wait_corners(dz)
            wide.take_corners(dz)

    @pl.when(place.edge & place.early & jnp.logical_not(place.upper))
    def _():
        for exchange in exchanges:
            exchange.start_by(True)

    @pl.when(place.low & place.early)
    def _():
        for exchange in exchanges:
            exchange.start_wrap(-1)
            exchange.start_corners(-1)


def dot_nn(left, right):
    return lax.dot_general(left, right, (((1,), (0,)), ((), ())), preferred_element_type=F32)


def dot_nt(left, right):
    return lax.dot_general(left, right, (((1,), (1,)), ((), ())), preferred_element_type=F32)


def split(value):
    high = value.astype(BF16)
    return high, (value - high.astype(F32)).astype(BF16)


def cell_digits(row):
    return row >> 7, (row >> 5) & 3, (row >> 3) & 3, row & 7


def coordinates(row):
    ci, cj, ck, w = cell_digits(row)
    return (
        2 * (ci - 1) + (w >> 2),
        2 * (cj - 1) + ((w >> 1) & 1),
        2 * (ck - 1) + (w & 1),
    )


def table_row(row):
    ci, cj, ck, w = cell_digits(row)
    ox, oz = ci - 1, ck - 1
    inner_x = (ci == 1) | (ci == 2)
    inner_y = (cj == 1) | (cj == 2)
    inner_z = (ck == 1) | (ck == 2)
    x_side, z_side = ci >> 1, ck >> 1
    base = jnp.where(
        inner_x,
        jnp.where(inner_z, 32 * oz + 16 * ox, 64 + 32 * z_side + 16 * ox),
        jnp.where(inner_z, 128 + 32 * x_side + 16 * oz, 192 + 32 * x_side + 16 * z_side),
    )
    y_part = jnp.where(inner_y, 8 * (cj - 1), HALF + 8 * (cj >> 1))
    return base + y_part + w


def inner_atom(row):
    ci, cj, ck, w = cell_digits(row)
    inside = (ci == 1) | (ci == 2)
    inside = inside & ((cj == 1) | (cj == 2)) & ((ck == 1) | (ck == 2))
    return jnp.where(inside, 8 * (4 * (ci - 1) + 2 * (cj - 1) + ck - 1) + w, -1)


def lane_slot(shape):
    return lax.broadcasted_iota(jnp.int32, shape, 1) >> 5


def over_edges(columns, slots):
    spread = [jnp.broadcast_to(column, slots.shape) for column in columns]
    low = jnp.where(slots == 0, spread[0], spread[1])
    high = jnp.where(slots == 2, spread[2], spread[3])
    return jnp.where(slots < 2, low, high)


def turned_rows(value):
    rows, columns = value.shape
    value = jnp.concatenate([value, jnp.zeros((8 - rows, columns), F32)], axis=0)
    return jnp.concatenate([value, jnp.zeros((8, 128 - columns), F32)], axis=1).T


def slot_mask():
    slots = lane_slot((8, LANES))
    return jnp.where(slots == lax.broadcasted_iota(jnp.int32, (8, LANES), 0), 1.0, 0.0).astype(F32)


def edge_work(
    stop,
    begin,
    slim_ready,
    wide_ready,
    slim,
    wide,
    count_ref,
    centres_ref,
    neighbours_ref,
    w_pair_ref,
    w_radial_ref,
    w_mix_ref,
    w_self_ref,
    w_tensor_ref,
    w_out_ref,
    result_ref,
    turned,
    spots,
    scalars,
    shift_rows,
    centre_slim,
    centre_wide,
    basis_rows,
    sphere_rows,
    back_rows,
    pulled,
    far_spots,
    sphere_spread,
    self_rows,
    slope_rows,
    mixing_rows,
):
    begin()

    neighbours = neighbours_ref[...]
    centres = turned_rows(centres_ref[...].astype(F32))[0:BLOCKS].astype(jnp.int32)
    spots[...] = table_row(neighbours)
    centre_spots = table_row(centres)
    slots = lane_slot((BLOCKS, EDGES))
    centre_rows = over_edges([centres[:, j : j + 1] for j in range(4)], slots)
    steps = [
        (one - other).astype(F32) * site_spacing
        for one, other in zip(coordinates(neighbours), coordinates(centre_rows))
    ]
    mask = slot_mask()
    w_pair = w_pair_ref[...]
    radial = w_radial_ref[...]
    radial_high, radial_low = split(radial)
    radial_rows = jnp.concatenate([radial_high.astype(F32), radial_low.astype(F32)], axis=0).astype(BF16)
    mix_turned = w_mix_ref[...].astype(F32)
    mix_turned = jnp.concatenate(
        [mix_turned[128:192], mix_turned[64:128], mix_turned[0:64]], axis=0
    )
    mix_back = mix_turned.T.astype(BF16)
    mix_turned = mix_turned.astype(BF16)
    update = jnp.concatenate([w_self_ref[...], w_tensor_ref[...]], axis=0)
    update_turned = update.astype(F32).T.astype(BF16)
    from_latent = jnp.concatenate([mix_turned, update_turned[:, 0:128]], axis=0)
    tensor_turned = update_turned[:, 128:192]
    w_out = jnp.broadcast_to(w_out_ref[...].astype(F32), (128, 128)).T
    w_out = jnp.concatenate([w_out, w_out], axis=1)
    low_half = lax.broadcasted_iota(jnp.int32, (8, 128), 1) < 64
    nothing = jnp.zeros((8, 128), F32)

    slim_ready()
    if stop == 0:
        return

    turned[...] = slim[...].astype(F32).T[0:80].astype(BF16)

    centre_shift = []
    lanes_of_rows = lax.broadcasted_iota(jnp.int32, (BLOCKS, ROWS), 1)
    for place in range(4):
        hits = jnp.where(centre_spots[:, place : place + 1] == lanes_of_rows, 1.0, 0.0).astype(BF16)
        got = dot_nn(hits, slim[...])
        centre_slim[pl.ds(place, BLOCKS, stride=4), :] = got
        centre_shift.append([got[:, 64 + axis : 65 + axis] for axis in range(3)])

    def gather(turn, _):
        rows = lax.broadcasted_iota(jnp.int32, (ROWS, EDGES), 0).astype(jnp.int16)
        one, none = jnp.ones((), BF16), jnp.zeros((), BF16)
        for pair in [turn * GATHER + at for at in range(GATHER)]:
            hits = []
            for block in range(2):
                spot = spots[pl.ds(2 * pair + block, 1), :].astype(jnp.int16)
                hits.append(jnp.where(rows == spot, one, none))
            got = dot_nn(turned[...], jnp.concatenate(hits, axis=1))
            scalars[pair] = got[0:64].astype(BF16)
            for block in range(2):
                shift_rows[pl.ds(pl.multiple_of((2 * pair + block) * 8, 8), 8), :] = got[
                    64:72, EDGES * block : EDGES * block + EDGES
                ]
        return 0

    lax.fori_loop(0, PAIRS // GATHER, gather, 0)
    if stop == 1:
        return

    vector = []
    for axis in range(3):
        near = shift_rows[pl.ds(axis, BLOCKS, stride=8), :]
        far = over_edges([centre_shift[j][axis] for j in range(4)], slots)
        vector.append(steps[axis] + (near - far))
    distance = jnp.sqrt(vector[0] * vector[0] + vector[1] * vector[1] + vector[2] * vector[2])
    inverse = 1.0 / distance
    ux, uy, uz = [part * inverse for part in vector]
    inside = distance < cutoff_radius
    scaled = jnp.minimum(distance * (1.0 / cutoff_radius), 1.0)
    fifth = (scaled * scaled) * (scaled * scaled) * scaled
    envelope = 1.0 - fifth * scaled * (28.0 - scaled * (48.0 - 21.0 * scaled))
    envelope_slope = jnp.where(
        inside, fifth * (-168.0 + scaled * (336.0 - 168.0 * scaled)) * (1.0 / cutoff_radius), 0.0
    )
    sine, cosine = jnp.sin(math.pi * scaled), jnp.cos(math.pi * scaled)
    norm = math.sqrt(2.0 / cutoff_radius) * inverse
    cut_norm = norm * envelope
    slope_sine = norm * (envelope_slope - envelope * inverse)
    slope_cosine = jnp.where(inside, cut_norm * (math.pi / cutoff_radius), 0.0)
    sines, cosines = [sine], [cosine]
    for _ in range(7):
        s, c = sines[-1], cosines[-1]
        sines.append(s * cosine + c * sine)
        cosines.append(c * cosine - s * sine)
    for k in range(8):
        basis_rows[pl.ds(k, BLOCKS, stride=8), :] = sines[k] * cut_norm
    sphere = (
        root_three * ux,
        root_three * uy,
        root_three * uz,
        root_fifteen * ux * uy,
        root_fifteen * uy * uz,
        0.5 * root_five * (3.0 * uz * uz - 1.0),
        root_fifteen * ux * uz,
        0.5 * root_fifteen * (ux * ux - uy * uy),
    )
    for m in range(8):
        sphere_rows[pl.ds(m, BLOCKS, stride=8), :] = sphere[m]

    centre_slim[...] = dot_nn(centre_slim[:, 0:64].astype(BF16), w_pair[0:64])

    if stop == 2:
        return

    def latents(pair):
        at = pl.multiple_of(8 * pair, 8)
        high, low = split(centre_slim[pl.ds(at, 8), :])
        left = jnp.concatenate(
            [
                w_pair[64:128].astype(F32),
                high.astype(F32),
                low.astype(F32),
                radial_high.astype(F32),
                radial_high.astype(F32),
                radial_low.astype(F32),
                jnp.zeros((24, 128), F32),
            ],
            axis=0,
        ).T.astype(BF16)
        at = pl.multiple_of(16 * pair, 16)
        basis = jnp.concatenate(
            [basis_rows[pl.ds(at, 8), :], basis_rows[pl.ds(at + 8, 8), :]], axis=1
        )
        high, low = split(basis)
        right = jnp.concatenate(
            [mask, mask, high.astype(F32), low.astype(F32), high.astype(F32), jnp.zeros((24, LANES), F32)],
            axis=0,
        ).astype(BF16)
        return dot_nn(left, jnp.concatenate([scalars[pair], right], axis=0))

    def tensors(pair):
        at = pl.multiple_of(8 * pair, 8)
        parts = [centre_wide[g, pl.ds(at, 8), :] for g in range(5)]
        turns = [pltpu.roll(part, 64, 1) for part in parts]
        order_one = [turns[1], parts[1], turns[2]]
        order_two = [turns[2], parts[3], turns[3], parts[4], turns[4]]
        rows = [jnp.where(low_half, 0.0, part) for part in order_one]
        rows += [jnp.where(low_half, part, 0.0) for part in order_two]
        back = jnp.concatenate(rows, axis=0)
        zero = jnp.where(low_half, turns[0], 0.0)
        first = jnp.concatenate([back, nothing, nothing], axis=0).T
        second = jnp.concatenate([nothing] * 8 + [zero, nothing], axis=0).T[0:64]
        front = jnp.concatenate([first, second], axis=0)
        return front.astype(BF16), back.astype(BF16)

    def spheres(pair):
        at = pl.multiple_of(16 * pair, 16)
        sphere = jnp.concatenate(
            [sphere_rows[pl.ds(at, 8), :], sphere_rows[pl.ds(at + 8, 8), :]], axis=1
        )
        rows = [jnp.broadcast_to(sphere[m : m + 1], (8, LANES)) * mask for m in range(8)]
        return jnp.concatenate(rows + [mask, jnp.zeros((8, LANES), F32)], axis=0).astype(BF16)

    def silu_parts(x):
        gate = 0.5 * jnp.tanh(0.5 * x) + 0.5
        value = x * gate
        return value, gate + value * (1.0 - gate)

    each = range(FIRST)

    def first_group(turn, _):
        pairs = [turn * FIRST + g for g in each]
        first = [silu_parts(latents(p)) for p in pairs]
        for g in each:
            latent = first[g][0].astype(BF16)
            slope_rows[pairs[g]] = first[g][1]
            made = dot_nn(from_latent, latent)
            mixing_rows[pairs[g]] = made[0:192]
            self_rows[pairs[g]] = made[192:320]
            sphere_spread[pairs[g]] = spheres(pairs[g])
        return 0

    lax.fori_loop(0, PAIRS // FIRST, first_group, 0)
    if stop == 3:
        return

    wide_ready()
    for place in range(4):
        hits = jnp.where(centre_spots[:, place : place + 1] == lanes_of_rows, 1.0, 0.0).astype(BF16)
        got = dot_nn(hits, wide[...])
        for at in range(WIDE // 128):
            centre_wide[at, pl.ds(place, BLOCKS, stride=4), :] = got[:, 128 * at : 128 * at + 128]

    if stop == 4:
        return

    def second_group(turn, _):
        each = range(SECOND)
        pairs = [turn * SECOND + g for g in each]
        sides = [tensors(p) for p in pairs]
        contracted = [dot_nn(sides[g][0], sphere_spread[pairs[g]]) for g in each]
        mixing = [mixing_rows[p] for p in pairs]
        coupled = []
        for g in each:
            product = mixing[g] * contracted[g]
            coupled.append((product[0:64] + product[64:128] + product[128:192]).astype(BF16))
        hidden_in = [
            self_rows[pairs[g]] + dot_nn(tensor_turned, coupled[g]) for g in each
        ]
        second = [silu_parts(x) for x in hidden_in]
        readout = [jnp.sum(value * w_out, axis=0, keepdims=True) for value, _ in second]
        back = [dot_nn(update, (slope * w_out).astype(BF16)) for _, slope in second]
        to_mixing, to_contracted = [], []
        for g in each:
            cotangent = back[g][128:192].astype(BF16).astype(F32)
            cotangents = jnp.concatenate([cotangent, cotangent, cotangent], axis=0)
            to_mixing.append((cotangents * contracted[g]).astype(BF16))
            to_contracted.append((cotangents[0:128] * mixing[g][0:128]).astype(BF16))
        to_latent = [dot_nn(mix_back, to_mixing[g]) for g in each]
        to_sphere = [dot_nn(sides[g][1], to_contracted[g]) for g in each]
        to_input = [
            ((back[g][0:128] + to_latent[g]) * slope_rows[pairs[g]]).astype(BF16) for g in each
        ]
        to_basis = [dot_nn(radial_rows, to_input[g]) for g in each]
        for g in each:
            sphere = jnp.sum(to_sphere[g].reshape(8, 8, LANES) * mask[None], axis=1)
            basis = to_basis[g][0:8] + to_basis[g][8:16]
            for block in range(2):
                at = (2 * pairs[g] + block) * 24
                lanes = slice(EDGES * block, EDGES * block + EDGES)
                back_rows[pl.ds(pl.multiple_of(at, 8), 8), :] = sphere[:, lanes]
                back_rows[pl.ds(pl.multiple_of(at + 8, 8), 8), :] = basis[:, lanes]
                back_rows[pl.ds(pl.multiple_of(at + 16, 8), 8), :] = jnp.broadcast_to(
                    readout[g][:, lanes], (8, EDGES)
                )
        return 0

    lax.fori_loop(0, PAIRS // SECOND, second_group, 0)
    if stop == 5:
        return

    def backs(row):
        return back_rows[pl.ds(row, BLOCKS, stride=24), :]

    count = count_ref[...]
    active = lax.broadcasted_iota(jnp.int32, (BLOCKS, EDGES), 0) < count
    readout = backs(16)
    energy = jnp.where(active, envelope * readout, 0.0)
    radial_pull = envelope_slope * readout
    along_sine, along_cosine = 0.0, 0.0
    for k in range(8):
        to_basis = backs(8 + k)
        along_sine = along_sine + to_basis * sines[k]
        along_cosine = along_cosine + to_basis * (cosines[k] * (k + 1.0))
    radial_pull = radial_pull + envelope * (along_sine * slope_sine + along_cosine * slope_cosine)
    y1, y2, y3, y4, y5, y6, y7, y8 = [backs(m) for m in range(8)]
    gx = root_three * y1 + root_fifteen * (uy * y4 + uz * y7 + ux * y8)
    gy = root_three * y2 + root_fifteen * (ux * y4 + uz * y5 - uy * y8)
    gz = root_three * y3 + root_fifteen * (uy * y5 + ux * y7) + (3.0 * root_five) * uz * y6
    turn_norm = envelope * inverse
    radial_pull = radial_pull - turn_norm * (gx * ux + gy * uy + gz * uz)
    pulls = [
        jnp.where(active, radial_pull * u + turn_norm * g, 0.0)
        for u, g in ((ux, gx), (uy, gy), (uz, gz))
    ]
    for at, value in enumerate(pulls + [energy]):
        high, low = split(value)
        pulled[pl.ds(at, BLOCKS, stride=8), :] = high.astype(F32)
        pulled[pl.ds(4 + at, BLOCKS, stride=8), :] = low.astype(F32)
    spots[...] = inner_atom(neighbours)
    far_spots[...] = inner_atom(centre_rows)
    if stop == 6:
        return

    def scatter(turn, total):
        near, far, values = [], [], []
        atoms = lax.broadcasted_iota(jnp.int32, (64, EDGES), 0).astype(jnp.int16)
        one, none = jnp.ones((), BF16), jnp.zeros((), BF16)
        for at in range(SCATTER):
            block = turn * SCATTER + at
            spot = spots[pl.ds(block, 1), :].astype(jnp.int16)
            near.append(jnp.where(atoms == spot, one, none))
            spot = far_spots[pl.ds(block, 1), :].astype(jnp.int16)
            far.append(jnp.where(atoms == spot, one, none))
            values.append(pulled[pl.ds(pl.multiple_of(8 * block, 8), 8), :])
        near = jnp.concatenate(near, axis=1)
        far = jnp.concatenate(far, axis=1)
        values = jnp.concatenate(values, axis=1).astype(BF16)
        return total + dot_nt(jnp.concatenate([far - near, far], axis=0), values)

    total = lax.fori_loop(0, BLOCKS // SCATTER, scatter, jnp.zeros((128, 8), F32))
    total = jnp.concatenate([total, jnp.zeros((128, 120), F32)], axis=1).T
    total = total[0:4] + total[4:8]
    for axis in range(3):
        result_ref[axis] = total[axis : axis + 1, 0:64]
    result_ref[3] = total[3:4, 64:128]


def edge_scratch():
    return [
        pltpu.VMEM((80, ROWS), BF16),
        pltpu.VMEM((BLOCKS, EDGES), jnp.int32),
        pltpu.VMEM((PAIRS, 64, LANES), BF16),
        pltpu.VMEM((8 * BLOCKS, EDGES), F32),
        pltpu.VMEM((4 * BLOCKS, SLIM), F32),
        pltpu.VMEM((WIDE // 128, 4 * BLOCKS, 128), F32),
        pltpu.VMEM((8 * BLOCKS, EDGES), F32),
        pltpu.VMEM((8 * BLOCKS, EDGES), F32),
        pltpu.VMEM((24 * BLOCKS, EDGES), F32),
        pltpu.VMEM((8 * BLOCKS, EDGES), F32),
        pltpu.VMEM((BLOCKS, EDGES), jnp.int32),
        pltpu.VMEM((PAIRS, 80, LANES), BF16),
        pltpu.VMEM((PAIRS, 128, LANES), F32),
        pltpu.VMEM((PAIRS, 128, LANES), F32),
        pltpu.VMEM((PAIRS, 192, LANES), F32),
    ]


HALO_SCRATCH = 14


def whole_kernel(features_ref, shifts_ref, *refs):
    operands, refs = refs[:10], refs[10:]
    slim, wide, by_slim_out, by_wide_out, by_slim_in, by_wide_in = refs[:6]
    corner_slim, corner_wide, packed = refs[6:9]
    by_send, by_recv, send_sem, recv_sem, go = refs[9:HALO_SCRATCH]
    place = Place()
    greet(place)
    place_own(features_ref, shifts_ref, slim, wide, by_slim_out, by_wide_out, packed)
    exchanges = [
        kind(
            place,
            table,
            out,
            landed,
            corner,
            by_send.at[t],
            by_recv.at[t],
            send_sem.at[t],
            recv_sem.at[t],
        )
        for t, (kind, table, out, landed, corner) in enumerate(
            (
                (SlimExchange, slim, by_slim_out, by_slim_in, corner_slim),
                (Exchange, wide, by_wide_out, by_wide_in, corner_wide),
            )
        )
    ]

    def begin():
        meet(place)
        help_others(place, go)
        start_first(place, exchanges)

    def slim_ready():
        start_second(place, exchanges, go)
        pass_on(place, exchanges)
        exchanges[0].arrive()

    def wide_ready():
        exchanges[1].arrive()

    edge_work(None, begin, slim_ready, wide_ready, slim, wide, *operands, *refs[HALO_SCRATCH:])
    for exchange in exchanges:
        exchange.close()


VMEM = pl.BlockSpec(memory_space=pltpu.VMEM)


def whole(*operands):
    return pl.pallas_call(
        whole_kernel,
        out_shape=jax.ShapeDtypeStruct((4, 1, 64), F32),
        in_specs=[VMEM] * 11,
        out_specs=VMEM,
        scratch_shapes=[
            pltpu.VMEM((ROWS, SLIM), BF16),
            pltpu.VMEM((ROWS, WIDE), BF16),
            pltpu.VMEM((2, 32, SLIM), BF16),
            pltpu.VMEM((2, 32, WIDE), BF16),
            pltpu.VMEM((2, 32, SLIM), BF16),
            pltpu.VMEM((2, 32, WIDE), BF16),
            pltpu.VMEM((2, 16, SLIM), BF16),
            pltpu.VMEM((2, 16, WIDE), BF16),
            pltpu.VMEM((64, SLIM), F32),
            pltpu.SemaphoreType.DMA((2, 4)),
            pltpu.SemaphoreType.DMA((2, 4)),
            pltpu.SemaphoreType.DMA((2, 3, SENDS)),
            pltpu.SemaphoreType.DMA((2, 3, SENDS)),
            pltpu.SemaphoreType.REGULAR((2,)),
        ]
        + edge_scratch(),
        compiler_params=pltpu.CompilerParams(
            collective_id=0, has_side_effects=True, vmem_limit_bytes=56 * 2**20
        ),
        name="boxes",
    )(*operands)


def per_device(
    features,
    shifts,
    block_counts,
    block_centres,
    block_neighbours,
    w_pair,
    w_radial,
    w_mix,
    w_self,
    w_tensor,
    w_out,
):
    result = whole(
        features.reshape(64, WIDE),
        shifts.reshape(64, 3).T,
        block_counts.reshape(1, 1),
        block_centres.reshape(BLOCKS, 4).T,
        block_neighbours.reshape(BLOCKS, EDGES),
        w_pair,
        w_radial,
        w_mix.T,
        w_self,
        w_tensor,
        w_out.reshape(1, 128),
    )
    return result[3].reshape(1, 1, 1, 64), result[0:3].reshape(1, 1, 1, 3, 64)


def solution(mesh):
    in_specs = (
        P("bx", "by", "bz", None, None),
        P("bx", "by", "bz", None, None),
        P("bx", "by", "bz"),
        P("bx", "by", "bz", None, None),
        P("bx", "by", "bz", None, None),
        P(),
        P(),
        P(),
        P(),
        P(),
        P(),
    )
    out_specs = (P("bx", "by", "bz", None), P("bx", "by", "bz", None, None))
    return jax.shard_map(
        per_device, mesh=mesh, in_specs=in_specs, out_specs=out_specs, check_vma=False
    )
```

```python
import functools
import math

import jax
import jax.numpy as jnp
from jax import lax
from jax.experimental import pallas as pl
from jax.experimental.pallas import tpu as pltpu
from jax.sharding import PartitionSpec as P

MESH = pl.DeviceIdType.MESH
F32 = jnp.float32
BF16 = jnp.bfloat16

cutoff_radius = 6.0
site_spacing = 1.7
root_three = math.sqrt(3.0)
root_five = math.sqrt(5.0)
root_fifteen = math.sqrt(15.0)

ROWS = 512
HALF = 256
WIDE = 640
SLIM = 128
BLOCKS = 48
EDGES = 128
PAIRS = BLOCKS // 2
SCATTER = 24
GATHER = 24
FIRST = 24
SECOND = 12
LANES = 2 * EDGES


def phase_two_sends():
    return (
        (0, 1, 32, 64, 32),
        (0, -1, 0, 96, 32),
        (1, 0, 16, 128, 16),
        (1, 0, 48, 144, 16),
        (-1, 0, 0, 160, 16),
        (-1, 0, 32, 176, 16),
        (1, 1, 48, 192, 16),
        (1, -1, 16, 208, 16),
        (-1, 1, 32, 224, 16),
        (-1, -1, 0, 240, 16),
    )


SENDS = len(phase_two_sends())


def wrapped(axis, step):
    size = lax.axis_size(axis)
    return lax.rem(lax.axis_index(axis) + size + step, size)


def at_device(dx, dy, dz):
    return (wrapped("bx", dx), wrapped("by", dy), wrapped("bz", dz))


def octants(rows, order):
    return jnp.concatenate([rows[8 * o : 8 * o + 8] for o in order], axis=0)


def place_own(features_ref, shifts_ref, slim, wide, by_slim_out, by_wide_out, packed):
    packed[...] = jnp.zeros_like(packed)
    packed[:, 0:64] = features_ref[:, 0:64].astype(F32)
    packed[:, 64:72] = turned_rows(shifts_ref[...].astype(F32))[0:64]
    own = [4 * ox + 2 * oy + oz for oz in range(2) for ox in range(2) for oy in range(2)]
    for source, table, out in (
        (packed[...], slim, by_slim_out),
        (features_ref[...].astype(F32), wide, by_wide_out),
    ):
        table[0:64, :] = octants(source, own).astype(BF16)
        for oy in range(2):
            face = [4 * ox + 2 * oy + oz for oz in range(2) for ox in range(2)]
            out[oy] = octants(source, face).astype(BF16)


def place_octants(table, first, landed, count):
    pieces = []
    below, above = landed[0].astype(F32), landed[1].astype(F32)
    for q in range(count):
        pieces += [below[8 * q : 8 * q + 8], above[8 * q : 8 * q + 8]]
    table[first : first + 16 * count, :] = jnp.concatenate(pieces, axis=0).astype(BF16)


class Place:
    def __init__(self):
        self.bx, self.by, self.bz = (lax.axis_index(axis) for axis in ("bx", "by", "bz"))
        self.ends = lax.axis_size("bz") - 1
        self.x, self.z_hi = lax.rem(self.by, 4), lax.div(self.by, 4)
        self.first_x, self.last_x = self.x == 0, self.x == 3
        self.edge = self.first_x | self.last_x
        self.early = self.z_hi == 0
        self.late = self.z_hi == 1
        self.low = self.bz == 0
        self.high = self.bz == self.ends
        self.middle = lax.div(lax.axis_size("bz"), 2)
        self.upper = self.bz >= self.middle
        self.by_helper = jnp.logical_not(self.edge) & self.late & (self.bz < self.middle)
        self.wrap_helper = self.late & (self.bz == self.middle)


def flips(place, side):
    return place.last_x if side == 0 else place.first_x


def signal(semaphore, device):
    pl.semaphore_signal(semaphore, inc=1, device_id=device, device_id_type=MESH)


def as_count(condition, amount):
    return jnp.where(condition, amount, 0)


def greet(place):
    barrier = pltpu.get_barrier_semaphore()
    for dx in (-1, 1):
        signal(barrier, at_device(dx, 0, 0))
    for side, dy in ((0, 1), (1, -1)):

        @pl.when(jnp.logical_not(flips(place, side)) | place.early)
        def _():
            signal(barrier, at_device(0, dy, 0))

    for dx in (-1, 0, 1):
        signal(barrier, at_device(dx, 0, -1))

        @pl.when(jnp.logical_not(place.high))
        def _():
            signal(barrier, at_device(dx, 0, 1))

    for side, dy in ((0, 1), (1, -1)):

        @pl.when(place.low)
        def _():
            signal(barrier, at_device(0, dy, -1))

        @pl.when(place.high & place.early & flips(place, side))
        def _():
            signal(barrier, at_device(0, dy, 1))

    @pl.when(place.edge & place.upper)
    def _():
        near_first = place.first_x == place.early
        signal(barrier, (place.bx, jnp.where(near_first, 5, 6), place.bz - place.middle))

    @pl.when(place.late & place.low)
    def _():
        signal(barrier, (place.bx, place.by, place.middle))

    @pl.when(place.late & place.high)
    def _():
        for dx in (-1, 0, 1):
            signal(barrier, (wrapped("bx", dx), place.by, place.middle))

        for side, dy in ((0, 1), (1, -1)):

            @pl.when(jnp.logical_not(flips(place, side)))
            def _():
                signal(barrier, (place.bx, place.by + dy, place.middle))


def meet(place):
    count = 2 + as_count(jnp.logical_not(place.edge), 1) + 1
    count = count + as_count(place.edge & place.late, 1)
    count = count + as_count(jnp.logical_not(place.low), 3) + 3
    count = count + as_count(place.high, 2)
    count = count + as_count(place.low & place.late & place.edge, 1)
    count = count + as_count(place.by_helper, 2)
    count = count + as_count(place.wrap_helper, 5 + as_count(jnp.logical_not(place.edge), 1))
    pl.semaphore_wait(pltpu.get_barrier_semaphore(), count)


def help_others(place, go):
    @pl.when(place.by_helper)
    def _():
        signal(go.at[0], (place.bx, jnp.where(place.x == 1, 0, 3), place.bz + place.middle))

    @pl.when(place.wrap_helper)
    def _():
        signal(go.at[1], (place.bx, place.by, 0))


class Exchange:
    def __init__(self, place, table, out, landed, corner, by_send, by_recv, send, recv):
        self.place = place
        self.table, self.out, self.landed, self.corner = table, out, landed, corner
        self.by_send, self.by_recv, self.send, self.recv = by_send, by_recv, send, recv

    def copy(self, source, target, send, recv, dx, dy, dz):
        return pltpu.make_async_remote_copy(
            src_ref=source,
            dst_ref=target,
            send_sem=send,
            recv_sem=recv,
            device_id=at_device(dx, dy, dz),
            device_id_type=MESH,
        )

    def by_copy(self, side):
        return self.copy(
            self.out.at[1 - side],
            self.landed.at[side],
            self.by_send.at[side],
            self.by_recv.at[side],
            0,
            1 - 2 * side,
            0,
        )

    def corner_copy(self, dz, side):
        return self.copy(
            self.out.at[1 - side, pl.ds(16 if dz > 0 else 0, 16)],
            self.corner.at[side],
            self.by_send.at[2 + side],
            self.by_recv.at[2 + side],
            0,
            1 - 2 * side,
            dz,
        )

    def half_copies(self, half):
        return [
            (
                functools.partial(
                    self.copy,
                    self.table.at[pl.ds(HALF * half + source, rows)],
                    self.table.at[pl.ds(HALF * half + target, rows)],
                    self.send.at[half, at],
                    self.recv.at[half, at],
                    dx,
                    0,
                    dz,
                ),
                dz,
            )
            for at, (dx, dz, source, target, rows) in enumerate(phase_two_sends())
        ]

    def late_copies(self, high):
        piece = HALF + (96 if high else 64)
        return [
            self.copy(
                self.table.at[pl.ds(piece + 16, 16)],
                self.table.at[pl.ds(HALF + 192 + 16 * high, 16)],
                self.send.at[2, 0],
                self.recv.at[2, 0],
                1,
                0,
                0,
            ),
            self.copy(
                self.table.at[pl.ds(piece, 16)],
                self.table.at[pl.ds(HALF + 224 + 16 * high, 16)],
                self.send.at[2, 1],
                self.recv.at[2, 1],
                -1,
                0,
                0,
            ),
        ]

    def start_by(self, far):
        for side in range(2):

            @pl.when(flips(self.place, side) if far else jnp.logical_not(flips(self.place, side)))
            def _():
                self.by_copy(side).start()

    def start_wrap(self, dz):
        for copy, along in self.half_copies(0):
            if along == dz:
                copy().start()

    def start_corners(self, dz, flipped=(True, False)):
        for side in range(2):
            if len(flipped) == 2:
                self.corner_copy(dz, side).start()
            else:

                @pl.when(flips(self.place, side) == flipped[0])
                def _():
                    self.corner_copy(dz, side).start()

    def start_own(self):
        for copy, dz in self.half_copies(0):
            if dz == 0:
                copy().start()
            else:

                @pl.when(jnp.logical_not(self.place.high if dz > 0 else self.place.low))
                def _():
                    copy().start()

    def spread_by(self):
        place_octants(self.table, HALF, self.landed, 4)
        for copy, dz in self.half_copies(1):
            if dz == 0:
                copy().start()
            else:

                @pl.when(jnp.logical_not(self.place.high if dz > 0 else self.place.low))
                def _():
                    copy().start()

    def wait_corners(self, dz):
        for side in range(2):
            self.corner_copy(dz, side).wait_recv()

    def take_corners(self, dz):
        place_octants(self.table, HALF + (64 if dz < 0 else 96), self.corner, 2)
        for copy in self.late_copies(int(dz > 0)):
            copy.start()

    def wait_wrap(self, dz):
        for copy, along in self.half_copies(0):
            if along == dz:
                copy().wait_recv()

    def arrive(self):
        for copy, dz in self.half_copies(0):
            if self.wraps_waited(dz):

                @pl.when(jnp.logical_not(self.place.low & self.place.early))
                def _():
                    copy().wait_recv()
            else:
                copy().wait_recv()
        for copy, dz in self.half_copies(1):
            if dz == 0:
                copy().wait_recv()
            else:

                @pl.when(jnp.logical_not(self.place.low if dz > 0 else self.place.high))
                def _():
                    copy().wait_recv()

        for wraps, high in ((self.place.low, 0), (self.place.high, 1)):

            @pl.when(wraps)
            def _():
                for copy in self.late_copies(high):
                    copy.wait_recv()

    def wraps_waited(self, dz):
        return False

    def close(self):
        for side in range(2):
            self.by_copy(side).wait_send()
        for copy, _ in self.half_copies(0):
            copy().wait_send()
        for copy, dz in self.half_copies(1):
            if dz == 0:
                copy().wait_send()
            else:

                @pl.when(jnp.logical_not(self.place.high if dz > 0 else self.place.low))
                def _():
                    copy().wait_send()

        for wraps, high in ((self.place.low, 0), (self.place.high, 1)):

            @pl.when(wraps)
            def _():
                for side in range(2):
                    self.corner_copy(2 * high - 1, side).wait_send()
                for copy in self.late_copies(high):
                    copy.wait_send()


class SlimExchange(Exchange):
    def wraps_waited(self, dz):
        return dz > 0


def start_first(place, exchanges):
    slim, wide = exchanges

    @pl.when(place.edge & place.late)
    def _():
        for exchange in exchanges:
            exchange.start_by(True)

    @pl.when(place.high)
    def _():
        slim.start_corners(1)
        slim.start_wrap(1)
        wide.start_corners(1)

    @pl.when(place.low & place.late)
    def _():
        for exchange in exchanges:
            exchange.start_corners(-1, (True,))

    for exchange in exchanges:
        exchange.start_by(False)
    slim.start_own()


def start_second(place, exchanges, go):
    wide = exchanges[1]
    wide.start_own()

    @pl.when(place.high)
    def _():
        wide.start_wrap(1)

    @pl.when(place.edge & place.early & place.upper)
    def _():
        pl.semaphore_wait(go.at[0], 1)
        for exchange in exchanges:
            exchange.start_by(True)

    @pl.when(place.low & place.late)
    def _():
        pl.semaphore_wait(go.at[1], 1)
        for exchange in exchanges:
            exchange.start_wrap(-1)
            exchange.start_corners(-1, (False,))


def pass_on(place, exchanges):
    slim, wide = exchanges
    for side in range(2):
        slim.by_copy(side).wait_recv()

    slim.spread_by()
    lower = place.edge & place.early & jnp.logical_not(place.upper)
    hurried = place.bz >= lax.div(place.middle, 2)

    @pl.when(lower)
    def _():
        slim.start_by(True)

    @pl.when(lower & hurried)
    def _():
        wide.start_by(True)

    @pl.when(place.low & place.early)
    def _():
        slim.wait_wrap(1)
        slim.wait_corners(-1)
        slim.take_corners(-1)

    @pl.when(place.low & place.late)
    def _():
        slim.wait_corners(-1)
        slim.take_corners(-1)

    @pl.when(place.high)
    def _():
        slim.wait_corners(1)
        slim.take_corners(1)

    for side in range(2):
        wide.by_copy(side).wait_recv()
    wide.spread_by()
    for wraps, dz in ((place.low, -1), (place.high, 1)):

        @pl.when(wraps)
        def _():
            wide.wait_corners(dz)
            wide.take_corners(dz)

    @pl.when(lower & jnp.logical_not(hurried))
    def _():
        wide.start_by(True)

    @pl.when(place.low & place.early)
    def _():
        for exchange in exchanges:
            exchange.start_wrap(-1)
            exchange.start_corners(-1)


def dot_nn(left, right):
    return lax.dot_general(left, right, (((1,), (0,)), ((), ())), preferred_element_type=F32)


def dot_nt(left, right):
    return lax.dot_general(left, right, (((1,), (1,)), ((), ())), preferred_element_type=F32)


def split(value):
    high = value.astype(BF16)
    return high, (value - high.astype(F32)).astype(BF16)


def cell_digits(row):
    return row >> 7, (row >> 5) & 3, (row >> 3) & 3, row & 7


def coordinates(row):
    ci, cj, ck, w = cell_digits(row)
    return (
        2 * (ci - 1) + (w >> 2),
        2 * (cj - 1) + ((w >> 1) & 1),
        2 * (ck - 1) + (w & 1),
    )


def table_row(row):
    ci, cj, ck, w = cell_digits(row)
    ox, oz = ci - 1, ck - 1
    inner_x = (ci == 1) | (ci == 2)
    inner_y = (cj == 1) | (cj == 2)
    inner_z = (ck == 1) | (ck == 2)
    x_side, z_side = ci >> 1, ck >> 1
    base = jnp.where(
        inner_x,
        jnp.where(inner_z, 32 * oz + 16 * ox, 64 + 32 * z_side + 16 * ox),
        jnp.where(inner_z, 128 + 32 * x_side + 16 * oz, 192 + 32 * x_side + 16 * z_side),
    )
    y_part = jnp.where(inner_y, 8 * (cj - 1), HALF + 8 * (cj >> 1))
    return base + y_part + w


def inner_atom(row):
    ci, cj, ck, w = cell_digits(row)
    inside = (ci == 1) | (ci == 2)
    inside = inside & ((cj == 1) | (cj == 2)) & ((ck == 1) | (ck == 2))
    return jnp.where(inside, 8 * (4 * (ci - 1) + 2 * (cj - 1) + ck - 1) + w, -1)


def lane_slot(shape):
    return lax.broadcasted_iota(jnp.int32, shape, 1) >> 5


def over_edges(columns, slots):
    spread = [jnp.broadcast_to(column, slots.shape) for column in columns]
    low = jnp.where(slots == 0, spread[0], spread[1])
    high = jnp.where(slots == 2, spread[2], spread[3])
    return jnp.where(slots < 2, low, high)


def turned_rows(value):
    rows, columns = value.shape
    value = jnp.concatenate([value, jnp.zeros((8 - rows, columns), F32)], axis=0)
    return jnp.concatenate([value, jnp.zeros((8, 128 - columns), F32)], axis=1).T


def slot_mask():
    slots = lane_slot((8, LANES))
    return jnp.where(slots == lax.broadcasted_iota(jnp.int32, (8, LANES), 0), 1.0, 0.0).astype(F32)


def edge_work(
    stop,
    begin,
    slim_ready,
    wide_ready,
    slim,
    wide,
    count_ref,
    centres_ref,
    neighbours_ref,
    w_pair_ref,
    w_radial_ref,
    w_mix_ref,
    w_self_ref,
    w_tensor_ref,
    w_out_ref,
    energies_ref,
    forces_ref,
    turned,
    spots,
    scalars,
    shift_rows,
    centre_slim,
    centre_wide,
    basis_rows,
    sphere_rows,
    back_rows,
    pulled,
    far_spots,
    atom_hits,
    sphere_spread,
    self_rows,
    slope_rows,
    mixing_rows,
):
    begin()

    neighbours = neighbours_ref[...]
    centres = turned_rows(centres_ref[...].astype(F32))[0:BLOCKS].astype(jnp.int32)
    spots[...] = table_row(neighbours)
    centre_spots = table_row(centres)
    slots = lane_slot((BLOCKS, EDGES))
    centre_rows = over_edges([centres[:, j : j + 1] for j in range(4)], slots)
    steps = [
        (one - other).astype(F32) * site_spacing
        for one, other in zip(coordinates(neighbours), coordinates(centre_rows))
    ]
    mask = slot_mask()
    w_pair = w_pair_ref[...]
    radial = w_radial_ref[...]
    radial_high, radial_low = split(radial)
    radial_rows = jnp.concatenate([radial_high.astype(F32), radial_low.astype(F32)], axis=0).astype(BF16)
    mix_turned = w_mix_ref[...].astype(F32)
    mix_turned = jnp.concatenate(
        [mix_turned[128:192], mix_turned[64:128], mix_turned[0:64]], axis=0
    )
    mix_back = mix_turned.T.astype(BF16)
    mix_turned = mix_turned.astype(BF16)
    update = jnp.concatenate([w_self_ref[...], w_tensor_ref[...]], axis=0)
    update_turned = update.astype(F32).T.astype(BF16)
    from_latent = jnp.concatenate([mix_turned, update_turned[:, 0:128]], axis=0)
    tensor_turned = update_turned[:, 128:192]
    w_out = jnp.broadcast_to(w_out_ref[...].astype(F32), (128, 128)).T
    w_out = jnp.concatenate([w_out, w_out], axis=1)
    low_half = lax.broadcasted_iota(jnp.int32, (8, 128), 1) < 64
    nothing = jnp.zeros((8, 128), F32)

    slim_ready()
    if stop == 0:
        return

    turned[...] = slim[...].astype(F32).T[0:80].astype(BF16)

    centre_shift = []
    lanes_of_rows = lax.broadcasted_iota(jnp.int32, (BLOCKS, ROWS), 1)
    for place in range(4):
        hits = jnp.where(centre_spots[:, place : place + 1] == lanes_of_rows, 1.0, 0.0).astype(BF16)
        got = dot_nn(hits, slim[...])
        centre_slim[pl.ds(place, BLOCKS, stride=4), :] = got
        centre_shift.append([got[:, 64 + axis : 65 + axis] for axis in range(3)])

    def gather(turn, _):
        rows = lax.broadcasted_iota(jnp.int32, (ROWS, EDGES), 0).astype(jnp.int16)
        one, none = jnp.ones((), BF16), jnp.zeros((), BF16)
        for pair in [turn * GATHER + at for at in range(GATHER)]:
            hits = []
            for block in range(2):
                spot = spots[pl.ds(2 * pair + block, 1), :].astype(jnp.int16)
                hits.append(jnp.where(rows == spot, one, none))
            got = dot_nn(turned[...], jnp.concatenate(hits, axis=1))
            scalars[pair] = got[0:64].astype(BF16)
            for block in range(2):
                shift_rows[pl.ds(pl.multiple_of((2 * pair + block) * 8, 8), 8), :] = got[
                    64:72, EDGES * block : EDGES * block + EDGES
                ]
        return 0

    lax.fori_loop(0, PAIRS // GATHER, gather, 0)
    if stop == 1:
        return

    vector = []
    for axis in range(3):
        near = shift_rows[pl.ds(axis, BLOCKS, stride=8), :]
        far = over_edges([centre_shift[j][axis] for j in range(4)], slots)
        vector.append(steps[axis] + (near - far))
    distance = jnp.sqrt(vector[0] * vector[0] + vector[1] * vector[1] + vector[2] * vector[2])
    inverse = 1.0 / distance
    ux, uy, uz = [part * inverse for part in vector]
    inside = distance < cutoff_radius
    scaled = jnp.minimum(distance * (1.0 / cutoff_radius), 1.0)
    fifth = (scaled * scaled) * (scaled * scaled) * scaled
    envelope = 1.0 - fifth * scaled * (28.0 - scaled * (48.0 - 21.0 * scaled))
    envelope_slope = jnp.where(
        inside, fifth * (-168.0 + scaled * (336.0 - 168.0 * scaled)) * (1.0 / cutoff_radius), 0.0
    )
    sine, cosine = jnp.sin(math.pi * scaled), jnp.cos(math.pi * scaled)
    norm = math.sqrt(2.0 / cutoff_radius) * inverse
    cut_norm = norm * envelope
    slope_sine = norm * (envelope_slope - envelope * inverse)
    slope_cosine = jnp.where(inside, cut_norm * (math.pi / cutoff_radius), 0.0)
    sines, cosines = [sine], [cosine]
    for _ in range(7):
        s, c = sines[-1], cosines[-1]
        sines.append(s * cosine + c * sine)
        cosines.append(c * cosine - s * sine)
    for k in range(8):
        basis_rows[pl.ds(k, BLOCKS, stride=8), :] = sines[k] * cut_norm
    sphere = (
        root_three * ux,
        root_three * uy,
        root_three * uz,
        root_fifteen * ux * uy,
        root_fifteen * uy * uz,
        0.5 * root_five * (3.0 * uz * uz - 1.0),
        root_fifteen * ux * uz,
        0.5 * root_fifteen * (ux * ux - uy * uy),
    )
    for m in range(8):
        sphere_rows[pl.ds(m, BLOCKS, stride=8), :] = sphere[m]

    centre_slim[...] = dot_nn(centre_slim[:, 0:64].astype(BF16), w_pair[0:64])

    if stop == 2:
        return

    def latents(pair):
        at = pl.multiple_of(8 * pair, 8)
        high, low = split(centre_slim[pl.ds(at, 8), :])
        left = jnp.concatenate(
            [
                w_pair[64:128].astype(F32),
                high.astype(F32),
                low.astype(F32),
                radial_high.astype(F32),
                radial_high.astype(F32),
                radial_low.astype(F32),
                jnp.zeros((24, 128), F32),
            ],
            axis=0,
        ).T.astype(BF16)
        at = pl.multiple_of(16 * pair, 16)
        basis = jnp.concatenate(
            [basis_rows[pl.ds(at, 8), :], basis_rows[pl.ds(at + 8, 8), :]], axis=1
        )
        high, low = split(basis)
        right = jnp.concatenate(
            [mask, mask, high.astype(F32), low.astype(F32), high.astype(F32), jnp.zeros((24, LANES), F32)],
            axis=0,
        ).astype(BF16)
        return dot_nn(left, jnp.concatenate([scalars[pair], right], axis=0))

    def tensors(pair):
        at = pl.multiple_of(8 * pair, 8)
        parts = [centre_wide[g, pl.ds(at, 8), :] for g in range(5)]
        turns = [pltpu.roll(part, 64, 1) for part in parts]
        order_one = [turns[1], parts[1], turns[2]]
        order_two = [turns[2], parts[3], turns[3], parts[4], turns[4]]
        rows = [jnp.where(low_half, 0.0, part) for part in order_one]
        rows += [jnp.where(low_half, part, 0.0) for part in order_two]
        back = jnp.concatenate(rows, axis=0)
        zero = jnp.where(low_half, turns[0], 0.0)
        first = jnp.concatenate([back, nothing, nothing], axis=0).T
        second = jnp.concatenate([nothing] * 8 + [zero, nothing], axis=0).T[0:64]
        front = jnp.concatenate([first, second], axis=0)
        return front.astype(BF16), back.astype(BF16)

    def spheres(pair):
        at = pl.multiple_of(16 * pair, 16)
        sphere = jnp.concatenate(
            [sphere_rows[pl.ds(at, 8), :], sphere_rows[pl.ds(at + 8, 8), :]], axis=1
        )
        rows = [jnp.broadcast_to(sphere[m : m + 1], (8, LANES)) * mask for m in range(8)]
        return jnp.concatenate(rows + [mask, jnp.zeros((8, LANES), F32)], axis=0).astype(BF16)

    def silu_parts(x):
        gate = 0.5 * jnp.tanh(0.5 * x) + 0.5
        value = x * gate
        return value, gate + value * (1.0 - gate)

    each = range(FIRST)

    def first_group(turn, _):
        pairs = [turn * FIRST + g for g in each]
        first = [silu_parts(latents(p)) for p in pairs]
        for g in each:
            latent = first[g][0].astype(BF16)
            slope_rows[pairs[g]] = first[g][1]
            made = dot_nn(from_latent, latent)
            mixing_rows[pairs[g]] = made[0:192]
            self_rows[pairs[g]] = made[192:320]
            sphere_spread[pairs[g]] = spheres(pairs[g])
        return 0

    lax.fori_loop(0, PAIRS // FIRST, first_group, 0)
    if stop == 3:
        return

    spots[...] = inner_atom(neighbours)
    far_spots[...] = inner_atom(centre_rows)
    atoms = lax.broadcasted_iota(jnp.int32, (64, EDGES), 0).astype(jnp.int16)
    one, none = jnp.ones((), BF16), jnp.zeros((), BF16)
    for block in range(BLOCKS):
        near = jnp.where(atoms == spots[block : block + 1, :].astype(jnp.int16), one, none)
        far = jnp.where(atoms == far_spots[block : block + 1, :].astype(jnp.int16), one, none)
        lanes = slice(EDGES * block, EDGES * block + EDGES)
        atom_hits[0:64, lanes] = far - near
        atom_hits[64:128, lanes] = far

    wide_ready()
    for place in range(4):
        hits = jnp.where(centre_spots[:, place : place + 1] == lanes_of_rows, 1.0, 0.0).astype(BF16)
        got = dot_nn(hits, wide[...])
        for at in range(WIDE // 128):
            centre_wide[at, pl.ds(place, BLOCKS, stride=4), :] = got[:, 128 * at : 128 * at + 128]

    if stop == 4:
        return

    def second_group(turn, _):
        each = range(SECOND)
        pairs = [turn * SECOND + g for g in each]
        sides = [tensors(p) for p in pairs]
        contracted = [dot_nn(sides[g][0], sphere_spread[pairs[g]]) for g in each]
        mixing = [mixing_rows[p] for p in pairs]
        coupled = []
        for g in each:
            product = mixing[g] * contracted[g]
            coupled.append((product[0:64] + product[64:128] + product[128:192]).astype(BF16))
        hidden_in = [
            self_rows[pairs[g]] + dot_nn(tensor_turned, coupled[g]) for g in each
        ]
        second = [silu_parts(x) for x in hidden_in]
        readout = [jnp.sum(value * w_out, axis=0, keepdims=True) for value, _ in second]
        back = [dot_nn(update, (slope * w_out).astype(BF16)) for _, slope in second]
        to_mixing, to_contracted = [], []
        for g in each:
            cotangent = back[g][128:192].astype(BF16).astype(F32)
            cotangents = jnp.concatenate([cotangent, cotangent, cotangent], axis=0)
            to_mixing.append((cotangents * contracted[g]).astype(BF16))
            to_contracted.append((cotangents[0:128] * mixing[g][0:128]).astype(BF16))
        to_latent = [dot_nn(mix_back, to_mixing[g]) for g in each]
        to_sphere = [dot_nn(sides[g][1], to_contracted[g]) for g in each]
        to_input = [
            ((back[g][0:128] + to_latent[g]) * slope_rows[pairs[g]]).astype(BF16) for g in each
        ]
        to_basis = [dot_nn(radial_rows, to_input[g]) for g in each]
        for g in each:
            sphere = jnp.sum(to_sphere[g].reshape(8, 8, LANES) * mask[None], axis=1)
            basis = to_basis[g][0:8] + to_basis[g][8:16]
            for block in range(2):
                at = (2 * pairs[g] + block) * 24
                lanes = slice(EDGES * block, EDGES * block + EDGES)
                back_rows[pl.ds(pl.multiple_of(at, 8), 8), :] = sphere[:, lanes]
                back_rows[pl.ds(pl.multiple_of(at + 8, 8), 8), :] = basis[:, lanes]
                back_rows[pl.ds(pl.multiple_of(at + 16, 8), 8), :] = jnp.broadcast_to(
                    readout[g][:, lanes], (8, EDGES)
                )
        return 0

    lax.fori_loop(0, PAIRS // SECOND, second_group, 0)
    if stop == 5:
        return

    def backs(row):
        return back_rows[pl.ds(row, BLOCKS, stride=24), :]

    count = count_ref[...]
    active = lax.broadcasted_iota(jnp.int32, (BLOCKS, EDGES), 0) < count
    readout = backs(16)
    energy = jnp.where(active, envelope * readout, 0.0)
    radial_pull = envelope_slope * readout
    along_sine, along_cosine = 0.0, 0.0
    for k in range(8):
        to_basis = backs(8 + k)
        along_sine = along_sine + to_basis * sines[k]
        along_cosine = along_cosine + to_basis * (cosines[k] * (k + 1.0))
    radial_pull = radial_pull + envelope * (along_sine * slope_sine + along_cosine * slope_cosine)
    y1, y2, y3, y4, y5, y6, y7, y8 = [backs(m) for m in range(8)]
    gx = root_three * y1 + root_fifteen * (uy * y4 + uz * y7 + ux * y8)
    gy = root_three * y2 + root_fifteen * (ux * y4 + uz * y5 - uy * y8)
    gz = root_three * y3 + root_fifteen * (uy * y5 + ux * y7) + (3.0 * root_five) * uz * y6
    turn_norm = envelope * inverse
    radial_pull = radial_pull - turn_norm * (gx * ux + gy * uy + gz * uz)
    pulls = [
        jnp.where(active, radial_pull * u + turn_norm * g, 0.0)
        for u, g in ((ux, gx), (uy, gy), (uz, gz))
    ]
    for at, value in enumerate(pulls + [energy]):
        high, low = split(value)
        pulled[pl.ds(at, BLOCKS, stride=8), :] = high.astype(F32)
        pulled[pl.ds(4 + at, BLOCKS, stride=8), :] = low.astype(F32)
    if stop == 6:
        return

    total = jnp.zeros((128, 8), F32)
    for turn in range(BLOCKS // SCATTER):
        values = [pulled[8 * at : 8 * at + 8, :] for at in range(turn * SCATTER, (turn + 1) * SCATTER)]
        values = jnp.concatenate(values, axis=1).astype(BF16)
        lanes = slice(turn * SCATTER * EDGES, (turn + 1) * SCATTER * EDGES)
        total = total + dot_nt(atom_hits[:, lanes], values)
    total = jnp.concatenate([total, jnp.zeros((128, 120), F32)], axis=1).T
    total = total[0:4] + total[4:8]
    for axis in range(3):
        forces_ref[axis] = total[axis : axis + 1, 0:64]
    energies_ref[...] = total[3:4, 64:128]


def edge_scratch():
    return [
        pltpu.VMEM((80, ROWS), BF16),
        pltpu.VMEM((BLOCKS, EDGES), jnp.int32),
        pltpu.VMEM((PAIRS, 64, LANES), BF16),
        pltpu.VMEM((8 * BLOCKS, EDGES), F32),
        pltpu.VMEM((4 * BLOCKS, SLIM), F32),
        pltpu.VMEM((WIDE // 128, 4 * BLOCKS, 128), F32),
        pltpu.VMEM((8 * BLOCKS, EDGES), F32),
        pltpu.VMEM((8 * BLOCKS, EDGES), F32),
        pltpu.VMEM((24 * BLOCKS, EDGES), F32),
        pltpu.VMEM((8 * BLOCKS, EDGES), F32),
        pltpu.VMEM((BLOCKS, EDGES), jnp.int32),
        pltpu.VMEM((128, BLOCKS * EDGES), BF16),
        pltpu.VMEM((PAIRS, 80, LANES), BF16),
        pltpu.VMEM((PAIRS, 128, LANES), F32),
        pltpu.VMEM((PAIRS, 128, LANES), F32),
        pltpu.VMEM((PAIRS, 192, LANES), F32),
    ]


HALO_SCRATCH = 14


def whole_kernel(features_ref, shifts_ref, *refs):
    operands, refs = refs[:11], refs[11:]
    slim, wide, by_slim_out, by_wide_out, by_slim_in, by_wide_in = refs[:6]
    corner_slim, corner_wide, packed = refs[6:9]
    by_send, by_recv, send_sem, recv_sem, go = refs[9:HALO_SCRATCH]
    place = Place()
    greet(place)
    place_own(features_ref, shifts_ref, slim, wide, by_slim_out, by_wide_out, packed)
    exchanges = [
        kind(
            place,
            table,
            out,
            landed,
            corner,
            by_send.at[t],
            by_recv.at[t],
            send_sem.at[t],
            recv_sem.at[t],
        )
        for t, (kind, table, out, landed, corner) in enumerate(
            (
                (SlimExchange, slim, by_slim_out, by_slim_in, corner_slim),
                (Exchange, wide, by_wide_out, by_wide_in, corner_wide),
            )
        )
    ]

    def begin():
        meet(place)
        help_others(place, go)
        start_first(place, exchanges)

    def slim_ready():
        start_second(place, exchanges, go)
        pass_on(place, exchanges)
        exchanges[0].arrive()

    def wide_ready():
        exchanges[1].arrive()

    edge_work(None, begin, slim_ready, wide_ready, slim, wide, *operands, *refs[HALO_SCRATCH:])
    for exchange in exchanges:
        exchange.close()


VMEM = pl.BlockSpec(memory_space=pltpu.VMEM)


def whole(*operands):
    return pl.pallas_call(
        whole_kernel,
        out_shape=(
            jax.ShapeDtypeStruct((1, 64), F32),
            jax.ShapeDtypeStruct((3, 1, 64), F32),
        ),
        in_specs=[VMEM] * 11,
        out_specs=(VMEM, VMEM),
        scratch_shapes=[
            pltpu.VMEM((ROWS, SLIM), BF16),
            pltpu.VMEM((ROWS, WIDE), BF16),
            pltpu.VMEM((2, 32, SLIM), BF16),
            pltpu.VMEM((2, 32, WIDE), BF16),
            pltpu.VMEM((2, 32, SLIM), BF16),
            pltpu.VMEM((2, 32, WIDE), BF16),
            pltpu.VMEM((2, 16, SLIM), BF16),
            pltpu.VMEM((2, 16, WIDE), BF16),
            pltpu.VMEM((64, SLIM), F32),
            pltpu.SemaphoreType.DMA((2, 4)),
            pltpu.SemaphoreType.DMA((2, 4)),
            pltpu.SemaphoreType.DMA((2, 3, SENDS)),
            pltpu.SemaphoreType.DMA((2, 3, SENDS)),
            pltpu.SemaphoreType.REGULAR((2,)),
        ]
        + edge_scratch(),
        compiler_params=pltpu.CompilerParams(
            collective_id=0, has_side_effects=True, vmem_limit_bytes=56 * 2**20
        ),
        name="boxes",
    )(*operands)


def per_device(
    features,
    shifts,
    block_counts,
    block_centres,
    block_neighbours,
    w_pair,
    w_radial,
    w_mix,
    w_self,
    w_tensor,
    w_out,
):
    energies, forces = whole(
        features.reshape(64, WIDE),
        shifts.reshape(64, 3).T,
        block_counts.reshape(1, 1),
        block_centres.reshape(BLOCKS, 4).T,
        block_neighbours.reshape(BLOCKS, EDGES),
        w_pair,
        w_radial,
        w_mix.T,
        w_self,
        w_tensor,
        w_out.reshape(1, 128),
    )
    return energies.reshape(1, 1, 1, 64), forces.reshape(1, 1, 1, 3, 64)


def solution(mesh):
    in_specs = (
        P("bx", "by", "bz", None, None),
        P("bx", "by", "bz", None, None),
        P("bx", "by", "bz"),
        P("bx", "by", "bz", None, None),
        P("bx", "by", "bz", None, None),
        P(),
        P(),
        P(),
        P(),
        P(),
        P(),
    )
    out_specs = (P("bx", "by", "bz", None), P("bx", "by", "bz", None, None))
    return jax.shard_map(
        per_device, mesh=mesh, in_specs=in_specs, out_specs=out_specs, check_vma=False
    )
```

```python
import functools
import math

import jax
import jax.numpy as jnp
from jax import lax
from jax.experimental import pallas as pl
from jax.experimental.pallas import tpu as pltpu
from jax.sharding import PartitionSpec as P

MESH = pl.DeviceIdType.MESH
F32 = jnp.float32
BF16 = jnp.bfloat16

cutoff_radius = 6.0
site_spacing = 1.7
root_three = math.sqrt(3.0)
root_five = math.sqrt(5.0)
root_fifteen = math.sqrt(15.0)

ROWS = 512
HALF = 256
WIDE = 640
SLIM = 128
BLOCKS = 48
EDGES = 128
PAIRS = BLOCKS // 2
SCATTER = 12
GATHER = 24
FIRST = 24
SECOND = 12
LANES = 2 * EDGES


def phase_two_sends():
    return (
        (0, 1, 32, 64, 32),
        (0, -1, 0, 96, 32),
        (1, 0, 16, 128, 16),
        (1, 0, 48, 144, 16),
        (-1, 0, 0, 160, 16),
        (-1, 0, 32, 176, 16),
        (1, 1, 48, 192, 16),
        (1, -1, 16, 208, 16),
        (-1, 1, 32, 224, 16),
        (-1, -1, 0, 240, 16),
    )


SENDS = len(phase_two_sends())


def wrapped(axis, step):
    size = lax.axis_size(axis)
    return lax.rem(lax.axis_index(axis) + size + step, size)


def at_device(dx, dy, dz):
    return (wrapped("bx", dx), wrapped("by", dy), wrapped("bz", dz))


def octants(rows, order):
    return jnp.concatenate([rows[8 * o : 8 * o + 8] for o in order], axis=0)


def place_own(features_ref, shifts_ref, slim, wide, by_slim_out, by_wide_out, packed):
    packed[...] = jnp.zeros_like(packed)
    packed[:, 0:64] = features_ref[:, 0:64].astype(F32)
    packed[:, 64:72] = turned_rows(shifts_ref[...].astype(F32))[0:64]
    own = [4 * ox + 2 * oy + oz for oz in range(2) for ox in range(2) for oy in range(2)]
    for source, table, out in (
        (packed[...], slim, by_slim_out),
        (features_ref[...].astype(F32), wide, by_wide_out),
    ):
        table[0:64, :] = octants(source, own).astype(BF16)
        for oy in range(2):
            face = [4 * ox + 2 * oy + oz for oz in range(2) for ox in range(2)]
            out[oy] = octants(source, face).astype(BF16)


def place_octants(table, first, landed, count):
    pieces = []
    below, above = landed[0].astype(F32), landed[1].astype(F32)
    for q in range(count):
        pieces += [below[8 * q : 8 * q + 8], above[8 * q : 8 * q + 8]]
    table[first : first + 16 * count, :] = jnp.concatenate(pieces, axis=0).astype(BF16)


class Place:
    def __init__(self):
        self.bx, self.by, self.bz = (lax.axis_index(axis) for axis in ("bx", "by", "bz"))
        self.ends = lax.axis_size("bz") - 1
        self.x, self.z_hi = lax.rem(self.by, 4), lax.div(self.by, 4)
        self.first_x, self.last_x = self.x == 0, self.x == 3
        self.edge = self.first_x | self.last_x
        self.early = self.z_hi == 0
        self.late = self.z_hi == 1
        self.low = self.bz == 0
        self.high = self.bz == self.ends
        self.middle = lax.div(lax.axis_size("bz"), 2)
        self.upper = self.bz >= self.middle
        self.by_helper = jnp.logical_not(self.edge) & self.late & (self.bz < self.middle)
        self.wrap_helper = self.late & (self.bz == self.middle)


def flips(place, side):
    return place.last_x if side == 0 else place.first_x


def signal(semaphore, device):
    pl.semaphore_signal(semaphore, inc=1, device_id=device, device_id_type=MESH)


def as_count(condition, amount):
    return jnp.where(condition, amount, 0)


def greet(place):
    barrier = pltpu.get_barrier_semaphore()
    for dx in (-1, 1):
        signal(barrier, at_device(dx, 0, 0))
    for side, dy in ((0, 1), (1, -1)):

        @pl.when(jnp.logical_not(flips(place, side)) | place.early)
        def _():
            signal(barrier, at_device(0, dy, 0))

    for dx in (-1, 0, 1):
        signal(barrier, at_device(dx, 0, -1))

        @pl.when(jnp.logical_not(place.high))
        def _():
            signal(barrier, at_device(dx, 0, 1))

    for side, dy in ((0, 1), (1, -1)):

        @pl.when(place.low)
        def _():
            signal(barrier, at_device(0, dy, -1))

        @pl.when(place.high & place.early & flips(place, side))
        def _():
            signal(barrier, at_device(0, dy, 1))

    @pl.when(place.edge & place.upper)
    def _():
        near_first = place.first_x == place.early
        signal(barrier, (place.bx, jnp.where(near_first, 5, 6), place.bz - place.middle))

    @pl.when(place.late & place.low)
    def _():
        signal(barrier, (place.bx, place.by, place.middle))

    @pl.when(place.late & place.high)
    def _():
        for dx in (-1, 0, 1):
            signal(barrier, (wrapped("bx", dx), place.by, place.middle))

        for side, dy in ((0, 1), (1, -1)):

            @pl.when(jnp.logical_not(flips(place, side)))
            def _():
                signal(barrier, (place.bx, place.by + dy, place.middle))


def meet(place):
    count = 2 + as_count(jnp.logical_not(place.edge), 1) + 1
    count = count + as_count(place.edge & place.late, 1)
    count = count + as_count(jnp.logical_not(place.low), 3) + 3
    count = count + as_count(place.high, 2)
    count = count + as_count(place.low & place.late & place.edge, 1)
    count = count + as_count(place.by_helper, 2)
    count = count + as_count(place.wrap_helper, 5 + as_count(jnp.logical_not(place.edge), 1))
    pl.semaphore_wait(pltpu.get_barrier_semaphore(), count)


def help_others(place, go):
    @pl.when(place.by_helper)
    def _():
        signal(go.at[0], (place.bx, jnp.where(place.x == 1, 0, 3), place.bz + place.middle))

    @pl.when(place.wrap_helper)
    def _():
        signal(go.at[1], (place.bx, place.by, 0))


class Exchange:
    def __init__(self, place, table, out, landed, corner, by_send, by_recv, send, recv):
        self.place = place
        self.table, self.out, self.landed, self.corner = table, out, landed, corner
        self.by_send, self.by_recv, self.send, self.recv = by_send, by_recv, send, recv

    def copy(self, source, target, send, recv, dx, dy, dz):
        return pltpu.make_async_remote_copy(
            src_ref=source,
            dst_ref=target,
            send_sem=send,
            recv_sem=recv,
            device_id=at_device(dx, dy, dz),
            device_id_type=MESH,
        )

    def by_copy(self, side):
        return self.copy(
            self.out.at[1 - side],
            self.landed.at[side],
            self.by_send.at[side],
            self.by_recv.at[side],
            0,
            1 - 2 * side,
            0,
        )

    def corner_copy(self, dz, side):
        return self.copy(
            self.out.at[1 - side, pl.ds(16 if dz > 0 else 0, 16)],
            self.corner.at[side],
            self.by_send.at[2 + side],
            self.by_recv.at[2 + side],
            0,
            1 - 2 * side,
            dz,
        )

    def half_copies(self, half):
        return [
            (
                functools.partial(
                    self.copy,
                    self.table.at[pl.ds(HALF * half + source, rows)],
                    self.table.at[pl.ds(HALF * half + target, rows)],
                    self.send.at[half, at],
                    self.recv.at[half, at],
                    dx,
                    0,
                    dz,
                ),
                dz,
            )
            for at, (dx, dz, source, target, rows) in enumerate(phase_two_sends())
        ]

    def late_copies(self, high):
        piece = HALF + (96 if high else 64)
        return [
            self.copy(
                self.table.at[pl.ds(piece + 16, 16)],
                self.table.at[pl.ds(HALF + 192 + 16 * high, 16)],
                self.send.at[2, 0],
                self.recv.at[2, 0],
                1,
                0,
                0,
            ),
            self.copy(
                self.table.at[pl.ds(piece, 16)],
                self.table.at[pl.ds(HALF + 224 + 16 * high, 16)],
                self.send.at[2, 1],
                self.recv.at[2, 1],
                -1,
                0,
                0,
            ),
        ]

    def start_by(self, far):
        for side in range(2):

            @pl.when(flips(self.place, side) if far else jnp.logical_not(flips(self.place, side)))
            def _():
                self.by_copy(side).start()

    def start_wrap(self, dz):
        for copy, along in self.half_copies(0):
            if along == dz:
                copy().start()

    def start_corners(self, dz, flipped=(True, False)):
        for side in range(2):
            if len(flipped) == 2:
                self.corner_copy(dz, side).start()
            else:

                @pl.when(flips(self.place, side) == flipped[0])
                def _():
                    self.corner_copy(dz, side).start()

    def start_own(self):
        for copy, dz in self.half_copies(0):
            if dz == 0:
                copy().start()
            else:

                @pl.when(jnp.logical_not(self.place.high if dz > 0 else self.place.low))
                def _():
                    copy().start()

    def spread_by(self):
        place_octants(self.table, HALF, self.landed, 4)
        for copy, dz in self.half_copies(1):
            if dz == 0:
                copy().start()
            else:

                @pl.when(jnp.logical_not(self.place.high if dz > 0 else self.place.low))
                def _():
                    copy().start()

    def wait_corners(self, dz):
        for side in range(2):
            self.corner_copy(dz, side).wait_recv()

    def take_corners(self, dz):
        place_octants(self.table, HALF + (64 if dz < 0 else 96), self.corner, 2)
        for copy in self.late_copies(int(dz > 0)):
            copy.start()

    def wait_wrap(self, dz):
        for copy, along in self.half_copies(0):
            if along == dz:
                copy().wait_recv()

    def arrive(self):
        for copy, dz in self.half_copies(0):
            if self.wraps_waited(dz):

                @pl.when(jnp.logical_not(self.place.low & self.place.early))
                def _():
                    copy().wait_recv()
            else:
                copy().wait_recv()
        for copy, dz in self.half_copies(1):
            if dz == 0:
                copy().wait_recv()
            else:

                @pl.when(jnp.logical_not(self.place.low if dz > 0 else self.place.high))
                def _():
                    copy().wait_recv()

        for wraps, high in ((self.place.low, 0), (self.place.high, 1)):

            @pl.when(wraps)
            def _():
                for copy in self.late_copies(high):
                    copy.wait_recv()

    def wraps_waited(self, dz):
        return False

    def close(self):
        for side in range(2):
            self.by_copy(side).wait_send()
        for copy, _ in self.half_copies(0):
            copy().wait_send()
        for copy, dz in self.half_copies(1):
            if dz == 0:
                copy().wait_send()
            else:

                @pl.when(jnp.logical_not(self.place.high if dz > 0 else self.place.low))
                def _():
                    copy().wait_send()

        for wraps, high in ((self.place.low, 0), (self.place.high, 1)):

            @pl.when(wraps)
            def _():
                for side in range(2):
                    self.corner_copy(2 * high - 1, side).wait_send()
                for copy in self.late_copies(high):
                    copy.wait_send()


class SlimExchange(Exchange):
    def wraps_waited(self, dz):
        return dz > 0


def start_first(place, exchanges):
    slim, wide = exchanges

    @pl.when(place.edge & place.late)
    def _():
        for exchange in exchanges:
            exchange.start_by(True)

    @pl.when(place.high)
    def _():
        slim.start_corners(1)
        slim.start_wrap(1)
        wide.start_corners(1)

    @pl.when(place.low & place.late)
    def _():
        for exchange in exchanges:
            exchange.start_corners(-1, (True,))

    for exchange in exchanges:
        exchange.start_by(False)
    slim.start_own()


def start_second(place, exchanges, go):
    wide = exchanges[1]
    wide.start_own()

    @pl.when(place.high)
    def _():
        wide.start_wrap(1)

    @pl.when(place.edge & place.early & place.upper)
    def _():
        pl.semaphore_wait(go.at[0], 1)
        for exchange in exchanges:
            exchange.start_by(True)

    @pl.when(place.low & place.late)
    def _():
        pl.semaphore_wait(go.at[1], 1)
        for exchange in exchanges:
            exchange.start_wrap(-1)
            exchange.start_corners(-1, (False,))


def pass_on(place, exchanges):
    slim, wide = exchanges
    for side in range(2):
        slim.by_copy(side).wait_recv()

    slim.spread_by()
    lower = place.edge & place.early & jnp.logical_not(place.upper)

    @pl.when(lower)
    def _():
        slim.start_by(True)

    @pl.when(place.low & place.early)
    def _():
        slim.wait_wrap(1)
        slim.wait_corners(-1)
        slim.take_corners(-1)

    @pl.when(place.low & place.late)
    def _():
        slim.wait_corners(-1)
        slim.take_corners(-1)

    @pl.when(place.high)
    def _():
        slim.wait_corners(1)
        slim.take_corners(1)

    @pl.when(place.low)
    def _():
        wide.wait_corners(-1)
        wide.take_corners(-1)

    for side in range(2):
        wide.by_copy(side).wait_recv()
    wide.spread_by()

    @pl.when(place.high)
    def _():
        wide.wait_corners(1)
        wide.take_corners(1)

    @pl.when(lower)
    def _():
        wide.start_by(True)

    @pl.when(place.low & place.early)
    def _():
        for exchange in exchanges:
            exchange.start_wrap(-1)
            exchange.start_corners(-1)


def dot_nn(left, right):
    return lax.dot_general(left, right, (((1,), (0,)), ((), ())), preferred_element_type=F32)


def dot_nt(left, right):
    return lax.dot_general(left, right, (((1,), (1,)), ((), ())), preferred_element_type=F32)


def split(value):
    high = value.astype(BF16)
    return high, (value - high.astype(F32)).astype(BF16)


def cell_digits(row):
    return row >> 7, (row >> 5) & 3, (row >> 3) & 3, row & 7


def coordinates(row):
    ci, cj, ck, w = cell_digits(row)
    return (
        2 * (ci - 1) + (w >> 2),
        2 * (cj - 1) + ((w >> 1) & 1),
        2 * (ck - 1) + (w & 1),
    )


def table_row(row):
    ci, cj, ck, w = cell_digits(row)
    ox, oz = ci - 1, ck - 1
    inner_x = (ci == 1) | (ci == 2)
    inner_y = (cj == 1) | (cj == 2)
    inner_z = (ck == 1) | (ck == 2)
    x_side, z_side = ci >> 1, ck >> 1
    base = jnp.where(
        inner_x,
        jnp.where(inner_z, 32 * oz + 16 * ox, 64 + 32 * z_side + 16 * ox),
        jnp.where(inner_z, 128 + 32 * x_side + 16 * oz, 192 + 32 * x_side + 16 * z_side),
    )
    y_part = jnp.where(inner_y, 8 * (cj - 1), HALF + 8 * (cj >> 1))
    return base + y_part + w


def inner_atom(row):
    ci, cj, ck, w = cell_digits(row)
    inside = (ci == 1) | (ci == 2)
    inside = inside & ((cj == 1) | (cj == 2)) & ((ck == 1) | (ck == 2))
    return jnp.where(inside, 8 * (4 * (ci - 1) + 2 * (cj - 1) + ck - 1) + w, -1)


def lane_slot(shape):
    return lax.broadcasted_iota(jnp.int32, shape, 1) >> 5


def over_edges(columns, slots):
    spread = [jnp.broadcast_to(column, slots.shape) for column in columns]
    low = jnp.where(slots == 0, spread[0], spread[1])
    high = jnp.where(slots == 2, spread[2], spread[3])
    return jnp.where(slots < 2, low, high)


def turned_rows(value):
    rows, columns = value.shape
    value = jnp.concatenate([value, jnp.zeros((8 - rows, columns), F32)], axis=0)
    return jnp.concatenate([value, jnp.zeros((8, 128 - columns), F32)], axis=1).T


def slot_mask():
    slots = lane_slot((8, LANES))
    return jnp.where(slots == lax.broadcasted_iota(jnp.int32, (8, LANES), 0), 1.0, 0.0).astype(F32)


def edge_work(
    stop,
    begin,
    slim_ready,
    wide_ready,
    slim,
    wide,
    count_ref,
    centres_ref,
    neighbours_ref,
    w_pair_ref,
    w_radial_ref,
    w_mix_ref,
    w_self_ref,
    w_tensor_ref,
    w_out_ref,
    energies_ref,
    forces_ref,
    turned,
    spots,
    scalars,
    shift_rows,
    centre_slim,
    centre_wide,
    basis_rows,
    sphere_rows,
    back_rows,
    pulled,
    far_spots,
    atom_hits,
    sphere_spread,
    self_rows,
    slope_rows,
    mixing_rows,
):
    begin()

    neighbours = neighbours_ref[...]
    centres = turned_rows(centres_ref[...].astype(F32))[0:BLOCKS].astype(jnp.int32)
    spots[...] = table_row(neighbours)
    centre_spots = table_row(centres)
    slots = lane_slot((BLOCKS, EDGES))
    centre_rows = over_edges([centres[:, j : j + 1] for j in range(4)], slots)
    steps = [
        (one - other).astype(F32) * site_spacing
        for one, other in zip(coordinates(neighbours), coordinates(centre_rows))
    ]
    mask = slot_mask()
    w_pair = w_pair_ref[...]
    radial = w_radial_ref[...]
    radial_high, radial_low = split(radial)
    radial_rows = jnp.concatenate([radial_high.astype(F32), radial_low.astype(F32)], axis=0).astype(BF16)
    mix_turned = w_mix_ref[...].astype(F32)
    mix_turned = jnp.concatenate(
        [mix_turned[128:192], mix_turned[64:128], mix_turned[0:64]], axis=0
    )
    mix_back = mix_turned.T.astype(BF16)
    mix_turned = mix_turned.astype(BF16)
    update = jnp.concatenate([w_self_ref[...], w_tensor_ref[...]], axis=0)
    update_turned = update.astype(F32).T.astype(BF16)
    from_latent = jnp.concatenate([mix_turned, update_turned[:, 0:128]], axis=0)
    tensor_turned = update_turned[:, 128:192]
    w_out = jnp.broadcast_to(w_out_ref[...].astype(F32), (128, 128)).T
    w_out = jnp.concatenate([w_out, w_out], axis=1)
    low_half = lax.broadcasted_iota(jnp.int32, (8, 128), 1) < 64
    nothing = jnp.zeros((8, 128), F32)

    slim_ready()
    if stop == 0:
        return

    turned[...] = slim[...].astype(F32).T[0:80].astype(BF16)

    centre_shift = []
    lanes_of_rows = lax.broadcasted_iota(jnp.int32, (BLOCKS, ROWS), 1)
    for place in range(4):
        hits = jnp.where(centre_spots[:, place : place + 1] == lanes_of_rows, 1.0, 0.0).astype(BF16)
        got = dot_nn(hits, slim[...])
        centre_slim[pl.ds(place, BLOCKS, stride=4), :] = got
        centre_shift.append([got[:, 64 + axis : 65 + axis] for axis in range(3)])

    def gather(turn, _):
        rows = lax.broadcasted_iota(jnp.int32, (ROWS, EDGES), 0).astype(jnp.int16)
        one, none = jnp.ones((), BF16), jnp.zeros((), BF16)
        for pair in [turn * GATHER + at for at in range(GATHER)]:
            hits = []
            for block in range(2):
                spot = spots[pl.ds(2 * pair + block, 1), :].astype(jnp.int16)
                hits.append(jnp.where(rows == spot, one, none))
            got = dot_nn(turned[...], jnp.concatenate(hits, axis=1))
            scalars[pair] = got[0:64].astype(BF16)
            for block in range(2):
                shift_rows[pl.ds(pl.multiple_of((2 * pair + block) * 8, 8), 8), :] = got[
                    64:72, EDGES * block : EDGES * block + EDGES
                ]
        return 0

    lax.fori_loop(0, PAIRS // GATHER, gather, 0)
    if stop == 1:
        return

    vector = []
    for axis in range(3):
        near = shift_rows[pl.ds(axis, BLOCKS, stride=8), :]
        far = over_edges([centre_shift[j][axis] for j in range(4)], slots)
        vector.append(steps[axis] + (near - far))
    distance = jnp.sqrt(vector[0] * vector[0] + vector[1] * vector[1] + vector[2] * vector[2])
    inverse = 1.0 / distance
    ux, uy, uz = [part * inverse for part in vector]
    inside = distance < cutoff_radius
    scaled = jnp.minimum(distance * (1.0 / cutoff_radius), 1.0)
    fifth = (scaled * scaled) * (scaled * scaled) * scaled
    envelope = 1.0 - fifth * scaled * (28.0 - scaled * (48.0 - 21.0 * scaled))
    envelope_slope = jnp.where(
        inside, fifth * (-168.0 + scaled * (336.0 - 168.0 * scaled)) * (1.0 / cutoff_radius), 0.0
    )
    sine, cosine = jnp.sin(math.pi * scaled), jnp.cos(math.pi * scaled)
    norm = math.sqrt(2.0 / cutoff_radius) * inverse
    cut_norm = norm * envelope
    slope_sine = norm * (envelope_slope - envelope * inverse)
    slope_cosine = jnp.where(inside, cut_norm * (math.pi / cutoff_radius), 0.0)
    sines, cosines = [sine], [cosine]
    for _ in range(7):
        s, c = sines[-1], cosines[-1]
        sines.append(s * cosine + c * sine)
        cosines.append(c * cosine - s * sine)
    for k in range(8):
        basis_rows[pl.ds(k, BLOCKS, stride=8), :] = sines[k] * cut_norm
    sphere = (
        root_three * ux,
        root_three * uy,
        root_three * uz,
        root_fifteen * ux * uy,
        root_fifteen * uy * uz,
        0.5 * root_five * (3.0 * uz * uz - 1.0),
        root_fifteen * ux * uz,
        0.5 * root_fifteen * (ux * ux - uy * uy),
    )
    for m in range(8):
        sphere_rows[pl.ds(m, BLOCKS, stride=8), :] = sphere[m]

    centre_slim[...] = dot_nn(centre_slim[:, 0:64].astype(BF16), w_pair[0:64])

    if stop == 2:
        return

    def latents(pair):
        at = pl.multiple_of(8 * pair, 8)
        high, low = split(centre_slim[pl.ds(at, 8), :])
        left = jnp.concatenate(
            [
                w_pair[64:128].astype(F32),
                high.astype(F32),
                low.astype(F32),
                radial_high.astype(F32),
                radial_high.astype(F32),
                radial_low.astype(F32),
                jnp.zeros((24, 128), F32),
            ],
            axis=0,
        ).T.astype(BF16)
        at = pl.multiple_of(16 * pair, 16)
        basis = jnp.concatenate(
            [basis_rows[pl.ds(at, 8), :], basis_rows[pl.ds(at + 8, 8), :]], axis=1
        )
        high, low = split(basis)
        right = jnp.concatenate(
            [mask, mask, high.astype(F32), low.astype(F32), high.astype(F32), jnp.zeros((24, LANES), F32)],
            axis=0,
        ).astype(BF16)
        return dot_nn(left, jnp.concatenate([scalars[pair], right], axis=0))

    def tensors(pair):
        at = pl.multiple_of(8 * pair, 8)
        parts = [centre_wide[g, pl.ds(at, 8), :] for g in range(5)]
        turns = [pltpu.roll(part, 64, 1) for part in parts]
        order_one = [turns[1], parts[1], turns[2]]
        order_two = [turns[2], parts[3], turns[3], parts[4], turns[4]]
        rows = [jnp.where(low_half, 0.0, part) for part in order_one]
        rows += [jnp.where(low_half, part, 0.0) for part in order_two]
        back = jnp.concatenate(rows, axis=0)
        zero = jnp.where(low_half, turns[0], 0.0)
        first = jnp.concatenate([back, nothing, nothing], axis=0).T
        second = jnp.concatenate([nothing] * 8 + [zero, nothing], axis=0).T[0:64]
        front = jnp.concatenate([first, second], axis=0)
        return front.astype(BF16), back.astype(BF16)

    def spheres(pair):
        at = pl.multiple_of(16 * pair, 16)
        sphere = jnp.concatenate(
            [sphere_rows[pl.ds(at, 8), :], sphere_rows[pl.ds(at + 8, 8), :]], axis=1
        )
        rows = [jnp.broadcast_to(sphere[m : m + 1], (8, LANES)) * mask for m in range(8)]
        return jnp.concatenate(rows + [mask, jnp.zeros((8, LANES), F32)], axis=0).astype(BF16)

    def silu_parts(x):
        gate = 0.5 * jnp.tanh(0.5 * x) + 0.5
        value = x * gate
        return value, gate + value * (1.0 - gate)

    each = range(FIRST)

    def first_group(turn, _):
        pairs = [turn * FIRST + g for g in each]
        first = [silu_parts(latents(p)) for p in pairs]
        for g in each:
            latent = first[g][0].astype(BF16)
            slope_rows[pairs[g]] = first[g][1]
            made = dot_nn(from_latent, latent)
            mixing_rows[pairs[g]] = made[0:192]
            self_rows[pairs[g]] = made[192:320]
            sphere_spread[pairs[g]] = spheres(pairs[g])
        return 0

    lax.fori_loop(0, PAIRS // FIRST, first_group, 0)
    if stop == 3:
        return

    spots[...] = inner_atom(neighbours)
    far_spots[...] = inner_atom(centre_rows)
    atoms = lax.broadcasted_iota(jnp.int32, (64, EDGES), 0).astype(jnp.int16)
    one, none = jnp.ones((), BF16), jnp.zeros((), BF16)
    for block in range(BLOCKS):
        near = jnp.where(atoms == spots[block : block + 1, :].astype(jnp.int16), one, none)
        far = jnp.where(atoms == far_spots[block : block + 1, :].astype(jnp.int16), one, none)
        lanes = slice(EDGES * block, EDGES * block + EDGES)
        atom_hits[0:64, lanes] = far - near
        atom_hits[64:128, lanes] = far

    wide_ready()
    for place in range(4):
        hits = jnp.where(centre_spots[:, place : place + 1] == lanes_of_rows, 1.0, 0.0).astype(BF16)
        got = dot_nn(hits, wide[...])
        for at in range(WIDE // 128):
            centre_wide[at, pl.ds(place, BLOCKS, stride=4), :] = got[:, 128 * at : 128 * at + 128]

    if stop == 4:
        return

    def second_group(turn, _):
        each = range(SECOND)
        pairs = [turn * SECOND + g for g in each]
        sides = [tensors(p) for p in pairs]
        contracted = [dot_nn(sides[g][0], sphere_spread[pairs[g]]) for g in each]
        mixing = [mixing_rows[p] for p in pairs]
        coupled = []
        for g in each:
            product = mixing[g] * contracted[g]
            coupled.append((product[0:64] + product[64:128] + product[128:192]).astype(BF16))
        hidden_in = [
            self_rows[pairs[g]] + dot_nn(tensor_turned, coupled[g]) for g in each
        ]
        second = [silu_parts(x) for x in hidden_in]
        readout = [jnp.sum(value * w_out, axis=0, keepdims=True) for value, _ in second]
        back = [dot_nn(update, (slope * w_out).astype(BF16)) for _, slope in second]
        to_mixing, to_contracted = [], []
        for g in each:
            cotangent = back[g][128:192].astype(BF16).astype(F32)
            cotangents = jnp.concatenate([cotangent, cotangent, cotangent], axis=0)
            to_mixing.append((cotangents * contracted[g]).astype(BF16))
            to_contracted.append((cotangents[0:128] * mixing[g][0:128]).astype(BF16))
        to_latent = [dot_nn(mix_back, to_mixing[g]) for g in each]
        to_sphere = [dot_nn(sides[g][1], to_contracted[g]) for g in each]
        to_input = [
            ((back[g][0:128] + to_latent[g]) * slope_rows[pairs[g]]).astype(BF16) for g in each
        ]
        to_basis = [dot_nn(radial_rows, to_input[g]) for g in each]
        for g in each:
            sphere = jnp.sum(to_sphere[g].reshape(8, 8, LANES) * mask[None], axis=1)
            basis = to_basis[g][0:8] + to_basis[g][8:16]
            for block in range(2):
                at = (2 * pairs[g] + block) * 24
                lanes = slice(EDGES * block, EDGES * block + EDGES)
                back_rows[pl.ds(pl.multiple_of(at, 8), 8), :] = sphere[:, lanes]
                back_rows[pl.ds(pl.multiple_of(at + 8, 8), 8), :] = basis[:, lanes]
                back_rows[pl.ds(pl.multiple_of(at + 16, 8), 8), :] = jnp.broadcast_to(
                    readout[g][:, lanes], (8, EDGES)
                )
        return 0

    lax.fori_loop(0, PAIRS // SECOND, second_group, 0)
    if stop == 5:
        return

    def backs(row):
        return back_rows[pl.ds(row, BLOCKS, stride=24), :]

    count = count_ref[...]
    active = lax.broadcasted_iota(jnp.int32, (BLOCKS, EDGES), 0) < count
    readout = backs(16)
    energy = jnp.where(active, envelope * readout, 0.0)
    radial_pull = envelope_slope * readout
    along_sine, along_cosine = 0.0, 0.0
    for k in range(8):
        to_basis = backs(8 + k)
        along_sine = along_sine + to_basis * sines[k]
        along_cosine = along_cosine + to_basis * (cosines[k] * (k + 1.0))
    radial_pull = radial_pull + envelope * (along_sine * slope_sine + along_cosine * slope_cosine)
    y1, y2, y3, y4, y5, y6, y7, y8 = [backs(m) for m in range(8)]
    gx = root_three * y1 + root_fifteen * (uy * y4 + uz * y7 + ux * y8)
    gy = root_three * y2 + root_fifteen * (ux * y4 + uz * y5 - uy * y8)
    gz = root_three * y3 + root_fifteen * (uy * y5 + ux * y7) + (3.0 * root_five) * uz * y6
    turn_norm = envelope * inverse
    radial_pull = radial_pull - turn_norm * (gx * ux + gy * uy + gz * uz)
    pulls = [
        jnp.where(active, radial_pull * u + turn_norm * g, 0.0)
        for u, g in ((ux, gx), (uy, gy), (uz, gz))
    ]
    for at, value in enumerate(pulls + [energy]):
        high, low = split(value)
        pulled[pl.ds(at, BLOCKS, stride=8), :] = high.astype(F32)
        pulled[pl.ds(4 + at, BLOCKS, stride=8), :] = low.astype(F32)
    if stop == 6:
        return

    total = jnp.zeros((8, 128), F32)
    for turn in range(BLOCKS // SCATTER):
        values = [pulled[8 * at : 8 * at + 8, :] for at in range(turn * SCATTER, (turn + 1) * SCATTER)]
        values = jnp.concatenate(values, axis=1).astype(BF16)
        lanes = slice(turn * SCATTER * EDGES, (turn + 1) * SCATTER * EDGES)
        total = total + dot_nt(values, atom_hits[:, lanes])
    total = total[0:4] + total[4:8]
    for axis in range(3):
        forces_ref[axis] = total[axis : axis + 1, 0:64]
    energies_ref[...] = total[3:4, 64:128]


def edge_scratch():
    return [
        pltpu.VMEM((80, ROWS), BF16),
        pltpu.VMEM((BLOCKS, EDGES), jnp.int32),
        pltpu.VMEM((PAIRS, 64, LANES), BF16),
        pltpu.VMEM((8 * BLOCKS, EDGES), F32),
        pltpu.VMEM((4 * BLOCKS, SLIM), F32),
        pltpu.VMEM((WIDE // 128, 4 * BLOCKS, 128), F32),
        pltpu.VMEM((8 * BLOCKS, EDGES), F32),
        pltpu.VMEM((8 * BLOCKS, EDGES), F32),
        pltpu.VMEM((24 * BLOCKS, EDGES), F32),
        pltpu.VMEM((8 * BLOCKS, EDGES), F32),
        pltpu.VMEM((BLOCKS, EDGES), jnp.int32),
        pltpu.VMEM((128, BLOCKS * EDGES), BF16),
        pltpu.VMEM((PAIRS, 80, LANES), BF16),
        pltpu.VMEM((PAIRS, 128, LANES), F32),
        pltpu.VMEM((PAIRS, 128, LANES), F32),
        pltpu.VMEM((PAIRS, 192, LANES), F32),
    ]


HALO_SCRATCH = 14


def whole_kernel(features_ref, shifts_ref, *refs):
    operands, refs = refs[:11], refs[11:]
    slim, wide, by_slim_out, by_wide_out, by_slim_in, by_wide_in = refs[:6]
    corner_slim, corner_wide, packed = refs[6:9]
    by_send, by_recv, send_sem, recv_sem, go = refs[9:HALO_SCRATCH]
    place = Place()
    greet(place)
    place_own(features_ref, shifts_ref, slim, wide, by_slim_out, by_wide_out, packed)
    exchanges = [
        kind(
            place,
            table,
            out,
            landed,
            corner,
            by_send.at[t],
            by_recv.at[t],
            send_sem.at[t],
            recv_sem.at[t],
        )
        for t, (kind, table, out, landed, corner) in enumerate(
            (
                (SlimExchange, slim, by_slim_out, by_slim_in, corner_slim),
                (Exchange, wide, by_wide_out, by_wide_in, corner_wide),
            )
        )
    ]

    def begin():
        meet(place)
        help_others(place, go)
        start_first(place, exchanges)

    def slim_ready():
        start_second(place, exchanges, go)
        pass_on(place, exchanges)
        exchanges[0].arrive()

    def wide_ready():
        exchanges[1].arrive()

    edge_work(None, begin, slim_ready, wide_ready, slim, wide, *operands, *refs[HALO_SCRATCH:])
    for exchange in exchanges:
        exchange.close()


VMEM = pl.BlockSpec(memory_space=pltpu.VMEM)


def whole(*operands):
    return pl.pallas_call(
        whole_kernel,
        out_shape=(
            jax.ShapeDtypeStruct((1, 64), F32),
            jax.ShapeDtypeStruct((3, 1, 64), F32),
        ),
        in_specs=[VMEM] * 11,
        out_specs=(VMEM, VMEM),
        scratch_shapes=[
            pltpu.VMEM((ROWS, SLIM), BF16),
            pltpu.VMEM((ROWS, WIDE), BF16),
            pltpu.VMEM((2, 32, SLIM), BF16),
            pltpu.VMEM((2, 32, WIDE), BF16),
            pltpu.VMEM((2, 32, SLIM), BF16),
            pltpu.VMEM((2, 32, WIDE), BF16),
            pltpu.VMEM((2, 16, SLIM), BF16),
            pltpu.VMEM((2, 16, WIDE), BF16),
            pltpu.VMEM((64, SLIM), F32),
            pltpu.SemaphoreType.DMA((2, 4)),
            pltpu.SemaphoreType.DMA((2, 4)),
            pltpu.SemaphoreType.DMA((2, 3, SENDS)),
            pltpu.SemaphoreType.DMA((2, 3, SENDS)),
            pltpu.SemaphoreType.REGULAR((2,)),
        ]
        + edge_scratch(),
        compiler_params=pltpu.CompilerParams(
            collective_id=0, has_side_effects=True, vmem_limit_bytes=56 * 2**20
        ),
        name="boxes",
    )(*operands)


def per_device(
    features,
    shifts,
    block_counts,
    block_centres,
    block_neighbours,
    w_pair,
    w_radial,
    w_mix,
    w_self,
    w_tensor,
    w_out,
):
    energies, forces = whole(
        features.reshape(64, WIDE),
        shifts.reshape(64, 3).T,
        block_counts.reshape(1, 1),
        block_centres.reshape(BLOCKS, 4).T,
        block_neighbours.reshape(BLOCKS, EDGES),
        w_pair,
        w_radial,
        w_mix.T,
        w_self,
        w_tensor,
        w_out.reshape(1, 128),
    )
    return energies.reshape(1, 1, 1, 64), forces.reshape(1, 1, 1, 3, 64)


def solution(mesh):
    in_specs = (
        P("bx", "by", "bz", None, None),
        P("bx", "by", "bz", None, None),
        P("bx", "by", "bz"),
        P("bx", "by", "bz", None, None),
        P("bx", "by", "bz", None, None),
        P(),
        P(),
        P(),
        P(),
        P(),
        P(),
    )
    out_specs = (P("bx", "by", "bz", None), P("bx", "by", "bz", None, None))
    return jax.shard_map(
        per_device, mesh=mesh, in_specs=in_specs, out_specs=out_specs, check_vma=False
    )
```
